32 devices in a mesh: section: 2 (over core), seq: 4 (over z), tp: 4 (over y, x).
Axes of the slice: x: 2, y: 2, z: 4, core: 2. Of those that a mesh axis runs over, the one named last changes fastest.
Arguments:
- hidden: bfloat16 [2, 2, 1, 1024, 768], P('section', None, None, 'seq'), may hold values from -6 to 6
- segments: int32 [2, 2, 1, 1024], replicated, may hold values from 0 to 2, as said below
- self_qkv: bfloat16 [2, 3, 768, 768], P('section', None, None, 'tp'), may hold values from -0.21875 to 0.21875
- self_out: bfloat16 [2, 768, 768], P('section', 'tp'), may hold values from -0.4375 to 0.4375
- ffn_in: bfloat16 [2, 768, 3072], P('section', None, 'tp'), may hold values from -0.21875 to 0.21875
- ffn_in_bias: float32 [2, 4, 768], P('section', 'tp'), may hold values from -3 to 3
- ffn_out: bfloat16 [2, 3072, 768], P('section', 'tp'), may hold values from -0.109375 to 0.109375
- norm_gains: float32 [2, 2, 768], P('section'), may hold values from 0.25 to 1.75
- norm_shifts: float32 [2, 3, 768], P('section'), may hold values from -2 to 2
- cross_qkv: bfloat16 [3, 768, 768], P(None, None, 'tp'), may hold values from -0.21875 to 0.21875
- cross_out: bfloat16 [768, 768], P('tp'), may hold values from -0.4375 to 0.4375
- cross_gain: float32 [768], replicated, may hold values from 0.25 to 1.75
- cross_shift: float32 [768], replicated, may hold values from -2 to 2
- cotangent: bfloat16 [2, 1, 1024, 768], P(None, None, 'seq'), may hold values from -6 to 6
Outputs:
- layer_out: bfloat16 [2, 2, 1, 1024, 768], P('section', None, None, 'seq')
- grad_hidden: bfloat16 [2, 2, 1, 1024, 768], P('section', None, None, 'seq')
- grad_self_qkv: float32 [2, 3, 768, 768], P('section', None, 'seq', 'tp')
- grad_self_out: float32 [2, 768, 768], P('section', 'tp', 'seq')
- grad_ffn_in: float32 [2, 768, 3072], P('section', 'seq', 'tp')
- grad_ffn_in_bias: float32 [2, 4, 768], P('section', 'tp', 'seq')
- grad_ffn_out: float32 [2, 3072, 768], P('section', 'tp', 'seq')
- grad_norm_gains: float32 [2, 2, 768], P('section', None, 'seq')
- grad_norm_shifts: float32 [2, 3, 768], P('section', None, 'seq')
- grad_cross_qkv: float32 [3, 768, 768], P(None, ('section', 'seq'), 'tp')
- grad_cross_out: float32 [768, 768], P('tp', ('section', 'seq'))
- grad_cross_gain: float32 [768], P(('section', 'seq'))
- grad_cross_shift: float32 [768], P(('section', 'seq'))
The draws below stay inside these ranges and needn't reach their ends.
Inputs may be any that keep to these rules, and one draw needn't show every extreme that they name: `segments`: along each row of either side the ids never fall, and every row of both sides holds all three ids.
All inputs are finite; a program needn't handle non-finite values.
Results may differ from the reference program's by a relative error of at most 0.015.
Values may be sent and summed in bfloat16 or wider, within the bound.
No kernel may reach another device: no remote copies, remote signals or barrier semaphores. Data moves between devices by JAX's collectives and lax.ppermute only.
A program may use at most 192 MiB of HBM per device.

```python
import math
import jax
import jax.numpy as jnp
from jax import lax

D = 768
HEADS = 12
HEAD_DIM = 64
FF = 3072
LEN = 1024
MB = 2
ROWS_MB = 1
SPAN = 256
N_TP = 4


def draw_segments(key, part):
    key = jax.random.fold_in(key, 11)
    key_first, key_last = jax.random.split(key)
    first_cut = jax.random.randint(key_first, (2, MB, ROWS_MB, 1), 1, SPAN)
    last_cut = jax.random.randint(key_last, (2, MB, ROWS_MB, 1), LEN - SPAN + 1, LEN)
    places = jnp.arange(LEN, dtype=jnp.int32)
    return (places >= first_cut).astype(jnp.int32) + (places >= last_cut).astype(jnp.int32)


def block_scale(own_key, dims, cuts, low, top_value):
    factor_of, own = 1.0, jax.random.fold_in(own_key, 6)
    for axis_at, blocks in cuts:
        draws = jnp.exp(jax.random.uniform(jax.random.fold_in(own, axis_at), (blocks,), jnp.float32, low / len(cuts), top_value / len(cuts)))
        factor_of = factor_of * jnp.repeat(draws, dims[axis_at] // blocks).reshape([-1 if axis == axis_at else 1 for axis in range(len(dims))])
    return factor_of


def gaussian(key, dims, scale, most, cuts=(), kind=jnp.bfloat16):
    entries = scale * jax.random.normal(key, dims, jnp.float32)
    if cuts:
        entries = entries * block_scale(key, dims, cuts, -0.22, 0.18)
    return jnp.clip(entries, -most, most).astype(kind)


def setup_inputs(seed: int = 0) -> dict:
    arg_keys = jax.random.split(jax.random.key(seed), 15)
    hidden = gaussian(arg_keys[0], (2, MB, ROWS_MB, LEN, D), 1.0, 6.0, ((0, 2), (3, 4)))
    segments = draw_segments(jax.random.fold_in(arg_keys[14], 71), 0)
    self_qkv = gaussian(arg_keys[2], (2, 3, D, D), D ** -0.5, 0.21875, ((0, 2), (3, 4)))
    self_out = gaussian(arg_keys[3], (2, D, D), (D // 4) ** -0.5, 0.4375, ((0, 2), (1, 4)))
    ffn_in = gaussian(arg_keys[4], (2, D, FF), D ** -0.5, 0.21875, ((0, 2), (2, 4)))
    ffn_in_bias = gaussian(arg_keys[5], (2, N_TP, FF // N_TP), 0.5, 3.0, ((0, 2), (1, 4)), jnp.float32)
    ffn_out = gaussian(arg_keys[6], (2, FF, D), FF ** -0.5, 0.109375, ((0, 2), (1, 4)))
    norm_gains = jnp.clip(1.0 + 0.15 * jax.random.normal(arg_keys[7], (2, 2, D), jnp.float32), 0.25, 1.75)
    norm_shifts = gaussian(arg_keys[8], (2, 3, D), 0.3, 2.0, ((0, 2),), jnp.float32)
    cross_qkv = gaussian(arg_keys[9], (3, D, D), D ** -0.5, 0.21875, ((2, 4),))
    cross_out = gaussian(arg_keys[10], (D, D), (D // 4) ** -0.5, 0.4375, ((0, 4),))
    cross_gain = jnp.clip(1.0 + 0.15 * jax.random.normal(arg_keys[11], (D,), jnp.float32), 0.25, 1.75)
    cross_shift = gaussian(arg_keys[12], (D,), 0.3, 2.0, (), jnp.float32)
    cotangent = gaussian(arg_keys[13], (MB, ROWS_MB, LEN, D), 1.0, 6.0, ((2, 4),))
    return dict(hidden=hidden, segments=segments, self_qkv=self_qkv, self_out=self_out, ffn_in=ffn_in, ffn_in_bias=ffn_in_bias, ffn_out=ffn_out, norm_gains=norm_gains, norm_shifts=norm_shifts, cross_qkv=cross_qkv, cross_out=cross_out, cross_gain=cross_gain, cross_shift=cross_shift, cotangent=cotangent)


highest = lax.Precision.HIGHEST
epsilon = 1e-05
masked_out = -1e+30

@jax.custom_vjp
def low(v):
    return lax.optimization_barrier(v.astype(jnp.bfloat16)).astype(jnp.float32)

@jax.custom_vjp
def low_back(v):
    return v

def low_keep(v):
    return (low(v), None)

def low_pass(kept, grad):
    return (grad,)

def back_keep(v):
    return (v, None)

def back_low(kept, grad):
    return (low(grad),)
low.defvjp(low_keep, low_pass)
low_back.defvjp(back_keep, back_low)

def norm_layer(values, norm_gain, norm_shift):
    centred = values - lax.optimization_barrier(jnp.mean(values, axis=-1, keepdims=True))
    spread = lax.optimization_barrier(jnp.mean(centred * centred, axis=-1, keepdims=True))
    return centred * lax.rsqrt(spread + epsilon) * norm_gain + norm_shift

def project(values, weight):
    return jnp.einsum('rtd,de->rte', values, weight, precision=highest)

def attend_rows(queries, key_rows, value_rows, query_ids, key_ids, causal):
    score_scale = 1.0 / math.sqrt(HEAD_DIM)

    def one_row(operands):
        query_row, key_row, value_row, query_seg, key_seg = operands
        length = query_row.shape[0]
        key_length = key_row.shape[0]
        query_heads = query_row.reshape(length, HEADS, HEAD_DIM)
        key_heads = key_row.reshape(key_length, HEADS, HEAD_DIM)
        value_heads = value_row.reshape(key_length, HEADS, HEAD_DIM)
        scores = low_back(jnp.einsum('qhd,khd->hqk', query_heads, key_heads, precision=highest) * score_scale)
        allowed = query_seg[:, None] == key_seg[None, :]
        if causal:
            places = jnp.arange(length)
            allowed = allowed & (places[None, :] <= places[:, None])
        scores = jnp.where(allowed[None], scores, masked_out)
        weights = low(jax.nn.softmax(scores, axis=-1))
        mixture = jnp.einsum('hqk,khd->qhd', weights, value_heads, precision=highest)
        return mixture.reshape(length, HEADS * HEAD_DIM)
    return lax.map(jax.checkpoint(one_row), (queries, key_rows, value_rows, query_ids, key_ids))

def self_branch(inputs, qkv_weight, out_weight, row_ids, causal):
    queries = low(low_back(project(inputs, qkv_weight[0])))
    key_rows = low(low_back(project(inputs, qkv_weight[1])))
    value_rows = low(low_back(project(inputs, qkv_weight[2])))
    mixture = low(low_back(attend_rows(queries, key_rows, value_rows, row_ids, row_ids, causal)))
    return low_back(project(mixture, out_weight))

def cross_branch(states, memory, qkv_weight, out_weight, row_ids, memory_ids):
    queries = low(low_back(project(low(states), qkv_weight[0])))
    key_rows = low(low_back(project(memory, qkv_weight[1])))
    value_rows = low(low_back(project(memory, qkv_weight[2])))
    mixture = low(low_back(attend_rows(queries, key_rows, value_rows, row_ids, memory_ids, False)))
    return low_back(project(mixture, out_weight))

def feed_forward(states, weight_in, bias_in, weight_out, bias_out):
    before = low_back(project(low(states), weight_in) + bias_in)
    after = low(jax.nn.gelu(before, approximate=False))
    return low_back(project(after, weight_out)) + bias_out

def run_layers(segments, hidden, self_qkv, self_out, ffn_in, ffn_in_bias, ffn_out, norm_gains, norm_shifts, cross_qkv, cross_out, cross_gain, cross_shift):
    bias_rows = ffn_in_bias.reshape(2, FF)
    encoded_all = []
    decoded_all = []
    for micro_index in range(MB):
        encoder_ids = segments[0, micro_index]
        decoder_ids = segments[1, micro_index]
        inputs = hidden[0, micro_index]
        after_self = norm_layer(inputs + self_branch(inputs, self_qkv[0], self_out[0], encoder_ids, False), norm_gains[0, 0], norm_shifts[0, 0])
        encoded = norm_layer(after_self + feed_forward(after_self, ffn_in[0], bias_rows[0], ffn_out[0], norm_shifts[0, 2]), norm_gains[0, 1], norm_shifts[0, 1])
        memory = low(low_back(encoded))
        targets = hidden[1, micro_index]
        after_target = norm_layer(targets + self_branch(targets, self_qkv[1], self_out[1], decoder_ids, True), norm_gains[1, 0], norm_shifts[1, 0])
        crossed = norm_layer(after_target + cross_branch(after_target, memory, cross_qkv, cross_out, decoder_ids, encoder_ids), cross_gain, cross_shift)
        decoded = norm_layer(crossed + feed_forward(crossed, ffn_in[1], bias_rows[1], ffn_out[1], norm_shifts[1, 2]), norm_gains[1, 1], norm_shifts[1, 1])
        encoded_all.append(encoded)
        decoded_all.append(decoded)
    return (jnp.stack(encoded_all), jnp.stack(decoded_all))

def reference(hidden, segments, self_qkv, self_out, ffn_in, ffn_in_bias, ffn_out, norm_gains, norm_shifts, cross_qkv, cross_out, cross_gain, cross_shift, cotangent):
    operands = tuple((operand.astype(jnp.float32) for operand in (hidden, self_qkv, self_out, ffn_in, ffn_in_bias, ffn_out, norm_gains, norm_shifts, cross_qkv, cross_out, cross_gain, cross_shift)))

    def layers(*inputs_all):
        return run_layers(segments, *inputs_all)
    (encoded, decoded), pullback = jax.vjp(layers, *operands)
    gradients = pullback((jnp.zeros_like(encoded), cotangent.astype(jnp.float32)))
    layer_out = jnp.stack([encoded, decoded]).astype(jnp.bfloat16)
    return (layer_out, gradients[0].astype(jnp.bfloat16), gradients[1], gradients[2], gradients[3], gradients[4], gradients[5], gradients[6], gradients[7], gradients[8], gradients[9], gradients[10], gradients[11])
```

```python
import math

import jax
import jax.numpy as jnp
from jax import lax
from jax.experimental import pallas as pl
from jax.experimental.pallas import tpu as pltpu
from jax.sharding import PartitionSpec as P

HEAD_DIM = 64
EPSILON = 1e-05
MASKED_OUT = -1e30
SCALE = 1.0 / math.sqrt(HEAD_DIM)
F32 = jnp.float32
BF16 = jnp.bfloat16
MIB = 1 << 20

GAIN_ATT, GAIN_END, SHIFT_ATT, SHIFT_END, BIAS_OUT, BIAS_IN = range(6)


def shape(dims, kind):
    return jax.ShapeDtypeStruct(dims, kind)


def dot(left, right, left_dim=1, right_dim=0):
    return lax.dot_general(
        left, right, (((left_dim,), (right_dim,)), ((), ())), preferred_element_type=F32
    )


def call(name, body, outs, *args, flops=0, vmem=24 * MIB):
    def kernel(*refs):
        body(refs[: len(args)], refs[len(args) :])

    moved = sum(math.prod(a.shape) * a.dtype.itemsize for a in (*args, *outs))
    return pl.pallas_call(
        kernel,
        out_shape=outs,
        in_specs=[pl.BlockSpec(memory_space=pltpu.VMEM)] * len(args),
        out_specs=[pl.BlockSpec(memory_space=pltpu.VMEM)] * len(outs),
        compiler_params=pltpu.CompilerParams(vmem_limit_bytes=vmem),
        cost_estimate=pl.CostEstimate(flops=flops, bytes_accessed=moved, transcendentals=0),
        name=name,
    )(*args)


def swap_cores(block):
    return lax.ppermute(block, "section", [(0, 1), (1, 0)])


def xor_perm(block, axis, bits):
    return lax.ppermute(block, axis, [(i, i ^ bits) for i in range(lax.axis_size(axis))])


def scatter_tp(pieces):
    order = sorted(range(1, len(pieces) + 1), key=lambda i: -bin(i).count("1"))
    got = {i: xor_perm(pieces[i - 1], "tp", i) for i in order}
    return [got[i] for i in range(1, len(pieces) + 1)]


def gather_tp(block):
    return [block] + scatter_tp([block] * (lax.axis_size("tp") - 1))


def normalized(values):
    centred = values - jnp.mean(values, axis=-1, keepdims=True)
    spread = jnp.mean(centred * centred, axis=-1, keepdims=True)
    inverse = lax.rsqrt(spread + EPSILON)
    return centred * inverse, inverse


def norm_back(values, gain, upstream):
    unit, inverse = normalized(values)
    scaled = gain * upstream
    grad = (
        scaled
        - jnp.mean(scaled, axis=-1, keepdims=True)
        - unit * jnp.mean(scaled * unit, axis=-1, keepdims=True)
    ) * inverse
    gain_grad = jnp.sum(upstream * unit, axis=0, keepdims=True)
    shift_grad = jnp.sum(upstream, axis=0, keepdims=True)
    return grad, gain_grad, shift_grad


def put_rows(ref, rows):
    width = ref.shape[1]
    ref[...] = jnp.concatenate(rows + [jnp.zeros((8 - len(rows), width), F32)], axis=0)


def summed(own, received):
    total = own[...]
    for ref in received:
        total = total + ref[...].astype(F32)
    return total


def norm_forward(name, own, received, residual, vectors, rows, bias_row=None):
    count = len(received)

    def body(ins, outs):
        total = summed(ins[0], ins[1 : 1 + count]) + ins[1 + count][...].astype(F32)
        vec = ins[2 + count]
        if bias_row is not None:
            total = total + vec[bias_row : bias_row + 1, :]
        unit, _ = normalized(total)
        result = unit * vec[rows[0] : rows[0] + 1, :] + vec[rows[1] : rows[1] + 1, :]
        outs[0][...] = total
        outs[1][...] = result
        outs[2][...] = result.astype(BF16)

    kinds = [shape(own.shape, F32), shape(own.shape, F32), shape(own.shape, BF16)]
    return call(name, body, kinds, own, *received, residual, vectors)


def norm_backward(name, own, received, residual, values, vectors, row, round_first=False):
    count = len(received)
    args = [own, *received, values, vectors] + ([] if residual is None else [residual])

    def body(ins, outs):
        upstream = summed(ins[0], ins[1 : 1 + count])
        values_ref, vec = ins[1 + count], ins[2 + count]
        if residual is not None:
            upstream = upstream + ins[3 + count][...]
        if round_first:
            upstream = upstream.astype(BF16).astype(F32)
        grad, gain_grad, shift_grad = norm_back(values_ref[...], vec[row : row + 1, :], upstream)
        outs[0][...] = grad
        outs[1][...] = grad.astype(BF16)
        put_rows(outs[2], [gain_grad, shift_grad, jnp.sum(grad, axis=0, keepdims=True)])

    kinds = [shape(own.shape, F32), shape(own.shape, BF16), shape((8, own.shape[1]), F32)]
    return call(name, body, kinds, *args)


def norm_turn(name, own, received, residual, cotangent, vectors):
    count = len(received)

    def body(ins, outs):
        vec = ins[3 + count]
        total = summed(ins[0], ins[1 : 1 + count]) + ins[1 + count][...]
        total = total + vec[BIAS_OUT : BIAS_OUT + 1, :]
        unit, _ = normalized(total)
        gain = vec[GAIN_END : GAIN_END + 1, :]
        outs[0][...] = (unit * gain + vec[SHIFT_END : SHIFT_END + 1, :]).astype(BF16)
        upstream = ins[2 + count][...].astype(F32)
        grad, gain_grad, shift_grad = norm_back(total, gain, upstream)
        outs[1][...] = grad
        outs[2][...] = grad.astype(BF16)
        put_rows(outs[3], [gain_grad, shift_grad, jnp.sum(grad, axis=0, keepdims=True)])

    dims = own.shape
    kinds = [shape(dims, BF16), shape(dims, F32), shape(dims, BF16), shape((8, dims[1]), F32)]
    return call(name, body, kinds, own, *received, residual, cotangent, vectors)


def joined(refs):
    return jnp.concatenate([ref[...] for ref in refs], axis=0)


def store_pieces(refs, value):
    rows = refs[0].shape[0]
    for i, ref in enumerate(refs):
        ref[...] = value[i * rows : (i + 1) * rows].astype(ref.dtype)


def piece_kinds(tokens, width, count):
    rows = tokens // count
    return [shape((rows, width), F32)] + [shape((rows, width), BF16)] * (count - 1)


def project(name, pieces, weight, groups):
    count = len(pieces)
    tokens = sum(p.shape[0] for p in pieces)
    width = weight.shape[2]

    def body(ins, outs):
        values = joined(ins[:count])
        for out, group in zip(outs, groups):
            for at, i in enumerate(group):
                out[:, at * width : (at + 1) * width] = dot(values, ins[count][i]).astype(BF16)

    kinds = [shape((tokens, width * len(g)), BF16) for g in groups]
    return call(name, body, kinds, *pieces, weight)


def project_back(name, grads, weight, picks, pieces):
    tokens = grads[0].shape[0]

    def body(ins, outs):
        total = 0.0
        for ref, (i, start, size) in zip(ins, picks):
            total = total + dot(ref[:, start : start + size], ins[len(grads)][i], 1, 1)
        store_pieces(outs, total)

    return call(name, body, piece_kinds(tokens, weight.shape[1], pieces), *grads, weight)


HALF_ROOT = 0.5**0.5
DENSITY = 1.0 / math.sqrt(2.0 * math.pi)


def feed_forward(name, pieces, weight_in, vectors, weight_out):
    count = len(pieces)
    tokens = sum(p.shape[0] for p in pieces)
    units, width = weight_out.shape
    step = 256

    def body(ins, outs):
        values = joined(ins[:count])
        win, vec, wout = ins[count : count + 3]
        total = 0.0
        for at in range(0, units, step):
            before = dot(values, win[:, at : at + step]) + vec[BIAS_IN : BIAS_IN + 1, at : at + step]
            outs[0][:, at : at + step] = before
            active = (0.5 * before * (1.0 + lax.erf(before * HALF_ROOT))).astype(BF16)
            outs[1][:, at : at + step] = active
            total = total + dot(active, wout[at : at + step, :])
        store_pieces(outs[2:], total)

    kinds = [shape((tokens, units), F32), shape((tokens, units), BF16)]
    kinds += piece_kinds(tokens, width, count)
    flops = 4 * tokens * units * width
    out = call(name, body, kinds, *pieces, weight_in, vectors, weight_out, flops=flops)
    return out[0], out[1], out[2:]


def feed_backward(name, pieces, before, weight_in, weight_out):
    count = len(pieces)
    tokens = sum(p.shape[0] for p in pieces)
    units, width = weight_out.shape
    step = 256

    def body(ins, outs):
        values = joined(ins[:count])
        before_ref, win, wout = ins[count : count + 3]
        total = 0.0
        sums = []
        for at in range(0, units, step):
            grad_active = dot(values, wout[at : at + step, :], 1, 1)
            u = before_ref[:, at : at + step]
            slope = 0.5 * (1.0 + lax.erf(u * HALF_ROOT)) + u * (DENSITY * jnp.exp(-0.5 * u * u))
            grad = (slope * grad_active).astype(BF16)
            outs[0][:, at : at + step] = grad
            sums.append(jnp.sum(grad.astype(F32), axis=0, keepdims=True))
            total = total + dot(grad, win[:, at : at + step], 1, 1)
        put_rows(outs[1], [jnp.concatenate(sums, axis=1)])
        store_pieces(outs[2:], total)

    kinds = [shape((tokens, units), BF16), shape((8, units), F32)]
    kinds += piece_kinds(tokens, width, count)
    flops = 4 * tokens * units * width
    out = call(name, body, kinds, *pieces, before, weight_in, weight_out, flops=flops)
    return out[0], out[1], out[2:]


def head_block(flipped, head, heads):
    tokens = flipped.shape[1]
    parts = []
    if head:
        parts.append(jnp.zeros((HEAD_DIM * head, tokens), flipped.dtype))
    parts.append(flipped[HEAD_DIM * head : HEAD_DIM * (head + 1)])
    if head < heads - 1:
        parts.append(jnp.zeros((HEAD_DIM * (heads - 1 - head), tokens), flipped.dtype))
    return jnp.concatenate(parts, axis=0) if len(parts) > 1 else parts[0]


def allowed_keys(ins, piece, tokens, group, span, causal):
    at = piece * tokens + group * span
    allowed = ins[1][at : at + span, :] == ins[0][:, group * span : (group + 1) * span]
    if causal:
        earlier = ins[3][at : at + span, :] <= ins[2][:, group * span : (group + 1) * span]
        allowed = allowed & earlier
    return allowed


def attend(name, queries, pieces, marks, causal, weight_out, rows, tp):
    tokens, width = queries.shape
    span = tokens // rows
    heads = width // HEAD_DIM
    count = len(pieces)

    def body(ins, outs):
        wout, mark = ins[1], ins[2 : 2 + len(marks)]
        kv = ins[2 + len(marks) :]
        mixed = []
        for group in range(rows):
            part = slice(group * span, (group + 1) * span)
            flipped = (ins[0][part, :] * BF16(SCALE)).T
            value_rows = [ref[part, width:].T for ref in kv]
            masks = [allowed_keys(mark, p, tokens, group, span, causal) for p in range(count)]
            mixtures, logs = [], []
            for head in range(heads):
                block = head_block(flipped, head, heads)
                scores = [
                    jnp.where(masks[p], dot(kv[p][part, :width], block), MASKED_OUT)
                    for p in range(count)
                ]
                largest = scores[0]
                for s in scores[1:]:
                    largest = jnp.maximum(largest, s)
                largest = jnp.max(largest, axis=0, keepdims=True)
                total, mixture = 0.0, 0.0
                for p in range(count):
                    e = jnp.exp(scores[p] - largest)
                    total = total + jnp.sum(e, axis=0, keepdims=True)
                    own = value_rows[p][HEAD_DIM * head : HEAD_DIM * (head + 1)]
                    mixture = mixture + dot(own, e.astype(BF16))
                mixtures.append(mixture * (1.0 / total))
                logs.append(largest + jnp.log(total))
            logs.append(jnp.zeros((8 - heads, span), F32))
            outs[1][group] = jnp.concatenate(logs, axis=0)
            mixed.append(jnp.concatenate(mixtures, axis=0).T.astype(BF16))
        result = jnp.concatenate(mixed, axis=0) if rows > 1 else mixed[0]
        outs[0][...] = result
        store_pieces(outs[2:], dot(result, wout[...]))

    kinds = [shape((tokens, width), BF16), shape((rows, 8, span), F32)]
    kinds += piece_kinds(tokens, weight_out.shape[1], tp)
    flops = 4 * tokens * span * count * heads * 256
    out = call(name, body, kinds, queries, weight_out, *marks, *pieces, flops=flops)
    return out[0], out[1], out[2:]


def attend_back(name, upstream, weight_out, queries, pieces, marks, causal, logs, rows, near):
    tokens, width = queries.shape
    span = tokens // rows
    heads = width // HEAD_DIM
    count = len(pieces)
    first = len(upstream)

    def body(ins, outs):
        wout = ins[first][...]
        mark = ins[first + 3 : first + 3 + len(marks)]
        kv = ins[first + 3 + len(marks) :]
        all_grad = joined(ins[:first])
        grad_rows = dot(all_grad, wout, 1, 1).astype(BF16)
        for group in range(rows):
            part = slice(group * span, (group + 1) * span)
            grad = grad_rows[part]
            grad_flipped = dot(wout, all_grad[part], 1, 1).astype(BF16)
            scaled = ins[first + 1][part, :] * BF16(SCALE)
            flipped = scaled.T
            key_rows = [ref[part, :width].T for ref in kv]
            masks = [allowed_keys(mark, p, tokens, group, span, causal) for p in range(count)]
            lane = lax.broadcasted_iota(jnp.int32, (span, width), 1)
            key_grads, value_grads, query_grads = [0.0] * count, [0.0] * count, []
            for head in range(heads):
                mine = (lane >= HEAD_DIM * head) & (lane < HEAD_DIM * (head + 1))
                block = head_block(flipped, head, heads)
                grad_block = head_block(grad_flipped, head, heads)
                query_part = jnp.where(mine, scaled, BF16(0.0))
                grad_part = jnp.where(mine, grad, BF16(0.0))
                log_row = ins[first + 2][group, head : head + 1, :]
                weights, weight_grads, inner = [], [], 0.0
                for p in range(count):
                    s = jnp.where(masks[p], dot(kv[p][part, :width], block), MASKED_OUT)
                    w = jnp.exp(s - log_row)
                    g = dot(kv[p][part, width:], grad_block)
                    inner = inner + jnp.sum(w * g, axis=0, keepdims=True)
                    value_grads[p] = value_grads[p] + dot(w.astype(BF16), grad_part)
                    weights.append(w)
                    weight_grads.append(g)
                query_grad = 0.0
                for p in range(count):
                    score_grad = (weights[p] * (weight_grads[p] - inner)).astype(BF16)
                    key_grads[p] = key_grads[p] + dot(score_grad, query_part)
                    own = key_rows[p][HEAD_DIM * head : HEAD_DIM * (head + 1)]
                    query_grad = query_grad + dot(own, score_grad)
                query_grads.append(query_grad)
            outs[0][part, :] = (jnp.concatenate(query_grads, axis=0) * SCALE).T.astype(BF16)
            for p in range(count):
                out, at = (outs[1], p) if p < near else (outs[2], p - near)
                at = slice(at * tokens + group * span, at * tokens + (group + 1) * span)
                out[at, :width] = key_grads[p].astype(out.dtype)
                out[at, width:] = value_grads[p].astype(out.dtype)

    kinds = [
        shape((tokens, width), BF16),
        shape((near * tokens, 2 * width), F32),
        shape(((count - near) * tokens, 2 * width), BF16),
    ]
    flops = 10 * tokens * span * count * heads * 256
    args = (*upstream, weight_out, queries, logs, *marks, *pieces)
    return call(name, body, kinds, *args, flops=flops)


def weight_partials(name, pairs, where, order, per):
    tokens, width = pairs[0][0].shape
    columns = sum(right.shape[1] for _, right in pairs)
    lefts, rights = [], []
    for left, right in pairs:
        lefts.append(left)
        rights.append(right)
    count = len(order)
    align = 16 if per % 16 == 0 else 8

    def kernel(where_ref, *refs):
        ins, out, turned = refs[: 2 * len(pairs)], refs[2 * len(pairs)], refs[2 * len(pairs) + 1 :]
        at = 0
        for i in range(len(pairs)):
            right = ins[len(pairs) + i][...]
            held = turned[i]
            held[...] = ins[i][...].astype(held.dtype).T
            for k in range(count):
                start = pl.multiple_of(where_ref[k] * per, align)
                got = dot(held[pl.ds(start, per), :].astype(BF16), right)
                out[k * per : (k + 1) * per, at : at + right.shape[1]] = got.astype(BF16)
            at += right.shape[1]

    moved = sum(math.prod(a.shape) * 2 for a in (*lefts, *rights)) + count * per * columns * 2
    return pl.pallas_call(
        kernel,
        out_shape=shape((count * per, columns), BF16),
        in_specs=[pl.BlockSpec(memory_space=pltpu.SMEM)]
        + [pl.BlockSpec(memory_space=pltpu.VMEM)] * (2 * len(pairs)),
        out_specs=pl.BlockSpec(memory_space=pltpu.VMEM),
        scratch_shapes=[pltpu.VMEM((width, tokens), BF16 if align == 16 else F32)] * len(pairs),
        compiler_params=pltpu.CompilerParams(vmem_limit_bytes=24 * MIB),
        cost_estimate=pl.CostEstimate(
            flops=2 * tokens * count * per * columns, bytes_accessed=moved, transcendentals=0
        ),
        name=name,
    )(where, *lefts, *rights)


def added(left, right, kind):
    return (left.astype(F32) + right.astype(F32)).astype(kind)


def on_device(
    hidden,
    segments,
    self_qkv,
    self_out,
    ffn_in,
    ffn_in_bias,
    ffn_out,
    norm_gains,
    norm_shifts,
    cross_qkv,
    cross_out,
    cross_gain,
    cross_shift,
    cotangent,
):
    section, seq, tp = (lax.axis_index(a) for a in ("section", "seq", "tp"))
    n_seq, n_tp = lax.axis_size("seq"), lax.axis_size("tp")
    half = n_seq // 2
    low_half = seq < half
    on_first = section == 0
    settled = on_first == low_half
    rows, span, width = hidden.shape[2:]
    tokens = rows * span
    sub = tokens // n_tp
    micro = seq // half

    both = ("section", "seq")
    low = range(half)
    to_encoder = [(z, z + half) for z in low] + [(z + half, n_seq + z) for z in low]
    to_decoder = [(n_seq + z, z + half) for z in low] + [(n_seq + z + half, n_seq + z) for z in low]
    across = [(z + half, n_seq + z + half) for z in low] + [(n_seq + z, z) for z in low]

    def spread(near, far):
        far_enc = lax.ppermute(far, both, to_encoder)
        core = lax.ppermute(near, both, across)
        far_dec = lax.ppermute(far, both, to_decoder)
        enc = jnp.where(settled, jnp.where(on_first, near, core), far_enc)
        dec = jnp.where(settled, jnp.where(on_first, core, near), far_dec)
        return enc, dec

    def collect(enc, dec):
        far_enc = lax.ppermute(enc, both, [(b, a) for a, b in to_encoder])
        far_dec = lax.ppermute(dec, both, [(b, a) for a, b in to_decoder])
        core = lax.ppermute(jnp.where(on_first, dec, enc), both, [(b, a) for a, b in across])
        near = jnp.where(settled, jnp.where(on_first, enc, dec), core)
        far = jnp.where(on_first, far_enc, far_dec)
        return jnp.stack([jnp.where(low_half, near, far), jnp.where(low_half, far, near)])

    def relative(block):
        cut = block.reshape(n_tp, sub, *block.shape[1:])
        return jnp.concatenate(
            [lax.dynamic_index_in_dim(cut, tp ^ i, 0, keepdims=False) for i in range(n_tp)]
        )

    both_micro = hidden[0].reshape(2, tokens, width)
    near = jnp.where(low_half, both_micro[0], both_micro[1])
    far = jnp.where(low_half, both_micro[1], both_micro[0])
    input_enc, input_dec = spread(near, far)
    input_enc, input_dec = relative(input_enc), relative(input_dec)

    vectors = jnp.concatenate(
        [norm_gains[0], norm_shifts[0], ffn_in_bias[0], jnp.zeros((2, width), F32)]
    )

    def layers(own):
        other = swap_cores(own)
        return jnp.where(on_first, own, other), jnp.where(on_first, other, own)

    qkv_enc, qkv_dec = layers(self_qkv[0])
    vec_enc, vec_dec = layers(vectors)
    out_enc, out_dec = layers(self_out[0])
    win_enc, win_dec = layers(ffn_in[0])
    wout_enc, wout_dec = layers(ffn_out[0])
    vec_cross = jnp.concatenate(
        [cross_gain[None], cross_gain[None], cross_shift[None], jnp.zeros((5, width), F32)]
    )

    ids = lax.dynamic_index_in_dim(segments, micro, 1, keepdims=False)
    own_z = seq % half

    def chunk_marks(at):
        cut = lax.dynamic_slice_in_dim(ids, at * span, span, 2).reshape(2, tokens)
        place = jnp.broadcast_to(at * span + jnp.arange(span), (rows, span)).reshape(1, tokens)
        return relative(jnp.concatenate([cut, place]).T)

    offsets = [(dc, dz) for dc in range(2) for dz in range(half)]
    key_marks = jnp.concatenate(
        [chunk_marks((section ^ dc) * half + (own_z ^ dz)) for dc, dz in offsets]
    )
    query_marks = key_marks[:tokens].T
    key_enc, key_dec, key_place = (key_marks[:, i : i + 1] for i in range(3))
    query_enc, query_dec, query_place = (query_marks[i : i + 1] for i in range(3))
    marks_enc = (query_enc, key_enc)
    marks_dec = (query_dec, key_dec, query_place, key_place)
    marks_cross = (query_dec, key_enc)

    def share(own):
        mine = [own] + [xor_perm(own, "seq", dz) for dz in range(1, half)]
        return mine + [swap_cores(block) for block in mine]

    def settle(mine, theirs):
        total = mine + swap_cores(theirs).astype(F32)
        sent = [
            xor_perm(total[dz * tokens : (dz + 1) * tokens].astype(BF16), "seq", dz)
            for dz in range(1, half)
        ]
        own = total[:tokens]
        for block in sent:
            own = own + block.astype(F32)
        return own.astype(BF16)

    q_enc, kv_enc = project("qkv_enc", [input_enc], qkv_enc, [(0,), (1, 2)])
    all_enc = share(kv_enc)
    a_enc, log_enc, part = attend(
        "attend_enc", q_enc, all_enc, marks_enc, False, out_enc, rows, n_tp
    )
    z1_enc, h1_enc, h1b_enc = norm_forward(
        "norm_att_enc", part[0], scatter_tp(part[1:]), input_enc[:sub], vec_enc,
        (GAIN_ATT, SHIFT_ATT),
    )
    h1_pieces_enc = gather_tp(h1b_enc)

    q_dec, kv_dec = project("qkv_dec", [input_dec], qkv_dec, [(0,), (1, 2)])
    all_dec = share(kv_dec)
    a_dec, log_dec, part = attend(
        "attend_dec", q_dec, all_dec, marks_dec, True, out_dec, rows, n_tp
    )
    z1_dec, h1_dec, h1b_dec = norm_forward(
        "norm_att_dec", part[0], scatter_tp(part[1:]), input_dec[:sub], vec_dec,
        (GAIN_ATT, SHIFT_ATT),
    )
    h1_pieces_dec = gather_tp(h1b_dec)
    (q_cross,) = project("q_cross", h1_pieces_dec, cross_qkv, [(0,)])

    u_enc, g_enc, part = feed_forward("ffn_enc", h1_pieces_enc, win_enc, vec_enc, wout_enc)
    z2_enc, _, memory = norm_forward(
        "norm_end_enc", part[0], scatter_tp(part[1:]), h1_enc, vec_enc,
        (GAIN_END, SHIFT_END), BIAS_OUT,
    )
    memory_pieces = gather_tp(memory)

    (kv_cross,) = project("kv_cross", memory_pieces, cross_qkv, [(1, 2)])
    all_cross = share(kv_cross)
    a_cross, log_cross, part = attend(
        "attend_cross", q_cross, all_cross, marks_cross, False, cross_out, rows, n_tp
    )
    z_cross, h2, h2b = norm_forward(
        "norm_cross", part[0], scatter_tp(part[1:]), h1_dec, vec_cross, (GAIN_ATT, SHIFT_ATT)
    )
    h2_pieces = gather_tp(h2b)
    u_dec, g_dec, part = feed_forward("ffn_dec", h2_pieces, win_dec, vec_dec, wout_dec)

    cot = lax.dynamic_slice_in_dim(cotangent.reshape(2, tokens, width), tp * sub, sub, 1)
    cot_near = jnp.where(low_half, cot[0], cot[1])
    cot_far = jnp.where(low_half, cot[1], cot[0])
    cot_moved = lax.ppermute(
        cot_far, both, [(z, z + half) for z in low] + [(n_seq + z + half, n_seq + z) for z in low]
    )
    cot_own = jnp.where(settled, cot_near, cot_moved)

    decoded, dz2_dec, dz2b_dec, sums_end_dec = norm_turn(
        "norm_end_dec", part[0], scatter_tp(part[1:]), h2, cot_own, vec_dec
    )

    r_pieces_dec = gather_tp(dz2b_dec)
    du_dec, sums_in_dec, part = feed_backward("ffn_back_dec", r_pieces_dec, u_dec, win_dec, wout_dec)
    dzc, dzcb, sums_cross = norm_backward(
        "norm_back_cross", part[0], scatter_tp(part[1:]), dz2_dec, z_cross, vec_cross, GAIN_ATT
    )
    dzc_pieces = gather_tp(dzcb)

    dq_cross, near_kv, far_kv = attend_back(
        "attend_back_cross", dzc_pieces, cross_out, q_cross, all_cross, marks_cross, False,
        log_cross, rows, half,
    )
    heads_width = q_cross.shape[1]
    dkv_cross = settle(near_kv, far_kv)
    part = project_back(
        "memory_back", [dkv_cross, dkv_cross], cross_qkv,
        [(1, 0, heads_width), (2, heads_width, heads_width)], n_tp,
    )
    dz2_enc, dz2b_enc, sums_end_enc = norm_backward(
        "norm_back_end_enc", part[0], scatter_tp(part[1:]), None, z2_enc, vec_enc, GAIN_END,
        round_first=True,
    )
    r_pieces_enc = gather_tp(dz2b_enc)

    du_enc, sums_in_enc, part = feed_backward("ffn_back_enc", r_pieces_enc, u_enc, win_enc, wout_enc)
    dz1_enc, dz1b_enc, sums_att_enc = norm_backward(
        "norm_back_att_enc", part[0], scatter_tp(part[1:]), dz2_enc, z1_enc, vec_enc, GAIN_ATT
    )
    dz1_pieces_enc = gather_tp(dz1b_enc)

    whole = [(0, 0, heads_width), (1, 0, heads_width), (2, heads_width, heads_width)]
    dq_enc, near_kv, far_kv = attend_back(
        "attend_back_enc", dz1_pieces_enc, out_enc, q_enc, all_enc, marks_enc, False,
        log_enc, rows, half,
    )
    dkv_enc = settle(near_kv, far_kv)
    part = project_back("input_back_enc", [dq_enc, dkv_enc, dkv_enc], qkv_enc, whole, n_tp)
    received = scatter_tp(part[1:])
    dx_enc = part[0] + dz1_enc
    for block in received:
        dx_enc = dx_enc + block.astype(F32)

    part = project_back("query_back", [dq_cross], cross_qkv, [(0, 0, heads_width)], n_tp)
    dz1_dec, dz1b_dec, sums_att_dec = norm_backward(
        "norm_back_att_dec", part[0], scatter_tp(part[1:]), dzc, z1_dec, vec_dec, GAIN_ATT
    )
    dz1_pieces_dec = gather_tp(dz1b_dec)
    dq_dec, near_kv, far_kv = attend_back(
        "attend_back_dec", dz1_pieces_dec, out_dec, q_dec, all_dec, marks_dec, True,
        log_dec, rows, half,
    )
    dkv_dec = settle(near_kv, far_kv)
    part = project_back("input_back_dec", [dq_dec, dkv_dec, dkv_dec], qkv_dec, whole, n_tp)
    received = scatter_tp(part[1:])
    dx_dec = part[0] + dz1_dec
    for block in received:
        dx_dec = dx_dec + block.astype(F32)

    def whole_chunk(enc, dec):
        found = collect(enc, dec)
        every = lax.all_gather(found, "tp", axis=1, tiled=True)
        return every.reshape(1, 2, rows, span, width)

    layer_out = whole_chunk(memory, decoded)
    grad_hidden = whole_chunk(dx_enc.astype(BF16), dx_dec.astype(BF16))

    bits = max(n_seq.bit_length() - 1, 0)
    order = sorted(range(n_seq), key=lambda r: int(format(r, f"0{bits}b")[::-1], 2))

    def along_seq(block, members):
        bit = 1
        while bit < n_seq:
            rows_now = block.shape[0] // 2
            route = [(s * n_seq + z, s * n_seq + (z ^ bit)) for s in members for z in range(n_seq)]
            got = lax.ppermute(block[rows_now:], both, route)
            bit *= 2
            block = added(block[:rows_now], got, F32 if bit == n_seq else BF16)
        return block

    def layer_grads(name, pairs, member):
        per = width // n_seq
        where = jnp.stack([seq ^ r for r in order]).astype(jnp.int32)
        block = weight_partials(name, pairs, where, order, per)
        other = lax.ppermute(block, "section", [(1 - member, member)])
        return along_seq(added(block, other, BF16), [member])

    ffn_grads, self_grads = [], []
    joined_h2 = jnp.concatenate(h2_pieces)
    joined_h1 = jnp.concatenate(h1_pieces_enc)
    joined_r_dec = jnp.concatenate(r_pieces_dec)
    joined_r_enc = jnp.concatenate(r_pieces_enc)
    joined_z_dec = jnp.concatenate(dz1_pieces_dec)
    joined_z_enc = jnp.concatenate(dz1_pieces_enc)
    dec_ffn = layer_grads("grad_ffn_dec", [(joined_h2, du_dec), (joined_r_dec, g_dec)], 1)

    per_cross = width // (2 * n_seq)
    cross_order = [(dc, r) for dc in range(2) for r in order]
    where = jnp.stack([(section ^ dc) * n_seq + (seq ^ r) for dc, r in cross_order])
    joined_h1_dec = jnp.concatenate(h1_pieces_dec)
    joined_memory = jnp.concatenate(memory_pieces)
    block = weight_partials(
        "grad_cross",
        [(joined_h1_dec, dq_cross), (joined_memory, dkv_cross), (jnp.concatenate(dzc_pieces), a_cross)],
        where.astype(jnp.int32), cross_order, per_cross,
    )
    mine = block.shape[0] // 2
    cross_sum = along_seq(added(block[:mine], swap_cores(block[mine:]), BF16), [0, 1])

    enc_ffn = layer_grads("grad_ffn_enc", [(joined_h1, du_enc), (joined_r_enc, g_enc)], 0)
    dec_self = layer_grads(
        "grad_self_dec", [(input_dec, dq_dec), (input_dec, dkv_dec), (joined_z_dec, a_dec)], 1
    )
    enc_self = layer_grads(
        "grad_self_enc", [(input_enc, dq_enc), (input_enc, dkv_enc), (joined_z_enc, a_enc)], 0
    )
    ffn_sum = jnp.where(on_first, enc_ffn, dec_ffn)
    self_sum = jnp.where(on_first, enc_self, dec_self)
    units = ffn_in.shape[2]

    def thirds(block):
        return jnp.stack([block[:, i * heads_width : (i + 1) * heads_width] for i in range(3)])

    mine_tp = (jnp.arange(n_tp) == tp)[:, None]
    table = jnp.concatenate(
        [
            sums_att_enc[:1], sums_end_enc[:1], sums_att_enc[1:2], sums_end_enc[1:3],
            sums_att_dec[:1], sums_end_dec[:1], sums_att_dec[1:2], sums_end_dec[1:3],
            sums_cross[:2],
            jnp.where(mine_tp, sums_in_enc[:1], 0.0),
            jnp.where(mine_tp, sums_in_dec[:1], 0.0),
        ]
    )
    table = lax.psum(table, ("section", "seq", "tp"))
    layer_rows = jnp.where(on_first, table[:5], table[5:10])
    bias_rows = jnp.where(on_first, table[12 : 12 + n_tp], table[12 + n_tp :])
    part_seq = lax.dynamic_slice_in_dim(layer_rows, seq * (width // n_seq), width // n_seq, 1)
    bias_row = lax.dynamic_index_in_dim(bias_rows, tp, 0)
    bias_part = lax.dynamic_slice_in_dim(bias_row, seq * (units // n_seq), units // n_seq, 1)
    cross_part = lax.dynamic_slice_in_dim(
        table[10:12], (section * n_seq + seq) * per_cross, per_cross, 1
    )

    return (
        layer_out,
        grad_hidden,
        thirds(self_sum)[None],
        self_sum[:, 3 * heads_width :].T[None],
        ffn_sum[:, :units][None],
        bias_part[None],
        ffn_sum[:, units:].T[None],
        part_seq[:2][None],
        part_seq[2:][None],
        thirds(cross_sum),
        cross_sum[:, 3 * heads_width :].T,
        cross_part[0],
        cross_part[1],
    )


def solution(mesh):
    return jax.shard_map(
        on_device,
        mesh=mesh,
        in_specs=(
            P("section", None, None, "seq", None),
            P(),
            P("section", None, None, "tp"),
            P("section", "tp", None),
            P("section", None, "tp"),
            P("section", "tp", None),
            P("section", "tp", None),
            P("section", None, None),
            P("section", None, None),
            P(None, None, "tp"),
            P("tp", None),
            P(),
            P(),
            P(None, None, "seq", None),
        ),
        out_specs=(
            P("section", None, None, "seq", None),
            P("section", None, None, "seq", None),
            P("section", None, "seq", "tp"),
            P("section", "tp", "seq"),
            P("section", "seq", "tp"),
            P("section", "tp", "seq"),
            P("section", "tp", "seq"),
            P("section", None, "seq"),
            P("section", None, "seq"),
            P(None, ("section", "seq"), "tp"),
            P("tp", ("section", "seq")),
            P(("section", "seq")),
            P(("section", "seq")),
        ),
        check_vma=False,
    )
```

```python
import math

import jax
import jax.numpy as jnp
import numpy as np
from jax import lax
from jax.experimental import pallas as pl
from jax.experimental.pallas import tpu as pltpu
from jax.sharding import PartitionSpec as P

HEAD_DIM = 64
EPSILON = 1e-05
MASKED_OUT = -1e30
SCALE = 1.0 / math.sqrt(HEAD_DIM)
F32 = jnp.float32
BF16 = jnp.bfloat16
MIB = 1 << 20

GAIN_ATT, GAIN_END, SHIFT_ATT, SHIFT_END, BIAS_OUT, BIAS_IN = range(6)


def shape(dims, kind):
    return jax.ShapeDtypeStruct(dims, kind)


def dot(left, right, left_dim=1, right_dim=0):
    return lax.dot_general(
        left, right, (((left_dim,), (right_dim,)), ((), ())), preferred_element_type=F32
    )


class Flags:
    FIRST, LOW, SETTLED, TP, SEQ = range(5)


def call(name, body, outs, *args, flags=None, after=(), flops=0, vmem=16 * MIB):
    scalars = [] if flags is None else [flags]
    after = list(after)
    count = len(scalars) + len(args)

    def kernel(*refs):
        body(refs[:count], refs[count + len(after) :])

    moved = sum(math.prod(a.shape) * a.dtype.itemsize for a in (*args, *outs))
    in_specs = [pl.BlockSpec(memory_space=pltpu.SMEM)] * len(scalars)
    in_specs += [pl.BlockSpec(memory_space=pltpu.VMEM)] * len(args)
    in_specs += [pl.BlockSpec(memory_space=pl.ANY)] * len(after)
    return pl.pallas_call(
        kernel,
        out_shape=outs,
        in_specs=in_specs,
        out_specs=[pl.BlockSpec(memory_space=pltpu.VMEM)] * len(outs),
        compiler_params=pltpu.CompilerParams(vmem_limit_bytes=vmem),
        cost_estimate=pl.CostEstimate(flops=flops, bytes_accessed=moved, transcendentals=0),
        name=name,
    )(*scalars, *args, *after)


def swap_cores(block):
    return lax.ppermute(block, "section", [(0, 1), (1, 0)])


def xor_perm(block, axis, bits):
    return lax.ppermute(block, axis, [(i, i ^ bits) for i in range(lax.axis_size(axis))])


def scatter_tp(pieces):
    order = sorted(range(1, len(pieces) + 1), key=lambda i: -bin(i).count("1"))
    got = {i: xor_perm(pieces[i - 1], "tp", i) for i in order}
    return [got[i] for i in range(1, len(pieces) + 1)]


def gather_tp(block):
    return [block] + scatter_tp([block] * (lax.axis_size("tp") - 1))


def normalized(values):
    centred = values - jnp.mean(values, axis=-1, keepdims=True)
    spread = jnp.mean(centred * centred, axis=-1, keepdims=True)
    inverse = lax.rsqrt(spread + EPSILON)
    return centred * inverse, inverse


def norm_back(values, gain, upstream):
    unit, inverse = normalized(values)
    scaled = gain * upstream
    grad = (
        scaled
        - jnp.mean(scaled, axis=-1, keepdims=True)
        - unit * jnp.mean(scaled * unit, axis=-1, keepdims=True)
    ) * inverse
    gain_grad = jnp.sum(upstream * unit, axis=0, keepdims=True)
    shift_grad = jnp.sum(upstream, axis=0, keepdims=True)
    return grad, gain_grad, shift_grad


def put_rows(ref, rows):
    width = ref.shape[1]
    ref[...] = jnp.concatenate(rows + [jnp.zeros((8 - len(rows), width), F32)], axis=0)


VECTOR_ROWS = 16


def put_vectors(ref, at, rows):
    half = VECTOR_ROWS // 2
    whole = jnp.concatenate(rows + [jnp.zeros((half - len(rows), ref.shape[1]), F32)], axis=0)
    top = whole.astype(BF16)
    left = (whole - top.astype(F32)).astype(BF16)
    ref[at : at + VECTOR_ROWS] = jnp.concatenate([top, left], axis=0)


def vector_sums(refs, at, count):
    half = VECTOR_ROWS // 2
    total = 0.0
    for ref in refs:
        rows = ref[at : at + VECTOR_ROWS].astype(F32)
        total = total + (rows[:half] + rows[half:])
    return total[:count]


def summed(own, received, part=slice(None)):
    total = own
    for ref in received:
        total = total + ref[part].astype(F32)
    return total


def joined(refs, part=slice(None)):
    return jnp.concatenate([ref[part] for ref in refs], axis=0)


def store_pieces(refs, value):
    rows = refs[0].shape[0]
    for i, ref in enumerate(refs):
        ref[...] = value[i * rows : (i + 1) * rows].astype(ref.dtype)


def piece_kinds(tokens, width, count, extra=0):
    rows = tokens // count
    return [shape((rows, width), F32)] + [shape((rows + extra, width), BF16)] * (count - 1)


class Layer:
    def __init__(self, mine, own, other):
        self.mine, self.pair = mine, (own, other)
        self.shape = own.shape

    def read(self, flags, refs, part=Ellipsis):
        return jnp.where(flags[Flags.FIRST] == self.mine, refs[0][part], refs[1][part])


def settle_input(name, near, core, far, flags, weight, layer_first, after=(), pass_on=None):
    tokens, width = near.shape
    features = weight.shape[1]
    n_tp = lax.axis_size("tp")
    sub = tokens // n_tp

    def body(ins, outs):
        flag, near_ref, core_ref = ins[:3]
        far_ref, weights = ins[3], ins[4:6]
        tp = flag[Flags.TP]
        is_own = flag[Flags.FIRST] == layer_first
        pieces = []
        for i in range(n_tp):
            at = pl.ds(pl.multiple_of((tp ^ i) * sub, sub), sub)
            settled = jnp.where(is_own, near_ref[at, :], core_ref[at, :])
            pieces.append(jnp.where(flag[Flags.SETTLED] == 1, settled, far_ref[at, :]))
        values = jnp.concatenate(pieces, axis=0)
        outs[0][...] = values
        for i in range(3):
            chosen = weight.read(flag, weights, i)
            out, at = (outs[1], 0) if i == 0 else (outs[2], (i - 1) * features)
            out[:, at : at + features] = dot(values, chosen, 1, 1).astype(BF16)
        if pass_on is not None:
            outs[3][...] = ins[6][...]

    kinds = [
        shape((tokens, width), BF16),
        shape((tokens, features), BF16),
        shape((tokens, 2 * features), BF16),
    ]
    extra = []
    if pass_on is not None:
        kinds.append(shape(pass_on.shape, pass_on.dtype))
        extra.append(pass_on)
    return call(
        name, body, kinds, near, core, far, *weight.pair, *extra, flags=flags, after=after
    )


HALF_ROOT = 0.5**0.5
DENSITY = 1.0 / math.sqrt(2.0 * math.pi)


def feed_forward(name, pieces, weight_in, vectors, weight_out, flags, rider=None, after=()):
    count = len(pieces)
    tokens = sum(p.shape[0] for p in pieces)
    units, width = weight_out.shape
    step = 256
    riders = [] if rider is None else list(rider[1:])

    def body(ins, outs):
        flag, ins = ins[0], ins[1:]
        values = joined(ins[:count])
        win, vec, wout = ins[count : count + 2], ins[count + 2 : count + 4], ins[count + 4 : count + 6]
        bias = vectors.read(flag, vec)[BIAS_IN : BIAS_IN + 1]
        total = 0.0
        for at in range(0, units, step):
            part = slice(at, at + step)
            before = dot(values, weight_in.read(flag, win, (slice(None), part))) + bias[:, part]
            outs[0][:, part] = before
            active = (0.5 * before * (1.0 + lax.erf(before * HALF_ROOT))).astype(BF16)
            outs[1][:, part] = active
            total = total + dot(active, weight_out.read(flag, wout, part))
        rows = tokens // count
        outs[2][...] = total[:rows]
        for i in range(1, count):
            outs[2 + i][:rows] = total[i * rows : (i + 1) * rows].astype(BF16)
            if riders:
                outs[2 + i][rows:] = ins[count + 5 + i][...]

    kinds = [shape((tokens, units), F32), shape((tokens, units), BF16)]
    extra = riders[0].shape[0] if riders else 0
    kinds += piece_kinds(tokens, width, count, extra)
    flops = 4 * tokens * units * width
    out = call(
        name, body, kinds, *pieces, *weight_in.pair, *vectors.pair, *weight_out.pair, *riders,
        flags=flags, after=after, flops=flops,
    )
    return out[0], out[1], out[2:]


def feed_backward(name, pieces, part_rows, before, weight_in, weight_out, flags, after=()):
    count = len(pieces)
    tokens, units = before.shape
    width = weight_out.shape[1]
    step = 256

    def body(ins, outs):
        flag, ins = ins[0], ins[1:]
        values = joined(ins[:count], part_rows)
        before_ref, win, wout = ins[count], ins[count + 1 : count + 3], ins[count + 3 : count + 5]
        total = 0.0
        sums = []
        for at in range(0, units, step):
            part = slice(at, at + step)
            grad_active = dot(values, weight_out.read(flag, wout, part), 1, 1)
            u = before_ref[:, part]
            slope = 0.5 * (1.0 + lax.erf(u * HALF_ROOT)) + u * (DENSITY * jnp.exp(-0.5 * u * u))
            grad = (slope * grad_active).astype(BF16)
            outs[0][:, part] = grad
            sums.append(jnp.sum(grad.astype(F32), axis=0, keepdims=True))
            total = total + dot(grad, weight_in.read(flag, win, (slice(None), part)), 1, 1)
        put_rows(outs[1], [jnp.concatenate(sums, axis=1)])
        store_pieces(outs[2:], total)

    kinds = [shape((tokens, units), BF16), shape((8, units), F32)]
    kinds += piece_kinds(tokens, width, count)
    flops = 4 * tokens * units * width
    out = call(
        name, body, kinds, *pieces, before, *weight_in.pair, *weight_out.pair,
        flags=flags, after=after, flops=flops,
    )
    return out[0], out[1], out[2:]


KEY_ENC, KEY_DEC, PLACE = range(3)


class Marks:
    def __init__(self, marks, query_row, key_row, causal):
        self.marks, self.query_row, self.key_row, self.causal = marks, query_row, key_row, causal

    def allowed(self, ref, columns, piece, tokens, group, span):
        at = piece * tokens + group * span
        own = slice(group * span, (group + 1) * span)
        allowed = (
            columns[at : at + span, self.key_row : self.key_row + 1]
            == ref[self.query_row : self.query_row + 1, own]
        )
        if self.causal:
            places = columns[at : at + span, PLACE : PLACE + 1]
            allowed = allowed & (places <= ref[PLACE : PLACE + 1, own])
        return allowed


def head_block(flipped, head, heads):
    tokens = flipped.shape[1]
    parts = []
    if head:
        parts.append(jnp.zeros((HEAD_DIM * head, tokens), flipped.dtype))
    parts.append(flipped[HEAD_DIM * head : HEAD_DIM * (head + 1)])
    if head < heads - 1:
        parts.append(jnp.zeros((HEAD_DIM * (heads - 1 - head), tokens), flipped.dtype))
    return jnp.concatenate(parts, axis=0) if len(parts) > 1 else parts[0]


def attend(name, queries, pieces, marks, weight_out, flags, rows, tp, after=()):
    tokens, width = queries.shape
    span = tokens // rows
    heads = width // HEAD_DIM
    count = len(pieces)
    weights = list(weight_out.pair) if isinstance(weight_out, Layer) else [weight_out]

    def body(ins, outs):
        flag, query_ref, mark = ins[:3]
        wout = ins[3 : 3 + len(weights)]
        kv = ins[3 + len(weights) :]
        columns = mark[...].T
        mixed = []
        for group in range(rows):
            part = slice(group * span, (group + 1) * span)
            flipped = (query_ref[part, :] * BF16(SCALE)).T
            value_rows = [ref[part, width:].T for ref in kv]
            masks = [marks.allowed(mark, columns, p, tokens, group, span) for p in range(count)]
            mixtures, logs = [], []
            for head in range(heads):
                block = head_block(flipped, head, heads)
                scores = [
                    jnp.where(masks[p], dot(kv[p][part, :width], block), MASKED_OUT)
                    for p in range(count)
                ]
                largest = scores[0]
                for s in scores[1:]:
                    largest = jnp.maximum(largest, s)
                largest = jnp.max(largest, axis=0, keepdims=True)
                total, mixture = 0.0, 0.0
                for p in range(count):
                    e = jnp.exp(scores[p] - largest)
                    total = total + jnp.sum(e, axis=0, keepdims=True)
                    own = value_rows[p][HEAD_DIM * head : HEAD_DIM * (head + 1)]
                    mixture = mixture + dot(own, e.astype(BF16))
                mixtures.append(mixture * (1.0 / total))
                logs.append(largest + jnp.log(total))
            logs.append(jnp.zeros((8 - heads, span), F32))
            outs[1][group] = jnp.concatenate(logs, axis=0)
            mixed.append(jnp.concatenate(mixtures, axis=0).T.astype(BF16))
        result = jnp.concatenate(mixed, axis=0) if rows > 1 else mixed[0]
        outs[0][...] = result
        if len(weights) > 1:
            store_pieces(outs[2:], dot(result, weight_out.read(flag, wout)))
        else:
            store_pieces(outs[2:], dot(result, wout[0][...]))

    kinds = [shape((tokens, width), BF16), shape((rows, 8, span), F32)]
    kinds += piece_kinds(tokens, weight_out.shape[1], tp)
    flops = 4 * tokens * span * count * heads * 256
    out = call(
        name, body, kinds, queries, marks.marks, *weights, *pieces,
        flags=flags, after=after, flops=flops,
    )
    return out[0], out[1], out[2:]


def attend_back(
    name, upstream, part_rows, weight_out, queries, pieces, marks, logs, flags, rows, near, after=()
):
    tokens, width = queries.shape
    span = tokens // rows
    heads = width // HEAD_DIM
    count = len(pieces)
    first = len(upstream)
    weights = list(weight_out.pair) if isinstance(weight_out, Layer) else [weight_out]

    def body(ins, outs):
        flag, ins = ins[0], ins[1:]
        all_grad = joined(ins[:first], part_rows)
        query_ref, log_ref, mark = ins[first : first + 3]
        wout = ins[first + 3 : first + 3 + len(weights)]
        wout = weight_out.read(flag, wout) if len(weights) > 1 else wout[0][...]
        kv = ins[first + 3 + len(weights) :]
        columns = mark[...].T
        grad_rows = dot(all_grad, wout, 1, 1).astype(BF16)
        for group in range(rows):
            part = slice(group * span, (group + 1) * span)
            grad = grad_rows[part]
            grad_flipped = dot(wout, all_grad[part], 1, 1).astype(BF16)
            scaled = query_ref[part, :] * BF16(SCALE)
            flipped = scaled.T
            key_rows = [ref[part, :width].T for ref in kv]
            masks = [marks.allowed(mark, columns, p, tokens, group, span) for p in range(count)]
            lane = lax.broadcasted_iota(jnp.int32, (span, width), 1)
            key_grads, value_grads, query_grads = [0.0] * count, [0.0] * count, []
            for head in range(heads):
                mine = (lane >= HEAD_DIM * head) & (lane < HEAD_DIM * (head + 1))
                block = head_block(flipped, head, heads)
                grad_block = head_block(grad_flipped, head, heads)
                query_part = jnp.where(mine, scaled, BF16(0.0))
                grad_part = jnp.where(mine, grad, BF16(0.0))
                log_row = log_ref[group, head : head + 1, :]
                shares, share_grads, inner = [], [], 0.0
                for p in range(count):
                    s = jnp.where(masks[p], dot(kv[p][part, :width], block), MASKED_OUT)
                    w = jnp.exp(s - log_row)
                    g = dot(kv[p][part, width:], grad_block)
                    inner = inner + jnp.sum(w * g, axis=0, keepdims=True)
                    value_grads[p] = value_grads[p] + dot(w.astype(BF16), grad_part)
                    shares.append(w)
                    share_grads.append(g)
                query_grad = 0.0
                for p in range(count):
                    score_grad = (shares[p] * (share_grads[p] - inner)).astype(BF16)
                    key_grads[p] = key_grads[p] + dot(score_grad, query_part)
                    own = key_rows[p][HEAD_DIM * head : HEAD_DIM * (head + 1)]
                    query_grad = query_grad + dot(own, score_grad)
                query_grads.append(query_grad)
            outs[0][part, :] = (jnp.concatenate(query_grads, axis=0) * SCALE).T.astype(BF16)
            for p in range(count):
                out, at = (outs[1], p) if p < near else (outs[2], p - near)
                at = slice(at * tokens + group * span, at * tokens + (group + 1) * span)
                out[at, :width] = key_grads[p].astype(out.dtype)
                out[at, width:] = value_grads[p].astype(out.dtype)

    kinds = [
        shape((tokens, width), BF16),
        shape((near * tokens, 2 * width), F32),
        shape(((count - near) * tokens, 2 * width), BF16),
    ]
    flops = 10 * tokens * span * count * heads * 256
    args = (*upstream, queries, logs, marks.marks, *weights, *pieces)
    return call(name, body, kinds, *args, flags=flags, after=after, flops=flops)


def settle_cores(name, mine, theirs, near, after=()):
    tokens = mine.shape[0] // near

    def body(ins, outs):
        total = ins[0][...] + ins[1][...].astype(F32)
        for i, out in enumerate(outs):
            out[...] = total[i * tokens : (i + 1) * tokens].astype(out.dtype)

    dims = (tokens, mine.shape[1])
    return call(
        name, body, [shape(dims, F32)] + [shape(dims, BF16)] * (near - 1), mine, theirs, after=after
    )


def project_back(
    name, flags, weight, pieces, queries=None, own_kv=None, received=(), rider=None, after=()
):
    features, width = weight.shape[1:]
    tokens = (queries if own_kv is None else own_kv).shape[0]
    weights = list(weight.pair) if isinstance(weight, Layer) else [weight]
    args = ([] if queries is None else [queries]) + ([] if own_kv is None else [own_kv, *received])
    riders = [] if rider is None else list(rider[1:])

    def body(ins, outs):
        flag, ins = ins[0], list(ins[1:])

        def chosen(i):
            if len(weights) > 1:
                return weight.read(flag, ins[len(args) : len(args) + 2], i)
            return ins[len(args)][i]

        outs = list(outs)
        total = 0.0
        at = 0
        if queries is not None:
            total = dot(ins[0][...], chosen(0))
            at = 1
        if own_kv is not None:
            kv = summed(ins[at][...], ins[at + 1 : at + 1 + len(received)]).astype(BF16)
            outs.pop(0)[...] = kv
            total = total + dot(kv[:, :features], chosen(1)) + dot(kv[:, features:], chosen(2))
        rows = tokens // pieces
        outs[0][...] = total[:rows]
        for i in range(1, pieces):
            outs[i][:rows] = total[i * rows : (i + 1) * rows].astype(BF16)
            if riders:
                outs[i][rows:] = ins[len(args) + len(weights) + i - 1][...]

    extra = riders[0].shape[0] if riders else 0
    kinds = [] if own_kv is None else [shape(own_kv.shape, BF16)]
    kinds += piece_kinds(tokens, width, pieces, extra)
    out = call(name, body, kinds, *args, *weights, *riders, flags=flags, after=after)
    return out if own_kv is None else (out[0], out[1:])


def turned_products(name, flags, halves, order, per, place, after=(), beside=None):
    columns = sum(r[2] for _, r in halves[0])
    count = len(order)
    arrays, index = [], {}
    for half in halves:
        for (lefts, _), (right, _, _) in half:
            for a in (*lefts, right):
                if id(a) not in index:
                    index[id(a)] = len(arrays)
                    arrays.append(a)
    if beside is not None:
        arrays.append(beside)
    tokens = halves[0][0][1][0].shape[0]
    width = arrays[index[id(halves[0][0][0][0][0])]].shape[1]
    align = 16 if per % 16 == 0 else 8
    kept = BF16 if align == 16 else F32
    n_pairs = len(halves[0])

    def kernel(*refs):
        flag = refs[0]
        ins = refs[1 : 1 + len(arrays)]
        outs = refs[1 + len(arrays) + len(after) :][:2]
        scratch = refs[1 + len(arrays) + len(after) + 2 :]
        first = flag[Flags.FIRST] == 1

        def left_value(half, i):
            lefts, rows = halves[half][i][0]
            return joined([ins[index[id(a)]] for a in lefts], rows)

        def right_value(half, i):
            right, at, size = halves[half][i][1]
            return ins[index[id(right)]][:, at : at + size]

        def same(i):
            a, b = halves[0][i][0], halves[1][i][0]
            return [id(x) for x in a[0]] == [id(x) for x in b[0]] and a[1] == b[1]

        for out_at, out in enumerate(outs):
            at = 0
            for i in range(n_pairs):
                turned = scratch[out_at * n_pairs + i]
                one, two = (0, 1) if out_at == 0 else (1, 0)
                if same(i):
                    left = left_value(0, i)
                else:
                    left = jnp.where(first, left_value(one, i), left_value(two, i))
                right = jnp.where(first, right_value(one, i), right_value(two, i))
                turned[...] = left.astype(kept).T
                size = right.shape[1]
                for k in range(count):
                    start = pl.multiple_of(place(flag, order[k]) * per, align)
                    got = dot(turned[pl.ds(start, per), :].astype(BF16), right)
                    out[k * per : (k + 1) * per, at : at + size] = got.astype(BF16)
                at += size
            for k in range(count if beside is not None else 0):
                start = pl.multiple_of(place(flag, order[k]) * per, align)
                chosen = ins[-1][pl.ds(start, per), :]
                out[k * per : (k + 1) * per, columns:] = chosen

    kind = shape((count * per, columns + (0 if beside is None else beside.shape[1])), BF16)
    moved = sum(math.prod(a.shape) * 2 for a in arrays) + 4 * count * per * columns
    return pl.pallas_call(
        kernel,
        out_shape=[kind, kind],
        in_specs=[pl.BlockSpec(memory_space=pltpu.SMEM)]
        + [pl.BlockSpec(memory_space=pltpu.VMEM)] * len(arrays)
        + [pl.BlockSpec(memory_space=pl.ANY)] * len(after),
        out_specs=[pl.BlockSpec(memory_space=pltpu.VMEM)] * 2,
        scratch_shapes=[pltpu.VMEM((width, tokens), kept)] * (2 * n_pairs),
        compiler_params=pltpu.CompilerParams(vmem_limit_bytes=20 * MIB),
        cost_estimate=pl.CostEstimate(
            flops=4 * tokens * count * per * columns, bytes_accessed=moved, transcendentals=0
        ),
        name=name,
    )(flags, *arrays, *after)


def halved(name, kept, received, last=False, after=()):
    rows, columns = kept.shape

    def body(ins, outs):
        total = ins[0][...].astype(F32) + ins[1][...].astype(F32)
        if last:
            outs[0][...] = total
        else:
            outs[0][...] = total[: rows // 2].astype(BF16)
            outs[1][...] = total[rows // 2 :].astype(BF16)

    kinds = [shape((rows, columns), F32)] if last else [shape((rows // 2, columns), BF16)] * 2
    return call(name, body, kinds, kept, received, after=after)


def one_sided(name, flags, pairs, order, per, place, after=(), sides=1, beside=None):
    arrays, index = [], {}
    for (lefts, _), (right, _, _) in pairs:
        for a in (*lefts, right):
            if id(a) not in index:
                index[id(a)] = len(arrays)
                arrays.append(a)
    if beside is not None:
        arrays.append(beside)
    tokens = pairs[0][1][0].shape[0]
    width = pairs[0][0][0][0].shape[1]
    columns = sum(r[2] for _, r in pairs)
    count = len(order)
    align = 16 if per % 16 == 0 else 8
    kept = BF16 if align == 16 else F32

    def kernel(*refs):
        flag = refs[0]
        ins = refs[1 : 1 + len(arrays)]
        outs = refs[1 + len(arrays) + len(after) :][:sides]
        scratch = refs[1 + len(arrays) + len(after) + sides :]
        at = 0
        for i, ((lefts, rows), (right, first, size)) in enumerate(pairs):
            turned = scratch[i]
            turned[...] = joined([ins[index[id(a)]] for a in lefts], rows).astype(kept).T
            value = ins[index[id(right)]][:, first : first + size]
            for side, out in enumerate(outs):
                for k in range(count):
                    where = place(flag, order[k]) if sides == 1 else place(flag, order[k], side)
                    start = pl.multiple_of(where * per, align)
                    got = dot(turned[pl.ds(start, per), :].astype(BF16), value)
                    out[k * per : (k + 1) * per, at : at + size] = got.astype(BF16)
            at += size
        for k in range(count if beside is not None else 0):
            start = pl.multiple_of(place(flag, order[k]) * per, align)
            outs[0][k * per : (k + 1) * per, columns:] = ins[-1][pl.ds(start, per), :]

    kind = shape((count * per, columns + (0 if beside is None else beside.shape[1])), BF16)
    moved = sum(math.prod(a.shape) * 2 for a in arrays) + 2 * sides * count * per * columns
    return pl.pallas_call(
        kernel,
        out_shape=[kind] * sides,
        in_specs=[pl.BlockSpec(memory_space=pltpu.SMEM)]
        + [pl.BlockSpec(memory_space=pltpu.VMEM)] * len(arrays)
        + [pl.BlockSpec(memory_space=pl.ANY)] * len(after),
        out_specs=[pl.BlockSpec(memory_space=pltpu.VMEM)] * sides,
        scratch_shapes=[pltpu.VMEM((width, tokens), kept)] * len(pairs),
        compiler_params=pltpu.CompilerParams(vmem_limit_bytes=16 * MIB),
        cost_estimate=pl.CostEstimate(
            flops=2 * sides * tokens * count * per * columns, bytes_accessed=moved, transcendentals=0
        ),
        name=name,
    )(flags, *arrays, *after)


def on_device(
    hidden,
    segments,
    self_qkv,
    self_out,
    ffn_in,
    ffn_in_bias,
    ffn_out,
    norm_gains,
    norm_shifts,
    cross_qkv,
    cross_out,
    cross_gain,
    cross_shift,
    cotangent,
):
    section, seq, tp = (lax.axis_index(a) for a in ("section", "seq", "tp"))
    n_seq, n_tp = lax.axis_size("seq"), lax.axis_size("tp")
    half = n_seq // 2
    low_half = seq < half
    on_first = section == 0
    settled = on_first == low_half
    rows, span, width = hidden.shape[2:]
    tokens = rows * span
    sub = tokens // n_tp
    units = ffn_in.shape[2]
    features = cross_out.shape[0]
    flags = jnp.stack([on_first, low_half, settled, tp, seq]).astype(jnp.int32)

    both = ("section", "seq")
    low = range(half)
    to_encoder = [(z, z + half) for z in low] + [(z + half, n_seq + z) for z in low]
    to_decoder = [(n_seq + z, z + half) for z in low] + [(n_seq + z + half, n_seq + z) for z in low]
    across = [(z + half, n_seq + z + half) for z in low] + [(n_seq + z, z) for z in low]

    both_micro = hidden[0].reshape(2, tokens, width)
    far = jnp.where(low_half, both_micro[1], both_micro[0])
    near = jnp.where(low_half, both_micro[0], both_micro[1])
    far_enc = lax.ppermute(far, both, to_encoder)
    core = lax.ppermute(near, both, across)

    def layers(own):
        other = swap_cores(own)
        return Layer(1, own, other), Layer(0, own, other)

    qkv_enc, qkv_dec = layers(jnp.swapaxes(self_qkv[0], 1, 2))
    cross_turned = jnp.swapaxes(cross_qkv, 1, 2)

    def pack(ins, outs):
        zeros = jnp.zeros((2, width), F32)
        outs[0][...] = jnp.concatenate([ins[0][...], ins[1][...], ins[2][...], zeros], axis=0)
        put_rows(outs[1], [ins[3][...], ins[4][...]])

    vectors, vec_cross = call(
        "pack", pack, [shape((8, width), F32)] * 2,
        norm_gains[0], norm_shifts[0], ffn_in_bias[0], cross_gain[None], cross_shift[None],
    )
    vec_enc, vec_dec = layers(vectors)
    out_enc, out_dec = layers(self_out[0])
    win_enc, win_dec = layers(ffn_in[0])
    wout_enc, wout_dec = layers(ffn_out[0])

    small, sums_kind = shape((sub, width), BF16), shape((8, width), F32)

    def cut(ins, outs):
        flag, cot = ins
        at = pl.ds(pl.multiple_of(flag[Flags.TP] * sub, sub), sub)
        low_here = flag[Flags.LOW] == 1
        outs[0][...] = jnp.where(low_here, cot[0, at, :], cot[1, at, :])
        outs[1][...] = jnp.where(low_here, cot[1, at, :], cot[0, at, :])

    cot_near, cot_far = call(
        "cut", cut, [small] * 2, cotangent.reshape(2, tokens, width), flags=flags
    )
    cot_moved = lax.ppermute(
        cot_far, both, [(z, z + half) for z in low] + [(n_seq + z + half, n_seq + z) for z in low]
    )

    n_chunks = 2 * half
    n_keys = n_chunks * tokens
    place = np.broadcast_to(np.arange(n_chunks * span, dtype=np.int32), (1, rows, n_chunks * span))
    base = jnp.concatenate([segments.reshape(4, rows, n_chunks * span), jnp.asarray(place)])
    base = base.reshape(5, rows, n_chunks, span).transpose(0, 2, 1, 3).reshape(5, n_keys)
    z_bits, tp_bits = half.bit_length() - 1, n_tp.bit_length() - 1

    def turn_marks(ins, outs):
        flag, ref = ins
        low_here = flag[Flags.LOW] == 1
        found = jnp.concatenate(
            [
                jnp.where(low_here, ref[0:1, :], ref[1:2, :]),
                jnp.where(low_here, ref[2:3, :], ref[3:4, :]),
                ref[4:5, :],
                jnp.zeros((5, n_keys), jnp.int32),
            ],
            axis=0,
        )
        lane = lax.broadcasted_iota(jnp.int32, found.shape, 1)
        turns = [(1 - flag[Flags.FIRST], half * tokens)]
        turns += [((flag[Flags.SEQ] >> b) & 1, tokens << b) for b in range(z_bits)]
        turns += [((flag[Flags.TP] >> b) & 1, sub << b) for b in range(tp_bits)]
        for turn, step in turns:
            up, down = pltpu.roll(found, step, 1), pltpu.roll(found, n_keys - step, 1)
            other = jnp.where((lane & step) != 0, up, down)
            found = jnp.where(turn == 1, other, found)
        outs[0][...] = found

    (marks,) = call("marks", turn_marks, [shape((8, n_keys), jnp.int32)], base, flags=flags)
    marks_enc = Marks(marks, KEY_ENC, KEY_ENC, False)
    marks_dec = Marks(marks, KEY_DEC, KEY_DEC, True)
    marks_cross = Marks(marks, KEY_DEC, KEY_ENC, False)

    def share(own):
        mine = [own] + [xor_perm(own, "seq", dz) for dz in range(1, half)]
        return mine + [swap_cores(block) for block in mine]

    def settle(name, near_kv, far_kv, after=()):
        own, *sent = settle_cores(name, near_kv, swap_cores(far_kv), half, after)
        return own, [xor_perm(block, "seq", dz + 1) for dz, block in enumerate(sent)]

    top, bottom = slice(0, sub), slice(sub, 2 * sub)

    input_enc, q_enc, kv_enc, far_later = settle_input(
        "qkv_enc", near, core, far_enc, flags, qkv_enc, 1, after=[marks, *vec_enc.pair], pass_on=far
    )
    far_dec = lax.ppermute(far_later, both, to_decoder)
    all_enc = share(kv_enc)
    a_enc, log_enc, part = attend(
        "attend_enc", q_enc, all_enc, marks_enc, out_enc, flags, rows, n_tp,
        after=[cot_moved, far_dec],
    )
    got = scatter_tp(part[1:])
    input_dec, q_dec, kv_dec = settle_input(
        "qkv_dec", near, core, far_dec, flags, qkv_dec, 0, after=[a_enc]
    )

    def norm_first(ins, outs):
        flag, ins = ins[0], ins[1:]
        total = summed(ins[0][...], ins[1:n_tp]) + ins[n_tp][:sub].astype(F32)
        vec = vec_enc.read(flag, ins[n_tp + 1 : n_tp + 3])
        unit, _ = normalized(total)
        result = unit * vec[GAIN_ATT : GAIN_ATT + 1] + vec[SHIFT_ATT : SHIFT_ATT + 1]
        outs[0][...] = total
        outs[1][...] = result.astype(BF16)

    full = shape((sub, width), F32)
    small_sums = shape((sub + VECTOR_ROWS, width), BF16)
    double_sums = shape((2 * sub + VECTOR_ROWS, width), BF16)
    z1_enc, h1b_enc = call(
        "norm_att_enc", norm_first, [full, small], part[0], *got, input_enc, *vec_enc.pair,
        flags=flags, after=[kv_dec],
    )
    h1_pieces_enc = gather_tp(h1b_enc)

    all_dec = share(kv_dec)
    a_dec, log_dec, part_dec = attend(
        "attend_dec", q_dec, all_dec, marks_dec, out_dec, flags, rows, n_tp
    )

    u_enc, g_enc, part = feed_forward(
        "ffn_enc", h1_pieces_enc, win_enc, vec_enc, wout_enc, flags, rider=part_dec
    )
    got = scatter_tp(part[1:])

    def norm_second(ins, outs):
        flag, ins = ins[0], ins[1:]
        own_enc, own_dec, z1, inputs = ins[:4]
        received = ins[4 : 3 + n_tp]
        vec = vec_enc.read(flag, ins[3 + n_tp : 5 + n_tp])
        unit, _ = normalized(z1[...])
        h1 = unit * vec[GAIN_ATT : GAIN_ATT + 1] + vec[SHIFT_ATT : SHIFT_ATT + 1]
        total = summed(own_enc[...], received, top) + h1 + vec[BIAS_OUT : BIAS_OUT + 1]
        unit, _ = normalized(total)
        memory = unit * vec[GAIN_END : GAIN_END + 1] + vec[SHIFT_END : SHIFT_END + 1]
        outs[0][...] = total
        outs[1][...] = memory.astype(BF16)
        outs[3][:sub] = memory.astype(BF16)
        vec = vec_dec.read(flag, ins[3 + n_tp : 5 + n_tp])
        total = summed(own_dec[...], received, bottom) + inputs[:sub].astype(F32)
        unit, _ = normalized(total)
        result = unit * vec[GAIN_ATT : GAIN_ATT + 1] + vec[SHIFT_ATT : SHIFT_ATT + 1]
        outs[2][...] = total
        outs[3][sub:] = result.astype(BF16)

    double = shape((2 * sub, width), BF16)
    z2_enc, memory, z1_dec, message = call(
        "norm_end_enc", norm_second, [full, small, full, double],
        part[0], part_dec[0], z1_enc, input_dec, *got, *vec_enc.pair, flags=flags,
    )
    mid_pieces = gather_tp(message)

    def cross_projections(ins, outs):
        refs, weight = ins[:n_tp], ins[n_tp]
        values = joined(refs, top)
        for i in (1, 2):
            outs[0][:, (i - 1) * features : i * features] = dot(values, weight[i], 1, 1).astype(BF16)
        outs[1][...] = dot(joined(refs, bottom), weight[0], 1, 1).astype(BF16)

    kv_cross, q_cross = call(
        "qkv_cross", cross_projections,
        [shape((tokens, 2 * features), BF16), shape((tokens, features), BF16)],
        *mid_pieces, cross_turned,
    )
    all_cross = share(kv_cross)
    a_cross, log_cross, part = attend(
        "attend_cross", q_cross, all_cross, marks_cross, cross_out, flags, rows, n_tp
    )
    got = scatter_tp(part[1:])

    def norm_crossed(ins, outs):
        flag, ins = ins[0], ins[1:]
        vec = vec_dec.read(flag, ins[n_tp + 2 : n_tp + 4])
        unit, _ = normalized(ins[n_tp][...])
        h1 = unit * vec[GAIN_ATT : GAIN_ATT + 1] + vec[SHIFT_ATT : SHIFT_ATT + 1]
        total = summed(ins[0][...], ins[1:n_tp]) + h1
        vec = ins[n_tp + 1]
        unit, _ = normalized(total)
        outs[0][...] = total
        outs[1][...] = (unit * vec[0:1] + vec[1:2]).astype(BF16)

    z_cross, h2b = call(
        "norm_cross", norm_crossed, [full, small], part[0], *got, z1_dec, vec_cross,
        *vec_dec.pair, flags=flags,
    )
    h2_pieces = gather_tp(h2b)
    u_dec, g_dec, part = feed_forward("ffn_dec", h2_pieces, win_dec, vec_dec, wout_dec, flags)
    got = scatter_tp(part[1:])

    def norm_turn(ins, outs):
        flag, ins = ins[0], ins[1:]
        crossed, cot_here, cot_there, cross_vec = ins[n_tp : n_tp + 4]
        vec = vec_dec.read(flag, ins[n_tp + 4 : n_tp + 6])
        unit, _ = normalized(crossed[...])
        h2 = unit * cross_vec[0:1] + cross_vec[1:2]
        total = summed(ins[0][...], ins[1:n_tp]) + h2 + vec[BIAS_OUT : BIAS_OUT + 1]
        unit, _ = normalized(total)
        gain = vec[GAIN_END : GAIN_END + 1]
        decoded = (unit * gain + vec[SHIFT_END : SHIFT_END + 1]).astype(BF16)
        upstream = jnp.where(flag[Flags.SETTLED] == 1, cot_here[...], cot_there[...]).astype(F32)
        grad, gain_grad, shift_grad = norm_back(total, gain, upstream)
        outs[0][...] = grad
        outs[1][:sub] = grad.astype(BF16)
        put_vectors(outs[1], sub, [gain_grad, shift_grad, jnp.sum(grad, axis=0, keepdims=True)])
        outs[2][...] = decoded

    dz2_dec, dz2b_dec, decoded = call(
        "norm_end_dec", norm_turn, [full, small_sums, small],
        part[0], *got, z_cross, cot_near, cot_moved, vec_cross, *vec_dec.pair, flags=flags,
    )

    bits = n_seq.bit_length() - 1
    order = sorted(range(n_seq), key=lambda r: int(format(r, f"0{bits}b")[::-1], 2))

    def seq_place(flag, r):
        return flag[Flags.SEQ] ^ r

    def grads_start(name, halves, the_order, per, place, after=(), beside=None):
        mine, theirs = turned_products(name, flags, halves, the_order, per, place, after, beside)
        return mine, swap_cores(theirs)

    def grads_step(name, state, step, after=()):
        kept, received = state
        if step == bits:
            (total,) = halved(f"{name}_sum", kept, received, last=True, after=after)
            return total
        kept, sent = halved(f"{name}_add{step}", kept, received, after=after)
        return kept, xor_perm(sent, "seq", 1 << step)

    def grads_finish(name, state, step=0, after=()):
        while isinstance(state, tuple):
            state = grads_step(name, state, step, after)
            step += 1
        return state

    def self_grads(name, member, pairs, after=(), beside=None):
        (block,) = one_sided(name, flags, pairs, order, per, seq_place, after, beside=beside)
        keeper = 1 - member
        return block, lax.ppermute(block, "section", [(1 - keeper, keeper)])

    def self_step(name, member, state, step, after=()):
        kept, received = state
        if step == bits:
            (total,) = halved(f"{name}_sum", kept, received, last=True, after=after)
            return total
        kept, sent = halved(f"{name}_add{step}", kept, received, after=after)
        at = (1 - member) * n_seq
        route = [(at + z, at + (z ^ (1 << step))) for z in range(n_seq)]
        return kept, lax.ppermute(sent, both, route)

    def self_finish(name, member, state, step, after=()):
        while isinstance(state, tuple):
            state = self_step(name, member, state, step, after)
            step += 1
        return state

    per = width // n_seq
    anything = slice(None)

    r_pieces_dec = gather_tp(dz2b_dec)
    du_dec, sums_in_dec, part = feed_backward(
        "ffn_back_dec", r_pieces_dec, top, u_dec, win_dec, wout_dec, flags
    )
    ffn_dec_state = grads_start(
        "grad_ffn_dec",
        [
            [((h2_pieces, anything), (du_dec, 0, units))],
            [((r_pieces_dec, top), (g_dec, 0, units))],
        ],
        order, per, seq_place,
    )

    got = scatter_tp(part[1:])

    def norm_cross_back(ins, outs):
        upstream = summed(ins[0][...], ins[1:n_tp]) + ins[n_tp][...]
        grad, gain_grad, shift_grad = norm_back(ins[n_tp + 1][...], ins[n_tp + 2][0:1], upstream)
        outs[0][...] = grad
        outs[1][:sub] = grad.astype(BF16)
        put_vectors(outs[1], sub, [gain_grad, shift_grad])

    dzc, dzcb = call(
        "norm_back_cross", norm_cross_back, [full, small_sums],
        part[0], *got, dz2_dec, z_cross, vec_cross, after=[ffn_dec_state[0]],
    )
    dzc_pieces = gather_tp(dzcb)
    ffn_dec_state = grads_step("grad_ffn_dec", ffn_dec_state, 0, after=[dzc])

    dq_cross, near_kv, far_kv = attend_back(
        "attend_back_cross", dzc_pieces, top, cross_out, q_cross, all_cross, marks_cross,
        log_cross, flags, rows, half, after=[ffn_dec_state[0]],
    )
    own_kv, received_kv = settle("settle_cross", near_kv, far_kv)
    part_query = project_back("query_back", flags, cross_turned, n_tp, queries=dq_cross)
    dkv_cross, part = project_back(
        "memory_back", flags, cross_turned, n_tp, own_kv=own_kv, received=received_kv,
        rider=part_query,
    )
    got = scatter_tp(part[1:])
    per_cross = width // (2 * n_seq)

    def cross_place(flag, r, side):
        return ((1 - flag[Flags.FIRST]) ^ side) * n_seq + (flag[Flags.SEQ] ^ r)

    cross_pairs = [
        ((mid_pieces, bottom), (dq_cross, 0, features)),
        ((mid_pieces, top), (dkv_cross, 0, 2 * features)),
        ((dzc_pieces, top), (a_cross, 0, features)),
    ]
    mine, theirs = one_sided("grad_cross", flags, cross_pairs, order, per_cross, cross_place, sides=2)
    cross_state = mine, swap_cores(theirs)

    def norm_middle_back(ins, outs):
        flag, ins = ins[0], ins[1:]
        own_memory, own_query, residual, z2, z1 = ins[:5]
        received = ins[5 : 4 + n_tp]
        vec = vec_enc.read(flag, ins[4 + n_tp : 6 + n_tp])
        upstream = summed(own_memory[...], received, top).astype(BF16).astype(F32)
        grad, gain_grad, shift_grad = norm_back(z2[...], vec[GAIN_END : GAIN_END + 1], upstream)
        sums = [gain_grad, shift_grad, jnp.sum(grad, axis=0, keepdims=True)]
        outs[0][...] = grad
        outs[2][:sub] = grad.astype(BF16)
        vec = vec_dec.read(flag, ins[4 + n_tp : 6 + n_tp])
        upstream = summed(own_query[...], received, bottom) + residual[...]
        grad, gain_grad, shift_grad = norm_back(z1[...], vec[GAIN_ATT : GAIN_ATT + 1], upstream)
        outs[1][...] = grad
        outs[2][sub : 2 * sub] = grad.astype(BF16)
        put_vectors(outs[2], 2 * sub, sums + [gain_grad, shift_grad])

    dz2_enc, dz1_dec, message = call(
        "norm_back_end_enc", norm_middle_back, [full, full, double_sums],
        part[0], part_query[0], dzc, z2_enc, z1_dec, *got, *vec_enc.pair, flags=flags,
        after=[cross_state[0]],
    )
    back_pieces = gather_tp(message)

    cross_state = grads_step("grad_cross", cross_state, 0, after=[dz2_enc])
    ffn_dec_state = grads_step("grad_ffn_dec", ffn_dec_state, 1, after=[dz2_enc])
    du_enc, sums_in_enc, part = feed_backward(
        "ffn_back_enc", back_pieces, top, u_enc, win_enc, wout_enc, flags,
        after=[cross_state[0], ffn_dec_state[0]],
    )
    got = scatter_tp(part[1:])
    dq_dec, near_kv, far_kv = attend_back(
        "attend_back_dec", back_pieces, bottom, out_dec, q_dec, all_dec, marks_dec,
        log_dec, flags, rows, half, after=[du_enc],
    )

    n_vec, n_columns = 14, 128

    def vector_columns(ins, outs):
        end_dec, cross, mid = (ins[i * n_tp : (i + 1) * n_tp] for i in range(3))
        in_enc, in_dec = ins[3 * n_tp : 3 * n_tp + 2]
        mid_rows = vector_sums(mid, 2 * sub, 5)
        zero = jnp.zeros((1, width), F32)
        dec_rows = vector_sums(end_dec, sub, 3)
        cross_rows = vector_sums(cross, sub, 2)
        found = [
            zero, mid_rows[0:1], zero, mid_rows[1:3], in_enc[0:1],
            mid_rows[3:4], dec_rows[0:1], mid_rows[4:5], dec_rows[1:3], in_dec[0:1],
            cross_rows, jnp.zeros((n_columns - n_vec, width), F32),
        ]
        columns = jnp.concatenate(found, axis=0).T
        moved = jnp.concatenate(
            [
                columns[(core * n_seq + z) * per_cross : (core * n_seq + z + 1) * per_cross]
                for z in range(n_seq)
                for core in range(2)
            ],
            axis=0,
        )
        lane = lax.broadcasted_iota(jnp.int32, columns.shape, 1)
        outs[0][...] = jnp.where(lane >= n_vec - 2, moved, columns).astype(BF16)

    (vectors_here,) = call(
        "vector_columns", vector_columns, [shape((width, n_columns), BF16)],
        *r_pieces_dec, *dzc_pieces, *back_pieces, sums_in_enc, sums_in_dec,
    )
    ffn_enc_state = grads_start(
        "grad_ffn_enc",
        [
            [((h1_pieces_enc, anything), (du_enc, 0, units))],
            [((back_pieces, top), (g_enc, 0, units))],
        ],
        order, per, seq_place, after=[dq_dec], beside=vectors_here,
    )

    dec_kv, dec_received = settle("settle_dec", near_kv, far_kv)

    def norm_first_back(ins, outs):
        flag, ins = ins[0], ins[1:]
        upstream = summed(ins[0][...], ins[1:n_tp]) + ins[n_tp][...]
        vec = vec_enc.read(flag, ins[n_tp + 2 : n_tp + 4])
        grad, gain_grad, shift_grad = norm_back(
            ins[n_tp + 1][...], vec[GAIN_ATT : GAIN_ATT + 1], upstream
        )
        outs[0][...] = grad
        outs[1][:sub] = grad.astype(BF16)
        put_vectors(outs[1], sub, [gain_grad, shift_grad])

    dz1_enc, dz1b_enc = call(
        "norm_back_att_enc", norm_first_back, [full, small_sums],
        part[0], *got, dz2_enc, z1_enc, *vec_enc.pair, flags=flags,
        after=[dec_kv, ffn_enc_state[0]],
    )
    dz1_pieces_enc = gather_tp(dz1b_enc)


    dkv_dec, part_dec = project_back(
        "input_back_dec", flags, qkv_dec, n_tp, queries=dq_dec, own_kv=dec_kv,
        received=dec_received, after=[dz1_enc],
    )
    ffn_enc_state = grads_step("grad_ffn_enc", ffn_enc_state, 0, after=[dz1_enc])
    ffn_dec = grads_finish("grad_ffn_dec", ffn_dec_state, 2, after=[dkv_dec])
    cross_state = grads_step("grad_cross", cross_state, 1, after=[dkv_dec])
    dq_enc, near_kv, far_kv = attend_back(
        "attend_back_enc", dz1_pieces_enc, top, out_enc, q_enc, all_enc, marks_enc,
        log_enc, flags, rows, half, after=[ffn_dec, ffn_enc_state[0], cross_state[0]],
    )
    own_kv, received_kv = settle("settle_enc", near_kv, far_kv)
    self_dec_state = self_grads(
        "grad_self_dec", 0,
        [
            (([input_dec], anything), (dq_dec, 0, features)),
            (([input_dec], anything), (dkv_dec, 0, 2 * features)),
            ((back_pieces, bottom), (a_dec, 0, features)),
        ],
        after=[own_kv],
    )
    ffn_enc_state = grads_step("grad_ffn_enc", ffn_enc_state, 1, after=[self_dec_state[0]])
    dkv_enc, part = project_back(
        "input_back_enc", flags, qkv_enc, n_tp, queries=dq_enc, own_kv=own_kv,
        received=received_kv, rider=part_dec, after=[ffn_enc_state[0]],
    )
    got = scatter_tp(part[1:])
    def att_columns(ins, outs):
        found = [vector_sums(ins, sub, 2), jnp.zeros((n_columns - 2, width), F32)]
        outs[0][...] = jnp.concatenate(found, axis=0).T.astype(BF16)

    (vectors_att,) = call(
        "vector_columns_att", att_columns, [shape((width, n_columns), BF16)], *dz1_pieces_enc,
        after=[part[0]],
    )
    self_enc_state = self_grads(
        "grad_self_enc", 1,
        [
            (([input_enc], anything), (dq_enc, 0, features)),
            (([input_enc], anything), (dkv_enc, 0, 2 * features)),
            ((dz1_pieces_enc, top), (a_enc, 0, features)),
        ],
        after=[part[0]], beside=vectors_att,
    )
    self_dec_state = self_step("grad_self_dec", 0, self_dec_state, 0, after=[part[0]])
    cross_sum = grads_finish("grad_cross", cross_state, 2, after=[self_dec_state[0]])


    def input_sums(ins, outs):
        flag, ins = ins[0], ins[1:]
        received = ins[4 : 3 + n_tp]
        enc = (summed(ins[0][...], received, top) + ins[2][...]).astype(BF16)
        dec = (summed(ins[1][...], received, bottom) + ins[3][...]).astype(BF16)
        enc = jnp.concatenate([ins[3 + n_tp][...], enc], axis=0)
        dec = jnp.concatenate([ins[4 + n_tp][...], dec], axis=0)
        outs[0][...] = enc
        outs[1][...] = dec
        outs[2][...] = jnp.where(flag[Flags.FIRST] == 1, dec, enc)

    done_enc, done_dec, done_across = call(
        "input_sums", input_sums, [double, double, double],
        part[0], part_dec[0], dz1_enc, dz1_dec, *got, memory, decoded, flags=flags,
        after=[self_enc_state[0], cross_sum],
    )
    self_enc_state = self_step("grad_self_enc", 1, self_enc_state, 0, after=[done_enc])
    self_dec_state = self_step("grad_self_dec", 0, self_dec_state, 1, after=[self_enc_state[0]])
    ffn_enc = grads_finish("grad_ffn_enc", ffn_enc_state, 2, after=[self_enc_state[0]])

    far_enc = lax.ppermute(done_enc, both, [(b, a) for a, b in to_encoder])
    far_dec = lax.ppermute(done_dec, both, [(b, a) for a, b in to_decoder])
    from_core = lax.ppermute(done_across, both, [(b, a) for a, b in across])

    def order_body(ins, outs):
        flag = ins[0]
        first = flag[Flags.FIRST] == 1
        stays = jnp.where(first, ins[1][...], ins[2][...])
        near = jnp.where(flag[Flags.SETTLED] == 1, stays, ins[3][...])
        far = jnp.where(first, ins[4][...], ins[5][...])
        low_here = flag[Flags.LOW] == 1
        outs[0][: 2 * sub] = jnp.where(low_here, near, far)
        outs[0][2 * sub :] = jnp.where(low_here, far, near)

    (found,) = call(
        "outputs_order", order_body, [shape((4 * sub, width), BF16)],
        done_enc, done_dec, from_core, far_enc, far_dec, flags=flags,
        after=[self_dec_state[0], ffn_enc],
    )
    self_enc_state = self_step("grad_self_enc", 1, self_enc_state, 1, after=[found])
    self_dec = self_finish("grad_self_dec", 0, self_dec_state, 2, after=[self_enc_state[0]])
    self_enc = self_finish("grad_self_enc", 1, self_enc_state, 2, after=[self_dec])
    pieces = gather_tp(found)
    def to_other(ins, outs):
        outs[0][...] = jnp.where(ins[0][Flags.FIRST] == 1, ins[1][...], ins[2][:, :units])

    (sent,) = call(
        "grad_swap", to_other, [shape((per, units), F32)], ffn_dec, ffn_enc, flags=flags, after=[found]
    )
    swapped = swap_cores(sent)

    def finish(ins, outs):
        flag, dec_ffn, enc_ffn, other = ins
        first = flag[Flags.FIRST] == 1
        mine = jnp.where(first, enc_ffn[:, :units], dec_ffn[...])
        theirs = other[...]
        outs[0][...] = jnp.where(first, mine, theirs)
        outs[1][...] = jnp.where(first, theirs, mine)
        table = enc_ffn[:, units:].T
        vectors_here = jnp.where(first, table[0:6], table[6:12])
        outs[2][...] = jnp.concatenate([vectors_here, jnp.zeros((2, per), F32)], axis=0)
        outs[3][...] = vectors_here[5:6]
        crossed = table[n_vec - 2 : n_vec]
        crossed = jnp.where(first, crossed[:, :per_cross], crossed[:, per_cross:])
        outs[4][...] = crossed[0:1]
        outs[5][...] = crossed[1:2]

    grad_in, grad_out, layer_vectors, grad_bias, grad_cross_gain, grad_cross_shift = call(
        "finish_ffn", finish,
        [shape((per, units), F32)] * 2
        + [shape((8, per), F32), shape((1, per), F32)]
        + [shape((1, per_cross), F32)] * 2,
        ffn_dec, ffn_enc, swapped, flags=flags,
    )


    def place_body(ins, outs):
        here = ins[0][Flags.TP]
        for i, ref in enumerate(ins[1:]):
            at = pl.ds(pl.multiple_of((here ^ i) * sub, sub), sub)
            for micro in range(2):
                first_row = 2 * micro * sub
                outs[0][micro, at, :] = ref[first_row : first_row + sub]
                outs[1][micro, at, :] = ref[first_row + sub : first_row + 2 * sub]

    layer_out, grad_hidden = call(
        "outputs_place", place_body, [shape((2, tokens, width), BF16)] * 2, *pieces, flags=flags,
        after=[self_enc, grad_in],
    )

    def finish_cross(ins, outs):
        whole = ins[0][...]
        for i in range(3):
            outs[0][i] = whole[:, i * features : (i + 1) * features]
        outs[1][...] = whole[:, 3 * features :].T

    grad_cross_qkv, grad_cross_out = call(
        "finish_cross", finish_cross,
        [shape((3, per_cross, features), F32), shape((features, per_cross), F32)], cross_sum,
    )

    def finish_self(ins, outs):
        first = ins[0][Flags.FIRST] == 1
        whole = jnp.where(first, ins[1][:, : 4 * features], ins[2][...])
        own = ins[3][...]
        att = ins[1][:, 4 * features :].T
        outs[2][0:1] = own[0:1] + jnp.where(first, att[0:1], 0.0)
        outs[2][1:2] = own[1:2]
        outs[3][0:1] = own[2:3] + jnp.where(first, att[1:2], 0.0)
        outs[3][1:3] = own[3:5]
        for i in range(3):
            outs[0][i] = whole[:, i * features : (i + 1) * features]
        outs[1][...] = whole[:, 3 * features :].T

    grad_qkv, grad_self_out, grad_gains, grad_shifts = call(
        "finish_self", finish_self,
        [
            shape((3, per, features), F32), shape((features, per), F32),
            shape((2, per), F32), shape((3, per), F32),
        ],
        self_enc, self_dec, layer_vectors, flags=flags,
    )

    return (
        layer_out.reshape(1, 2, rows, span, width),
        grad_hidden.reshape(1, 2, rows, span, width),
        grad_qkv[None],
        grad_self_out[None],
        grad_in[None],
        grad_bias[None],
        grad_out.T[None],
        grad_gains[None],
        grad_shifts[None],
        grad_cross_qkv,
        grad_cross_out,
        grad_cross_gain[0],
        grad_cross_shift[0],
    )


def solution(mesh):
    return jax.shard_map(
        on_device,
        mesh=mesh,
        in_specs=(
            P("section", None, None, "seq", None),
            P(),
            P("section", None, None, "tp"),
            P("section", "tp", None),
            P("section", None, "tp"),
            P("section", "tp", None),
            P("section", "tp", None),
            P("section", None, None),
            P("section", None, None),
            P(None, None, "tp"),
            P("tp", None),
            P(),
            P(),
            P(None, None, "seq", None),
        ),
        out_specs=(
            P("section", None, None, "seq", None),
            P("section", None, None, "seq", None),
            P("section", None, "seq", "tp"),
            P("section", "tp", "seq"),
            P("section", "seq", "tp"),
            P("section", "tp", "seq"),
            P("section", "tp", "seq"),
            P("section", None, "seq"),
            P("section", None, "seq"),
            P(None, ("section", "seq"), "tp"),
            P("tp", ("section", "seq")),
            P(("section", "seq")),
            P(("section", "seq")),
        ),
        check_vma=False,
    )
```

```python
import math

import jax
import jax.numpy as jnp
import numpy as np
from jax import lax
from jax.experimental import pallas as pl
from jax.experimental.pallas import tpu as pltpu
from jax.sharding import PartitionSpec as P

HEAD_DIM = 64
EPSILON = 1e-05
MASKED_OUT = -1e30
SCALE = 1.0 / math.sqrt(HEAD_DIM)
F32 = jnp.float32
BF16 = jnp.bfloat16
MIB = 1 << 20

GAIN_ATT, GAIN_END, SHIFT_ATT, SHIFT_END, BIAS_OUT, BIAS_IN = range(6)


def shape(dims, kind):
    return jax.ShapeDtypeStruct(dims, kind)


def dot(left, right, left_dim=1, right_dim=0):
    return lax.dot_general(
        left, right, (((left_dim,), (right_dim,)), ((), ())), preferred_element_type=F32
    )


class Flags:
    FIRST, LOW, SETTLED, TP, SEQ = range(5)


def call(name, body, outs, *args, flags=None, after=(), flops=0, vmem=16 * MIB):
    scalars = [] if flags is None else [flags]
    after = list(after)
    count = len(scalars) + len(args)

    def kernel(*refs):
        body(refs[:count], refs[count + len(after) :])

    moved = sum(math.prod(a.shape) * a.dtype.itemsize for a in (*args, *outs))
    in_specs = [pl.BlockSpec(memory_space=pltpu.SMEM)] * len(scalars)
    in_specs += [pl.BlockSpec(memory_space=pltpu.VMEM)] * len(args)
    in_specs += [pl.BlockSpec(memory_space=pl.ANY)] * len(after)
    return pl.pallas_call(
        kernel,
        out_shape=outs,
        in_specs=in_specs,
        out_specs=[pl.BlockSpec(memory_space=pltpu.VMEM)] * len(outs),
        compiler_params=pltpu.CompilerParams(vmem_limit_bytes=vmem),
        cost_estimate=pl.CostEstimate(flops=flops, bytes_accessed=moved, transcendentals=0),
        name=name,
    )(*scalars, *args, *after)


def swap_cores(block):
    return lax.ppermute(block, "section", [(0, 1), (1, 0)])


def xor_perm(block, axis, bits):
    return lax.ppermute(block, axis, [(i, i ^ bits) for i in range(lax.axis_size(axis))])


def scatter_tp(pieces):
    order = sorted(range(1, len(pieces) + 1), key=lambda i: -bin(i).count("1"))
    got = {i: xor_perm(pieces[i - 1], "tp", i) for i in order}
    return [got[i] for i in range(1, len(pieces) + 1)]


def gather_tp(block):
    return [block] + scatter_tp([block] * (lax.axis_size("tp") - 1))


def normalized(values):
    centred = values - jnp.mean(values, axis=-1, keepdims=True)
    spread = jnp.mean(centred * centred, axis=-1, keepdims=True)
    inverse = lax.rsqrt(spread + EPSILON)
    return centred * inverse, inverse


def norm_back(values, gain, upstream):
    unit, inverse = normalized(values)
    scaled = gain * upstream
    grad = (
        scaled
        - jnp.mean(scaled, axis=-1, keepdims=True)
        - unit * jnp.mean(scaled * unit, axis=-1, keepdims=True)
    ) * inverse
    gain_grad = jnp.sum(upstream * unit, axis=0, keepdims=True)
    shift_grad = jnp.sum(upstream, axis=0, keepdims=True)
    return grad, gain_grad, shift_grad


def put_rows(ref, rows):
    width = ref.shape[1]
    ref[...] = jnp.concatenate(rows + [jnp.zeros((8 - len(rows), width), F32)], axis=0)


VECTOR_ROWS = 16


def put_vectors(ref, at, rows):
    half = VECTOR_ROWS // 2
    whole = jnp.concatenate(rows + [jnp.zeros((half - len(rows), ref.shape[1]), F32)], axis=0)
    top = whole.astype(BF16)
    left = (whole - top.astype(F32)).astype(BF16)
    ref[at : at + VECTOR_ROWS] = jnp.concatenate([top, left], axis=0)


def vector_sums(refs, at, count):
    half = VECTOR_ROWS // 2
    total = 0.0
    for ref in refs:
        rows = ref[at : at + VECTOR_ROWS].astype(F32)
        total = total + (rows[:half] + rows[half:])
    return total[:count]


def summed(own, received, part=slice(None)):
    total = own
    for ref in received:
        total = total + ref[part].astype(F32)
    return total


def joined(refs, part=slice(None)):
    return jnp.concatenate([ref[part] for ref in refs], axis=0)


def store_pieces(refs, value):
    rows = refs[0].shape[0]
    for i, ref in enumerate(refs):
        ref[...] = value[i * rows : (i + 1) * rows].astype(ref.dtype)


def piece_kinds(tokens, width, count, extra=0):
    rows = tokens // count
    return [shape((rows, width), F32)] + [shape((rows + extra, width), BF16)] * (count - 1)


class Layer:
    def __init__(self, mine, own, other):
        self.mine, self.pair = mine, (own, other)
        self.shape = own.shape

    def read(self, flags, refs, part=Ellipsis):
        return jnp.where(flags[Flags.FIRST] == self.mine, refs[0][part], refs[1][part])


def settle_inputs(name, near, core, far_enc, far_dec, flags, weight_enc, weight_dec, after=()):
    tokens, width = near.shape
    features = weight_enc.shape[1]
    n_tp = lax.axis_size("tp")
    sub = tokens // n_tp

    def body(ins, outs):
        flag, near_ref, core_ref = ins[:3]
        tp = flag[Flags.TP]
        for layer, weight in enumerate((weight_enc, weight_dec)):
            far_ref, weights = ins[3 + layer], ins[5 + 2 * layer : 7 + 2 * layer]
            is_own = flag[Flags.FIRST] == 1 - layer
            pieces = []
            for i in range(n_tp):
                at = pl.ds(pl.multiple_of((tp ^ i) * sub, sub), sub)
                settled = jnp.where(is_own, near_ref[at, :], core_ref[at, :])
                pieces.append(jnp.where(flag[Flags.SETTLED] == 1, settled, far_ref[at, :]))
            values = jnp.concatenate(pieces, axis=0)
            outs[layer][...] = values
            for i in range(3):
                found = dot(values, weight.read(flag, weights, i), 1, 1).astype(BF16)
                if i == 0:
                    outs[2 + layer][...] = found
                else:
                    first = (2 * layer + i - 1) * features
                    outs[4][:, first : first + features] = found

    kinds = [shape((tokens, width), BF16)] * 2 + [shape((tokens, features), BF16)] * 2
    kinds.append(shape((tokens, 4 * features), BF16))
    return call(
        name, body, kinds, near, core, far_enc, far_dec, *weight_enc.pair, *weight_dec.pair,
        flags=flags, after=after,
    )


HALF_ROOT = 0.5**0.5
DENSITY = 1.0 / math.sqrt(2.0 * math.pi)


def feed_forward(name, pieces, weight_in, vectors, weight_out, flags, rider=None, after=()):
    count = len(pieces)
    tokens = sum(p.shape[0] for p in pieces)
    units, width = weight_out.shape
    step = 256
    riders = [] if rider is None else list(rider[1:])

    def body(ins, outs):
        flag, ins = ins[0], ins[1:]
        values = joined(ins[:count])
        win, vec, wout = ins[count : count + 2], ins[count + 2 : count + 4], ins[count + 4 : count + 6]
        bias = vectors.read(flag, vec)[BIAS_IN : BIAS_IN + 1]
        total = 0.0
        for at in range(0, units, step):
            part = slice(at, at + step)
            before = dot(values, weight_in.read(flag, win, (slice(None), part))) + bias[:, part]
            outs[0][:, part] = before
            active = (0.5 * before * (1.0 + lax.erf(before * HALF_ROOT))).astype(BF16)
            outs[1][:, part] = active
            total = total + dot(active, weight_out.read(flag, wout, part))
        rows = tokens // count
        outs[2][...] = total[:rows]
        for i in range(1, count):
            outs[2 + i][:rows] = total[i * rows : (i + 1) * rows].astype(BF16)
            if riders:
                outs[2 + i][rows:] = ins[count + 5 + i][...]

    kinds = [shape((tokens, units), F32), shape((tokens, units), BF16)]
    extra = riders[0].shape[0] if riders else 0
    kinds += piece_kinds(tokens, width, count, extra)
    flops = 4 * tokens * units * width
    out = call(
        name, body, kinds, *pieces, *weight_in.pair, *vectors.pair, *weight_out.pair, *riders,
        flags=flags, after=after, flops=flops,
    )
    return out[0], out[1], out[2:]


def feed_backward(name, pieces, part_rows, before, weight_in, weight_out, flags, after=()):
    count = len(pieces)
    tokens, units = before.shape
    width = weight_out.shape[1]
    step = 256

    def body(ins, outs):
        flag, ins = ins[0], ins[1:]
        values = joined(ins[:count], part_rows)
        before_ref, win, wout = ins[count], ins[count + 1 : count + 3], ins[count + 3 : count + 5]
        total = 0.0
        sums = []
        for at in range(0, units, step):
            part = slice(at, at + step)
            grad_active = dot(values, weight_out.read(flag, wout, part), 1, 1)
            u = before_ref[:, part]
            slope = 0.5 * (1.0 + lax.erf(u * HALF_ROOT)) + u * (DENSITY * jnp.exp(-0.5 * u * u))
            grad = (slope * grad_active).astype(BF16)
            outs[0][:, part] = grad
            sums.append(jnp.sum(grad.astype(F32), axis=0, keepdims=True))
            total = total + dot(grad, weight_in.read(flag, win, (slice(None), part)), 1, 1)
        put_rows(outs[1], [jnp.concatenate(sums, axis=1)])
        store_pieces(outs[2:], total)

    kinds = [shape((tokens, units), BF16), shape((8, units), F32)]
    kinds += piece_kinds(tokens, width, count)
    flops = 4 * tokens * units * width
    out = call(
        name, body, kinds, *pieces, before, *weight_in.pair, *weight_out.pair,
        flags=flags, after=after, flops=flops,
    )
    return out[0], out[1], out[2:]


KEY_ENC, KEY_DEC, PLACE = range(3)


class Marks:
    def __init__(self, marks, query_row, key_row, causal):
        self.marks, self.query_row, self.key_row, self.causal = marks, query_row, key_row, causal

    def allowed(self, ref, columns, piece, tokens, group, span):
        at = piece * tokens + group * span
        own = slice(group * span, (group + 1) * span)
        allowed = (
            columns[at : at + span, self.key_row : self.key_row + 1]
            == ref[self.query_row : self.query_row + 1, own]
        )
        if self.causal:
            places = columns[at : at + span, PLACE : PLACE + 1]
            allowed = allowed & (places <= ref[PLACE : PLACE + 1, own])
        return allowed


def head_block(flipped, head, heads):
    tokens = flipped.shape[1]
    parts = []
    if head:
        parts.append(jnp.zeros((HEAD_DIM * head, tokens), flipped.dtype))
    parts.append(flipped[HEAD_DIM * head : HEAD_DIM * (head + 1)])
    if head < heads - 1:
        parts.append(jnp.zeros((HEAD_DIM * (heads - 1 - head), tokens), flipped.dtype))
    return jnp.concatenate(parts, axis=0) if len(parts) > 1 else parts[0]


def attend(name, queries, pieces, marks, weight_out, flags, rows, tp, after=(), first=0):
    tokens, width = queries.shape
    span = tokens // rows
    heads = width // HEAD_DIM
    count = len(pieces)
    weights = list(weight_out.pair) if isinstance(weight_out, Layer) else [weight_out]

    def body(ins, outs):
        flag, query_ref, mark = ins[:3]
        wout = ins[3 : 3 + len(weights)]
        kv = ins[3 + len(weights) :]
        columns = mark[...].T
        mixed = []
        for group in range(rows):
            part = slice(group * span, (group + 1) * span)
            flipped = (query_ref[part, :] * BF16(SCALE)).T
            value_rows = [ref[part, first + width : first + 2 * width].T for ref in kv]
            masks = [marks.allowed(mark, columns, p, tokens, group, span) for p in range(count)]
            mixtures, logs = [], []
            for head in range(heads):
                block = head_block(flipped, head, heads)
                scores = [
                    jnp.where(
                        masks[p], dot(kv[p][part, first : first + width], block), MASKED_OUT
                    )
                    for p in range(count)
                ]
                largest = scores[0]
                for s in scores[1:]:
                    largest = jnp.maximum(largest, s)
                largest = jnp.max(largest, axis=0, keepdims=True)
                total, mixture = 0.0, 0.0
                for p in range(count):
                    e = jnp.exp(scores[p] - largest)
                    total = total + jnp.sum(e, axis=0, keepdims=True)
                    own = value_rows[p][HEAD_DIM * head : HEAD_DIM * (head + 1)]
                    mixture = mixture + dot(own, e.astype(BF16))
                mixtures.append(mixture * (1.0 / total))
                logs.append(largest + jnp.log(total))
            logs.append(jnp.zeros((8 - heads, span), F32))
            outs[1][group] = jnp.concatenate(logs, axis=0)
            mixed.append(jnp.concatenate(mixtures, axis=0).T.astype(BF16))
        result = jnp.concatenate(mixed, axis=0) if rows > 1 else mixed[0]
        outs[0][...] = result
        if len(weights) > 1:
            store_pieces(outs[2:], dot(result, weight_out.read(flag, wout)))
        else:
            store_pieces(outs[2:], dot(result, wout[0][...]))

    kinds = [shape((tokens, width), BF16), shape((rows, 8, span), F32)]
    kinds += piece_kinds(tokens, weight_out.shape[1], tp)
    flops = 4 * tokens * span * count * heads * 256
    out = call(
        name, body, kinds, queries, marks.marks, *weights, *pieces,
        flags=flags, after=after, flops=flops,
    )
    return out[0], out[1], out[2:]


def attend_back(
    name, upstream, part_rows, weight_out, queries, pieces, marks, logs, flags, rows, near, after=(),
    first_column=0,
):
    tokens, width = queries.shape
    span = tokens // rows
    heads = width // HEAD_DIM
    count = len(pieces)
    first = len(upstream)
    weights = list(weight_out.pair) if isinstance(weight_out, Layer) else [weight_out]

    def body(ins, outs):
        flag, ins = ins[0], ins[1:]
        all_grad = joined(ins[:first], part_rows)
        query_ref, log_ref, mark = ins[first : first + 3]
        wout = ins[first + 3 : first + 3 + len(weights)]
        wout = weight_out.read(flag, wout) if len(weights) > 1 else wout[0][...]
        kv = ins[first + 3 + len(weights) :]
        columns = mark[...].T
        grad_rows = dot(all_grad, wout, 1, 1).astype(BF16)
        for group in range(rows):
            part = slice(group * span, (group + 1) * span)
            grad = grad_rows[part]
            grad_flipped = dot(wout, all_grad[part], 1, 1).astype(BF16)
            scaled = query_ref[part, :] * BF16(SCALE)
            flipped = scaled.T
            keys_at = slice(first_column, first_column + width)
            values_at = slice(first_column + width, first_column + 2 * width)
            key_rows = [ref[part, keys_at].T for ref in kv]
            masks = [marks.allowed(mark, columns, p, tokens, group, span) for p in range(count)]
            lane = lax.broadcasted_iota(jnp.int32, (span, width), 1)
            key_grads, value_grads, query_grads = [0.0] * count, [0.0] * count, []
            for head in range(heads):
                mine = (lane >= HEAD_DIM * head) & (lane < HEAD_DIM * (head + 1))
                block = head_block(flipped, head, heads)
                grad_block = head_block(grad_flipped, head, heads)
                query_part = jnp.where(mine, scaled, BF16(0.0))
                grad_part = jnp.where(mine, grad, BF16(0.0))
                log_row = log_ref[group, head : head + 1, :]
                shares, share_grads, inner = [], [], 0.0
                for p in range(count):
                    s = jnp.where(masks[p], dot(kv[p][part, keys_at], block), MASKED_OUT)
                    w = jnp.exp(s - log_row)
                    g = dot(kv[p][part, values_at], grad_block)
                    inner = inner + jnp.sum(w * g, axis=0, keepdims=True)
                    value_grads[p] = value_grads[p] + dot(w.astype(BF16), grad_part)
                    shares.append(w)
                    share_grads.append(g)
                query_grad = 0.0
                for p in range(count):
                    score_grad = (shares[p] * (share_grads[p] - inner)).astype(BF16)
                    key_grads[p] = key_grads[p] + dot(score_grad, query_part)
                    own = key_rows[p][HEAD_DIM * head : HEAD_DIM * (head + 1)]
                    query_grad = query_grad + dot(own, score_grad)
                query_grads.append(query_grad)
            outs[0][part, :] = (jnp.concatenate(query_grads, axis=0) * SCALE).T.astype(BF16)
            for p in range(count):
                out, at = (outs[1], p) if p < near else (outs[2], p - near)
                at = slice(at * tokens + group * span, at * tokens + (group + 1) * span)
                out[at, :width] = key_grads[p].astype(out.dtype)
                out[at, width:] = value_grads[p].astype(out.dtype)

    kinds = [
        shape((tokens, width), BF16),
        shape((near * tokens, 2 * width), F32),
        shape(((count - near) * tokens, 2 * width), BF16),
    ]
    flops = 10 * tokens * span * count * heads * 256
    args = (*upstream, queries, logs, marks.marks, *weights, *pieces)
    return call(name, body, kinds, *args, flags=flags, after=after, flops=flops)


def settle_cores(name, mine, theirs, near, after=()):
    tokens = mine.shape[0] // near

    def body(ins, outs):
        total = ins[0][...] + ins[1][...].astype(F32)
        for i, out in enumerate(outs):
            out[...] = total[i * tokens : (i + 1) * tokens].astype(out.dtype)

    dims = (tokens, mine.shape[1])
    return call(
        name, body, [shape(dims, F32)] + [shape(dims, BF16)] * (near - 1), mine, theirs, after=after
    )


def project_back(
    name, flags, weight, pieces, queries=None, own_kv=None, received=(), rider=None, after=()
):
    features, width = weight.shape[1:]
    tokens = (queries if own_kv is None else own_kv).shape[0]
    weights = list(weight.pair) if isinstance(weight, Layer) else [weight]
    args = ([] if queries is None else [queries]) + ([] if own_kv is None else [own_kv, *received])
    riders = [] if rider is None else list(rider[1:])

    def body(ins, outs):
        flag, ins = ins[0], list(ins[1:])

        def chosen(i):
            if len(weights) > 1:
                return weight.read(flag, ins[len(args) : len(args) + 2], i)
            return ins[len(args)][i]

        outs = list(outs)
        total = 0.0
        at = 0
        if queries is not None:
            total = dot(ins[0][...], chosen(0))
            at = 1
        if own_kv is not None:
            kv = summed(ins[at][...], ins[at + 1 : at + 1 + len(received)]).astype(BF16)
            outs.pop(0)[...] = kv
            total = total + dot(kv[:, :features], chosen(1)) + dot(kv[:, features:], chosen(2))
        rows = tokens // pieces
        outs[0][...] = total[:rows]
        for i in range(1, pieces):
            outs[i][:rows] = total[i * rows : (i + 1) * rows].astype(BF16)
            if riders:
                outs[i][rows:] = ins[len(args) + len(weights) + i - 1][...]

    extra = riders[0].shape[0] if riders else 0
    kinds = [] if own_kv is None else [shape(own_kv.shape, BF16)]
    kinds += piece_kinds(tokens, width, pieces, extra)
    out = call(name, body, kinds, *args, *weights, *riders, flags=flags, after=after)
    return out if own_kv is None else (out[0], out[1:])


def turned_products(name, flags, halves, order, per, place, after=(), beside=None):
    columns = sum(r[2] for _, r in halves[0])
    count = len(order)
    arrays, index = [], {}
    for half in halves:
        for (lefts, _), (right, _, _) in half:
            for a in (*lefts, right):
                if id(a) not in index:
                    index[id(a)] = len(arrays)
                    arrays.append(a)
    if beside is not None:
        arrays.append(beside)
    tokens = halves[0][0][1][0].shape[0]
    width = arrays[index[id(halves[0][0][0][0][0])]].shape[1]
    align = 16 if per % 16 == 0 else 8
    kept = BF16 if align == 16 else F32
    n_pairs = len(halves[0])

    def kernel(*refs):
        flag = refs[0]
        ins = refs[1 : 1 + len(arrays)]
        outs = refs[1 + len(arrays) + len(after) :][:2]
        scratch = refs[1 + len(arrays) + len(after) + 2 :]
        first = flag[Flags.FIRST] == 1

        def left_value(half, i):
            lefts, rows = halves[half][i][0]
            return joined([ins[index[id(a)]] for a in lefts], rows)

        def right_value(half, i):
            right, at, size = halves[half][i][1]
            return ins[index[id(right)]][:, at : at + size]

        def same(i):
            a, b = halves[0][i][0], halves[1][i][0]
            return [id(x) for x in a[0]] == [id(x) for x in b[0]] and a[1] == b[1]

        for out_at, out in enumerate(outs):
            at = 0
            for i in range(n_pairs):
                turned = scratch[out_at * n_pairs + i]
                one, two = (0, 1) if out_at == 0 else (1, 0)
                if same(i):
                    left = left_value(0, i)
                else:
                    left = jnp.where(first, left_value(one, i), left_value(two, i))
                right = jnp.where(first, right_value(one, i), right_value(two, i))
                turned[...] = left.astype(kept).T
                size = right.shape[1]
                for k in range(count):
                    start = pl.multiple_of(place(flag, order[k]) * per, align)
                    got = dot(turned[pl.ds(start, per), :].astype(BF16), right)
                    out[k * per : (k + 1) * per, at : at + size] = got.astype(BF16)
                at += size
            for k in range(count if beside is not None else 0):
                start = pl.multiple_of(place(flag, order[k]) * per, align)
                chosen = ins[-1][pl.ds(start, per), :]
                out[k * per : (k + 1) * per, columns:] = chosen

    kind = shape((count * per, columns + (0 if beside is None else beside.shape[1])), BF16)
    moved = sum(math.prod(a.shape) * 2 for a in arrays) + 4 * count * per * columns
    return pl.pallas_call(
        kernel,
        out_shape=[kind, kind],
        in_specs=[pl.BlockSpec(memory_space=pltpu.SMEM)]
        + [pl.BlockSpec(memory_space=pltpu.VMEM)] * len(arrays)
        + [pl.BlockSpec(memory_space=pl.ANY)] * len(after),
        out_specs=[pl.BlockSpec(memory_space=pltpu.VMEM)] * 2,
        scratch_shapes=[pltpu.VMEM((width, tokens), kept)] * (2 * n_pairs),
        compiler_params=pltpu.CompilerParams(vmem_limit_bytes=20 * MIB),
        cost_estimate=pl.CostEstimate(
            flops=4 * tokens * count * per * columns, bytes_accessed=moved, transcendentals=0
        ),
        name=name,
    )(flags, *arrays, *after)


def halved(name, kept, received, last=False, after=(), cuts=None):
    rows, columns = kept.shape
    received = list(received) if isinstance(received, (list, tuple)) else [received]
    cuts = cuts or [columns]
    firsts = [sum(cuts[:i]) for i in range(len(cuts))]

    def body(ins, outs):
        there = [ref[...].astype(F32) for ref in ins[1:]]
        there = jnp.concatenate(there, axis=1) if len(there) > 1 else there[0]
        total = ins[0][...].astype(F32) + there
        if last:
            outs[0][...] = total
        else:
            outs[0][...] = total[: rows // 2].astype(BF16)
            for out, at, size in zip(outs[1:], firsts, cuts):
                out[...] = total[rows // 2 :, at : at + size].astype(BF16)

    if last:
        kinds = [shape((rows, columns), F32)]
    else:
        kinds = [shape((rows // 2, size), BF16) for size in [columns, *cuts]]
    return call(name, body, kinds, kept, *received, after=after)


def one_sided(name, flags, pairs, order, per, place, after=(), sides=1, beside=None):
    arrays, index = [], {}
    for (lefts, _), (right, _, _) in pairs:
        for a in (*lefts, right):
            if id(a) not in index:
                index[id(a)] = len(arrays)
                arrays.append(a)
    if beside is not None:
        arrays.append(beside)
    tokens = pairs[0][1][0].shape[0]
    width = pairs[0][0][0][0].shape[1]
    columns = sum(r[2] for _, r in pairs)
    count = len(order)
    align = 16 if per % 16 == 0 else 8
    kept = BF16 if align == 16 else F32

    def kernel(*refs):
        flag = refs[0]
        ins = refs[1 : 1 + len(arrays)]
        outs = refs[1 + len(arrays) + len(after) :][:sides]
        scratch = refs[1 + len(arrays) + len(after) + sides :]
        at = 0
        for i, ((lefts, rows), (right, first, size)) in enumerate(pairs):
            turned = scratch[i]
            turned[...] = joined([ins[index[id(a)]] for a in lefts], rows).astype(kept).T
            value = ins[index[id(right)]][:, first : first + size]
            for side, out in enumerate(outs):
                for k in range(count):
                    where = place(flag, order[k]) if sides == 1 else place(flag, order[k], side)
                    start = pl.multiple_of(where * per, align)
                    got = dot(turned[pl.ds(start, per), :].astype(BF16), value)
                    out[k * per : (k + 1) * per, at : at + size] = got.astype(BF16)
            at += size
        for k in range(count if beside is not None else 0):
            start = pl.multiple_of(place(flag, order[k]) * per, align)
            outs[0][k * per : (k + 1) * per, columns:] = ins[-1][pl.ds(start, per), :]

    kind = shape((count * per, columns + (0 if beside is None else beside.shape[1])), BF16)
    moved = sum(math.prod(a.shape) * 2 for a in arrays) + 2 * sides * count * per * columns
    return pl.pallas_call(
        kernel,
        out_shape=[kind] * sides,
        in_specs=[pl.BlockSpec(memory_space=pltpu.SMEM)]
        + [pl.BlockSpec(memory_space=pltpu.VMEM)] * len(arrays)
        + [pl.BlockSpec(memory_space=pl.ANY)] * len(after),
        out_specs=[pl.BlockSpec(memory_space=pltpu.VMEM)] * sides,
        scratch_shapes=[pltpu.VMEM((width, tokens), kept)] * len(pairs),
        compiler_params=pltpu.CompilerParams(vmem_limit_bytes=16 * MIB),
        cost_estimate=pl.CostEstimate(
            flops=2 * sides * tokens * count * per * columns, bytes_accessed=moved, transcendentals=0
        ),
        name=name,
    )(flags, *arrays, *after)


def on_device(
    hidden,
    segments,
    self_qkv,
    self_out,
    ffn_in,
    ffn_in_bias,
    ffn_out,
    norm_gains,
    norm_shifts,
    cross_qkv,
    cross_out,
    cross_gain,
    cross_shift,
    cotangent,
):
    section, seq, tp = (lax.axis_index(a) for a in ("section", "seq", "tp"))
    n_seq, n_tp = lax.axis_size("seq"), lax.axis_size("tp")
    half = n_seq // 2
    low_half = seq < half
    on_first = section == 0
    settled = on_first == low_half
    rows, span, width = hidden.shape[2:]
    tokens = rows * span
    sub = tokens // n_tp
    units = ffn_in.shape[2]
    features = cross_out.shape[0]
    flags = jnp.stack([on_first, low_half, settled, tp, seq]).astype(jnp.int32)

    both = ("section", "seq")
    low = range(half)
    to_encoder = [(z, z + half) for z in low] + [(z + half, n_seq + z) for z in low]
    to_decoder = [(n_seq + z, z + half) for z in low] + [(n_seq + z + half, n_seq + z) for z in low]
    across = [(z + half, n_seq + z + half) for z in low] + [(n_seq + z, z) for z in low]

    both_micro = hidden[0].reshape(2, tokens, width)
    far = jnp.where(low_half, both_micro[1], both_micro[0])
    near = jnp.where(low_half, both_micro[0], both_micro[1])
    far_enc = lax.ppermute(far, both, to_encoder)
    core = lax.ppermute(near, both, across)

    def layers(own):
        other = swap_cores(own)
        return Layer(1, own, other), Layer(0, own, other)

    qkv_enc, qkv_dec = layers(jnp.swapaxes(self_qkv[0], 1, 2))
    cross_turned = jnp.swapaxes(cross_qkv, 1, 2)

    def pack(ins, outs):
        zeros = jnp.zeros((2, width), F32)
        outs[0][...] = jnp.concatenate([ins[0][...], ins[1][...], ins[2][...], zeros], axis=0)
        put_rows(outs[1], [ins[3][...], ins[4][...]])

    vectors, vec_cross = call(
        "pack", pack, [shape((8, width), F32)] * 2,
        norm_gains[0], norm_shifts[0], ffn_in_bias[0], cross_gain[None], cross_shift[None],
    )
    vec_enc, vec_dec = layers(vectors)
    out_enc, out_dec = layers(self_out[0])

    small, sums_kind = shape((sub, width), BF16), shape((8, width), F32)

    def cut(ins, outs):
        flag, cot = ins
        at = pl.ds(pl.multiple_of(flag[Flags.TP] * sub, sub), sub)
        low_here = flag[Flags.LOW] == 1
        outs[0][...] = jnp.where(low_here, cot[0, at, :], cot[1, at, :])
        outs[1][...] = jnp.where(low_here, cot[1, at, :], cot[0, at, :])

    cot_near, cot_far = call(
        "cut", cut, [small] * 2, cotangent.reshape(2, tokens, width), flags=flags
    )
    cot_moved = lax.ppermute(
        cot_far, both, [(z, z + half) for z in low] + [(n_seq + z + half, n_seq + z) for z in low]
    )

    n_chunks = 2 * half
    n_keys = n_chunks * tokens
    place = np.broadcast_to(np.arange(n_chunks * span, dtype=np.int32), (1, rows, n_chunks * span))
    base = jnp.concatenate([segments.reshape(4, rows, n_chunks * span), jnp.asarray(place)])
    base = base.reshape(5, rows, n_chunks, span).transpose(0, 2, 1, 3).reshape(5, n_keys)
    z_bits, tp_bits = half.bit_length() - 1, n_tp.bit_length() - 1

    def turn_marks(ins, outs):
        flag, ref = ins
        low_here = flag[Flags.LOW] == 1
        found = jnp.concatenate(
            [
                jnp.where(low_here, ref[0:1, :], ref[1:2, :]),
                jnp.where(low_here, ref[2:3, :], ref[3:4, :]),
                ref[4:5, :],
                jnp.zeros((5, n_keys), jnp.int32),
            ],
            axis=0,
        )
        lane = lax.broadcasted_iota(jnp.int32, found.shape, 1)
        turns = [(1 - flag[Flags.FIRST], half * tokens)]
        turns += [((flag[Flags.SEQ] >> b) & 1, tokens << b) for b in range(z_bits)]
        turns += [((flag[Flags.TP] >> b) & 1, sub << b) for b in range(tp_bits)]
        for turn, step in turns:
            up, down = pltpu.roll(found, step, 1), pltpu.roll(found, n_keys - step, 1)
            other = jnp.where((lane & step) != 0, up, down)
            found = jnp.where(turn == 1, other, found)
        outs[0][...] = found

    (marks,) = call("marks", turn_marks, [shape((8, n_keys), jnp.int32)], base, flags=flags)
    marks_enc = Marks(marks, KEY_ENC, KEY_ENC, False)
    marks_dec = Marks(marks, KEY_DEC, KEY_DEC, True)
    marks_cross = Marks(marks, KEY_DEC, KEY_ENC, False)

    def share(own):
        mine = [own] + [xor_perm(own, "seq", dz) for dz in range(1, half)]
        return mine + [swap_cores(block) for block in mine]

    def settle(name, near_kv, far_kv, after=()):
        own, *sent = settle_cores(name, near_kv, swap_cores(far_kv), half, after)
        return own, [xor_perm(block, "seq", dz + 1) for dz, block in enumerate(sent)]

    top, bottom = slice(0, sub), slice(sub, 2 * sub)

    far_dec = lax.ppermute(far, both, to_decoder)
    input_enc, input_dec, q_enc, q_dec, kv_both = settle_inputs(
        "qkv_both", near, core, far_enc, far_dec, flags, qkv_enc, qkv_dec,
        after=[marks, cot_moved, *out_enc.pair],
    )
    late_in, late_out, kv_both = lax.optimization_barrier((ffn_in[0], ffn_out[0], kv_both))
    all_both = share(kv_both)
    win_enc, win_dec = layers(late_in)
    wout_enc, wout_dec = layers(late_out)
    a_enc, log_enc, part = attend(
        "attend_enc", q_enc, all_both, marks_enc, out_enc, flags, rows, n_tp
    )
    got = scatter_tp(part[1:])
    a_dec, log_dec, part_dec = attend(
        "attend_dec", q_dec, all_both, marks_dec, out_dec, flags, rows, n_tp,
        first=2 * features, after=[a_enc],
    )

    def norm_first(ins, outs):
        flag, ins = ins[0], ins[1:]
        total = summed(ins[0][...], ins[1:n_tp]) + ins[n_tp][:sub].astype(F32)
        vec = vec_enc.read(flag, ins[n_tp + 1 : n_tp + 3])
        unit, _ = normalized(total)
        result = unit * vec[GAIN_ATT : GAIN_ATT + 1] + vec[SHIFT_ATT : SHIFT_ATT + 1]
        outs[0][...] = total
        outs[1][...] = result.astype(BF16)

    full = shape((sub, width), F32)
    small_sums = shape((sub + VECTOR_ROWS, width), BF16)
    double_sums = shape((2 * sub + VECTOR_ROWS, width), BF16)
    z1_enc, h1b_enc = call(
        "norm_att_enc", norm_first, [full, small], part[0], *got, input_enc, *vec_enc.pair,
        flags=flags, after=[a_dec],
    )
    h1_pieces_enc = gather_tp(h1b_enc)

    u_enc, g_enc, part = feed_forward(
        "ffn_enc", h1_pieces_enc, win_enc, vec_enc, wout_enc, flags, rider=part_dec
    )
    got = scatter_tp(part[1:])

    def norm_second(ins, outs):
        flag, ins = ins[0], ins[1:]
        own_enc, own_dec, z1, inputs = ins[:4]
        received = ins[4 : 3 + n_tp]
        vec = vec_enc.read(flag, ins[3 + n_tp : 5 + n_tp])
        unit, _ = normalized(z1[...])
        h1 = unit * vec[GAIN_ATT : GAIN_ATT + 1] + vec[SHIFT_ATT : SHIFT_ATT + 1]
        total = summed(own_enc[...], received, top) + h1 + vec[BIAS_OUT : BIAS_OUT + 1]
        unit, _ = normalized(total)
        memory = unit * vec[GAIN_END : GAIN_END + 1] + vec[SHIFT_END : SHIFT_END + 1]
        outs[0][...] = total
        outs[1][...] = memory.astype(BF16)
        outs[3][:sub] = memory.astype(BF16)
        vec = vec_dec.read(flag, ins[3 + n_tp : 5 + n_tp])
        total = summed(own_dec[...], received, bottom) + inputs[:sub].astype(F32)
        unit, _ = normalized(total)
        result = unit * vec[GAIN_ATT : GAIN_ATT + 1] + vec[SHIFT_ATT : SHIFT_ATT + 1]
        outs[2][...] = total
        outs[3][sub:] = result.astype(BF16)

    double = shape((2 * sub, width), BF16)
    z2_enc, memory, z1_dec, message = call(
        "norm_end_enc", norm_second, [full, small, full, double],
        part[0], part_dec[0], z1_enc, input_dec, *got, *vec_enc.pair, flags=flags,
    )
    mid_pieces = gather_tp(message)

    def cross_projections(ins, outs):
        refs, weight = ins[:n_tp], ins[n_tp]
        values = joined(refs, top)
        for i in (1, 2):
            outs[0][:, (i - 1) * features : i * features] = dot(values, weight[i], 1, 1).astype(BF16)
        outs[1][...] = dot(joined(refs, bottom), weight[0], 1, 1).astype(BF16)

    kv_cross, q_cross = call(
        "qkv_cross", cross_projections,
        [shape((tokens, 2 * features), BF16), shape((tokens, features), BF16)],
        *mid_pieces, cross_turned,
    )
    all_cross = share(kv_cross)
    a_cross, log_cross, part = attend(
        "attend_cross", q_cross, all_cross, marks_cross, cross_out, flags, rows, n_tp
    )
    got = scatter_tp(part[1:])

    def norm_crossed(ins, outs):
        flag, ins = ins[0], ins[1:]
        vec = vec_dec.read(flag, ins[n_tp + 2 : n_tp + 4])
        unit, _ = normalized(ins[n_tp][...])
        h1 = unit * vec[GAIN_ATT : GAIN_ATT + 1] + vec[SHIFT_ATT : SHIFT_ATT + 1]
        total = summed(ins[0][...], ins[1:n_tp]) + h1
        vec = ins[n_tp + 1]
        unit, _ = normalized(total)
        outs[0][...] = total
        outs[1][...] = (unit * vec[0:1] + vec[1:2]).astype(BF16)

    z_cross, h2b = call(
        "norm_cross", norm_crossed, [full, small], part[0], *got, z1_dec, vec_cross,
        *vec_dec.pair, flags=flags,
    )
    h2_pieces = gather_tp(h2b)
    u_dec, g_dec, part = feed_forward("ffn_dec", h2_pieces, win_dec, vec_dec, wout_dec, flags)
    got = scatter_tp(part[1:])

    def norm_turn(ins, outs):
        flag, ins = ins[0], ins[1:]
        crossed, cot_here, cot_there, cross_vec = ins[n_tp : n_tp + 4]
        vec = vec_dec.read(flag, ins[n_tp + 4 : n_tp + 6])
        unit, _ = normalized(crossed[...])
        h2 = unit * cross_vec[0:1] + cross_vec[1:2]
        total = summed(ins[0][...], ins[1:n_tp]) + h2 + vec[BIAS_OUT : BIAS_OUT + 1]
        unit, _ = normalized(total)
        gain = vec[GAIN_END : GAIN_END + 1]
        decoded = (unit * gain + vec[SHIFT_END : SHIFT_END + 1]).astype(BF16)
        upstream = jnp.where(flag[Flags.SETTLED] == 1, cot_here[...], cot_there[...]).astype(F32)
        grad, gain_grad, shift_grad = norm_back(total, gain, upstream)
        outs[0][...] = grad
        outs[1][:sub] = grad.astype(BF16)
        put_vectors(outs[1], sub, [gain_grad, shift_grad, jnp.sum(grad, axis=0, keepdims=True)])
        outs[2][...] = decoded

    dz2_dec, dz2b_dec, decoded = call(
        "norm_end_dec", norm_turn, [full, small_sums, small],
        part[0], *got, z_cross, cot_near, cot_moved, vec_cross, *vec_dec.pair, flags=flags,
    )

    bits = n_seq.bit_length() - 1
    order = sorted(range(n_seq), key=lambda r: int(format(r, f"0{bits}b")[::-1], 2))

    def seq_place(flag, r):
        return flag[Flags.SEQ] ^ r

    def grads_start(name, halves, the_order, per, place, after=(), beside=None):
        mine, theirs = turned_products(name, flags, halves, the_order, per, place, after, beside)
        return mine, swap_cores(theirs)

    def grads_step(name, state, step, after=(), cuts=None):
        kept, received = state
        if step == bits:
            (total,) = halved(f"{name}_sum", kept, received, last=True, after=after)
            return total
        kept, *sent = halved(f"{name}_add{step}", kept, received, after=after, cuts=cuts)
        return kept, [xor_perm(block, "seq", 1 << step) for block in sent]

    def grads_finish(name, state, step=0, after=()):
        while isinstance(state, tuple):
            state = grads_step(name, state, step, after)
            step += 1
        return state

    def self_grads(name, member, pairs, after=(), beside=None):
        (block,) = one_sided(name, flags, pairs, order, per, seq_place, after, beside=beside)
        keeper = 1 - member
        return block, lax.ppermute(block, "section", [(1 - keeper, keeper)])

    def self_step(name, member, state, step, after=()):
        kept, received = state
        if step == bits:
            (total,) = halved(f"{name}_sum", kept, received, last=True, after=after)
            return total
        kept, sent = halved(f"{name}_add{step}", kept, received, after=after)
        at = (1 - member) * n_seq
        route = [(at + z, at + (z ^ (1 << step))) for z in range(n_seq)]
        return kept, lax.ppermute(sent, both, route)

    def self_finish(name, member, state, step, after=()):
        while isinstance(state, tuple):
            state = self_step(name, member, state, step, after)
            step += 1
        return state

    per = width // n_seq
    anything = slice(None)

    r_pieces_dec = gather_tp(dz2b_dec)
    du_dec, sums_in_dec, part = feed_backward(
        "ffn_back_dec", r_pieces_dec, top, u_dec, win_dec, wout_dec, flags
    )
    ffn_dec_state = grads_start(
        "grad_ffn_dec",
        [
            [((h2_pieces, anything), (du_dec, 0, units))],
            [((r_pieces_dec, top), (g_dec, 0, units))],
        ],
        order, per, seq_place,
    )

    got = scatter_tp(part[1:])

    ffn_dec_state = grads_step("grad_ffn_dec", ffn_dec_state, 0)

    def norm_cross_back(ins, outs):
        upstream = summed(ins[0][...], ins[1:n_tp]) + ins[n_tp][...]
        grad, gain_grad, shift_grad = norm_back(ins[n_tp + 1][...], ins[n_tp + 2][0:1], upstream)
        outs[0][...] = grad
        outs[1][:sub] = grad.astype(BF16)
        put_vectors(outs[1], sub, [gain_grad, shift_grad])

    dzc, dzcb = call(
        "norm_back_cross", norm_cross_back, [full, small_sums],
        part[0], *got, dz2_dec, z_cross, vec_cross, after=[ffn_dec_state[0]],
    )
    dzc_pieces = gather_tp(dzcb)

    dq_cross, near_kv, far_kv = attend_back(
        "attend_back_cross", dzc_pieces, top, cross_out, q_cross, all_cross, marks_cross,
        log_cross, flags, rows, half,
    )
    ffn_dec_state = grads_step("grad_ffn_dec", ffn_dec_state, 1, after=[dq_cross])
    own_kv, received_kv = settle("settle_cross", near_kv, far_kv, after=[ffn_dec_state[0]])
    part_query = project_back("query_back", flags, cross_turned, n_tp, queries=dq_cross)
    dkv_cross, part = project_back(
        "memory_back", flags, cross_turned, n_tp, own_kv=own_kv, received=received_kv,
        rider=part_query,
    )
    got = scatter_tp(part[1:])
    per_cross = width // (2 * n_seq)

    def cross_place(flag, r, side):
        return ((1 - flag[Flags.FIRST]) ^ side) * n_seq + (flag[Flags.SEQ] ^ r)

    cross_pairs = [
        ((mid_pieces, bottom), (dq_cross, 0, features)),
        ((mid_pieces, top), (dkv_cross, 0, 2 * features)),
        ((dzc_pieces, top), (a_cross, 0, features)),
    ]
    mine, theirs = one_sided("grad_cross", flags, cross_pairs, order, per_cross, cross_place, sides=2)
    cross_state = mine, swap_cores(theirs)
    cross_state = grads_step("grad_cross", cross_state, 0, after=[dkv_cross])

    def norm_middle_back(ins, outs):
        flag, ins = ins[0], ins[1:]
        own_memory, own_query, residual, z2, z1 = ins[:5]
        received = ins[5 : 4 + n_tp]
        vec = vec_enc.read(flag, ins[4 + n_tp : 6 + n_tp])
        upstream = summed(own_memory[...], received, top).astype(BF16).astype(F32)
        grad, gain_grad, shift_grad = norm_back(z2[...], vec[GAIN_END : GAIN_END + 1], upstream)
        sums = [gain_grad, shift_grad, jnp.sum(grad, axis=0, keepdims=True)]
        outs[0][...] = grad
        outs[2][:sub] = grad.astype(BF16)
        vec = vec_dec.read(flag, ins[4 + n_tp : 6 + n_tp])
        upstream = summed(own_query[...], received, bottom) + residual[...]
        grad, gain_grad, shift_grad = norm_back(z1[...], vec[GAIN_ATT : GAIN_ATT + 1], upstream)
        outs[1][...] = grad
        outs[2][sub : 2 * sub] = grad.astype(BF16)
        put_vectors(outs[2], 2 * sub, sums + [gain_grad, shift_grad])

    dz2_enc, dz1_dec, message = call(
        "norm_back_end_enc", norm_middle_back, [full, full, double_sums],
        part[0], part_query[0], dzc, z2_enc, z1_dec, *got, *vec_enc.pair, flags=flags,
        after=[cross_state[0]],
    )
    back_pieces = gather_tp(message)

    cross_state = grads_step("grad_cross", cross_state, 1, after=[dz2_enc])
    ffn_dec = grads_finish("grad_ffn_dec", ffn_dec_state, 2, after=[dz2_enc])
    du_enc, sums_in_enc, part = feed_backward(
        "ffn_back_enc", back_pieces, top, u_enc, win_enc, wout_enc, flags,
        after=[cross_state[0], ffn_dec],
    )
    got = scatter_tp(part[1:])
    dq_dec, near_kv, far_kv = attend_back(
        "attend_back_dec", back_pieces, bottom, out_dec, q_dec, all_both, marks_dec,
        log_dec, flags, rows, half, first_column=2 * features, after=[du_enc],
    )

    n_vec, n_columns = 14, 128

    def vector_columns(ins, outs):
        end_dec, cross, mid = (ins[i * n_tp : (i + 1) * n_tp] for i in range(3))
        in_enc, in_dec = ins[3 * n_tp : 3 * n_tp + 2]
        mid_rows = vector_sums(mid, 2 * sub, 5)
        zero = jnp.zeros((1, width), F32)
        dec_rows = vector_sums(end_dec, sub, 3)
        cross_rows = vector_sums(cross, sub, 2)
        found = [
            zero, mid_rows[0:1], zero, mid_rows[1:3], in_enc[0:1],
            mid_rows[3:4], dec_rows[0:1], mid_rows[4:5], dec_rows[1:3], in_dec[0:1],
            cross_rows, jnp.zeros((n_columns - n_vec, width), F32),
        ]
        columns = jnp.concatenate(found, axis=0).T
        moved = jnp.concatenate(
            [
                columns[(core * n_seq + z) * per_cross : (core * n_seq + z + 1) * per_cross]
                for z in range(n_seq)
                for core in range(2)
            ],
            axis=0,
        )
        lane = lax.broadcasted_iota(jnp.int32, columns.shape, 1)
        outs[0][...] = jnp.where(lane >= n_vec - 2, moved, columns).astype(BF16)

    (vectors_here,) = call(
        "vector_columns", vector_columns, [shape((width, n_columns), BF16)],
        *r_pieces_dec, *dzc_pieces, *back_pieces, sums_in_enc, sums_in_dec,
    )
    ffn_enc_state = grads_start(
        "grad_ffn_enc",
        [
            [((h1_pieces_enc, anything), (du_enc, 0, units))],
            [((back_pieces, top), (g_enc, 0, units))],
        ],
        order, per, seq_place, after=[dq_dec], beside=vectors_here,
    )

    dec_kv, dec_received = settle("settle_dec", near_kv, far_kv)
    ffn_enc_state = grads_step("grad_ffn_enc", ffn_enc_state, 0)

    def norm_first_back(ins, outs):
        flag, ins = ins[0], ins[1:]
        upstream = summed(ins[0][...], ins[1:n_tp]) + ins[n_tp][...]
        vec = vec_enc.read(flag, ins[n_tp + 2 : n_tp + 4])
        grad, gain_grad, shift_grad = norm_back(
            ins[n_tp + 1][...], vec[GAIN_ATT : GAIN_ATT + 1], upstream
        )
        outs[0][...] = grad
        outs[1][:sub] = grad.astype(BF16)
        put_vectors(outs[1], sub, [gain_grad, shift_grad])

    dz1_enc, dz1b_enc = call(
        "norm_back_att_enc", norm_first_back, [full, small_sums],
        part[0], *got, dz2_enc, z1_enc, *vec_enc.pair, flags=flags,
        after=[dec_kv, ffn_enc_state[0]],
    )
    dz1_pieces_enc = gather_tp(dz1b_enc)


    dkv_dec, part_dec = project_back(
        "input_back_dec", flags, qkv_dec, n_tp, queries=dq_dec, own_kv=dec_kv,
        received=dec_received, after=[dz1_enc],
    )
    cross_sum = grads_finish("grad_cross", cross_state, 2, after=[dkv_dec])
    dq_enc, near_kv, far_kv = attend_back(
        "attend_back_enc", dz1_pieces_enc, top, out_enc, q_enc, all_both, marks_enc,
        log_enc, flags, rows, half, after=[cross_sum],
    )
    own_kv, received_kv = settle("settle_enc", near_kv, far_kv)
    self_dec_state = self_grads(
        "grad_self_dec", 0,
        [
            (([input_dec], anything), (dq_dec, 0, features)),
            (([input_dec], anything), (dkv_dec, 0, 2 * features)),
            ((back_pieces, bottom), (a_dec, 0, features)),
        ],
        after=[own_kv],
    )
    ffn_enc_state = grads_step(
        "grad_ffn_enc", ffn_enc_state, 1, after=[self_dec_state[0]], cuts=[units // 2, units // 2 + n_columns]
    )
    dkv_enc, part = project_back(
        "input_back_enc", flags, qkv_enc, n_tp, queries=dq_enc, own_kv=own_kv,
        received=received_kv, rider=part_dec, after=[ffn_enc_state[0]],
    )
    got = scatter_tp(part[1:])
    def att_columns(ins, outs):
        found = [vector_sums(ins, sub, 2), jnp.zeros((n_columns - 2, width), F32)]
        outs[0][...] = jnp.concatenate(found, axis=0).T.astype(BF16)

    (vectors_att,) = call(
        "vector_columns_att", att_columns, [shape((width, n_columns), BF16)], *dz1_pieces_enc,
        after=[part[0]],
    )
    self_enc_state = self_grads(
        "grad_self_enc", 1,
        [
            (([input_enc], anything), (dq_enc, 0, features)),
            (([input_enc], anything), (dkv_enc, 0, 2 * features)),
            ((dz1_pieces_enc, top), (a_enc, 0, features)),
        ],
        after=[part[0]], beside=vectors_att,
    )
    self_dec_state = self_step("grad_self_dec", 0, self_dec_state, 0, after=[part[0]])


    def input_sums(ins, outs):
        flag, ins = ins[0], ins[1:]
        received = ins[4 : 3 + n_tp]
        enc = (summed(ins[0][...], received, top) + ins[2][...]).astype(BF16)
        dec = (summed(ins[1][...], received, bottom) + ins[3][...]).astype(BF16)
        enc = jnp.concatenate([ins[3 + n_tp][...], enc], axis=0)
        dec = jnp.concatenate([ins[4 + n_tp][...], dec], axis=0)
        outs[0][...] = enc
        outs[1][...] = dec
        outs[2][...] = jnp.where(flag[Flags.FIRST] == 1, dec, enc)

    done_enc, done_dec, done_across = call(
        "input_sums", input_sums, [double, double, double],
        part[0], part_dec[0], dz1_enc, dz1_dec, *got, memory, decoded, flags=flags,
        after=[self_enc_state[0], self_dec_state[0], ffn_enc_state[1][0]],
    )
    self_enc_state = self_step("grad_self_enc", 1, self_enc_state, 0, after=[done_enc])
    self_dec_state = self_step("grad_self_dec", 0, self_dec_state, 1, after=[self_enc_state[0]])

    ffn_enc = grads_finish("grad_ffn_enc", ffn_enc_state, 2, after=[self_enc_state[0]])
    def to_other(ins, outs):
        outs[0][...] = jnp.where(ins[0][Flags.FIRST] == 1, ins[1][...], ins[2][:, :units])

    (sent,) = call(
        "grad_swap", to_other, [shape((per, units), F32)], ffn_dec, ffn_enc, flags=flags
    )

    far_enc = lax.ppermute(done_enc, both, [(b, a) for a, b in to_encoder])
    far_dec = lax.ppermute(done_dec, both, [(b, a) for a, b in to_decoder])
    from_core = lax.ppermute(done_across, both, [(b, a) for a, b in across])

    def order_body(ins, outs):
        flag = ins[0]
        first = flag[Flags.FIRST] == 1
        stays = jnp.where(first, ins[1][...], ins[2][...])
        near = jnp.where(flag[Flags.SETTLED] == 1, stays, ins[3][...])
        far = jnp.where(first, ins[4][...], ins[5][...])
        low_here = flag[Flags.LOW] == 1
        outs[0][: 2 * sub] = jnp.where(low_here, near, far)
        outs[0][2 * sub :] = jnp.where(low_here, far, near)

    (found,) = call(
        "outputs_order", order_body, [shape((4 * sub, width), BF16)],
        done_enc, done_dec, from_core, far_enc, far_dec, flags=flags,
        after=[self_dec_state[0]],
    )
    self_enc_state = self_step("grad_self_enc", 1, self_enc_state, 1, after=[found])
    self_dec = self_finish("grad_self_dec", 0, self_dec_state, 2, after=[self_enc_state[0]])
    self_enc = self_finish("grad_self_enc", 1, self_enc_state, 2, after=[self_dec])
    pieces = gather_tp(found)
    swapped = swap_cores(sent)

    def finish(ins, outs):
        flag, dec_ffn, enc_ffn, other = ins
        first = flag[Flags.FIRST] == 1
        mine = jnp.where(first, enc_ffn[:, :units], dec_ffn[...])
        theirs = other[...]
        outs[0][...] = jnp.where(first, mine, theirs)
        outs[1][...] = jnp.where(first, theirs, mine)
        table = enc_ffn[:, units:].T
        vectors_here = jnp.where(first, table[0:6], table[6:12])
        outs[2][...] = jnp.concatenate([vectors_here, jnp.zeros((2, per), F32)], axis=0)
        outs[3][...] = vectors_here[5:6]
        crossed = table[n_vec - 2 : n_vec]
        crossed = jnp.where(first, crossed[:, :per_cross], crossed[:, per_cross:])
        outs[4][...] = crossed[0:1]
        outs[5][...] = crossed[1:2]

    grad_in, grad_out, layer_vectors, grad_bias, grad_cross_gain, grad_cross_shift = call(
        "finish_ffn", finish,
        [shape((per, units), F32)] * 2
        + [shape((8, per), F32), shape((1, per), F32)]
        + [shape((1, per_cross), F32)] * 2,
        ffn_dec, ffn_enc, swapped, flags=flags,
    )


    def place_body(ins, outs):
        here = ins[0][Flags.TP]
        for i, ref in enumerate(ins[1:]):
            at = pl.ds(pl.multiple_of((here ^ i) * sub, sub), sub)
            for micro in range(2):
                first_row = 2 * micro * sub
                outs[0][micro, at, :] = ref[first_row : first_row + sub]
                outs[1][micro, at, :] = ref[first_row + sub : first_row + 2 * sub]

    layer_out, grad_hidden = call(
        "outputs_place", place_body, [shape((2, tokens, width), BF16)] * 2, *pieces, flags=flags,
        after=[self_enc, grad_in],
    )

    def finish_cross(ins, outs):
        whole = ins[0][...]
        for i in range(3):
            outs[0][i] = whole[:, i * features : (i + 1) * features]
        outs[1][...] = whole[:, 3 * features :].T

    grad_cross_qkv, grad_cross_out = call(
        "finish_cross", finish_cross,
        [shape((3, per_cross, features), F32), shape((features, per_cross), F32)], cross_sum,
    )

    def finish_self(ins, outs):
        first = ins[0][Flags.FIRST] == 1
        whole = jnp.where(first, ins[1][:, : 4 * features], ins[2][...])
        own = ins[3][...]
        att = ins[1][:, 4 * features :].T
        outs[2][0:1] = own[0:1] + jnp.where(first, att[0:1], 0.0)
        outs[2][1:2] = own[1:2]
        outs[3][0:1] = own[2:3] + jnp.where(first, att[1:2], 0.0)
        outs[3][1:3] = own[3:5]
        for i in range(3):
            outs[0][i] = whole[:, i * features : (i + 1) * features]
        outs[1][...] = whole[:, 3 * features :].T

    grad_qkv, grad_self_out, grad_gains, grad_shifts = call(
        "finish_self", finish_self,
        [
            shape((3, per, features), F32), shape((features, per), F32),
            shape((2, per), F32), shape((3, per), F32),
        ],
        self_enc, self_dec, layer_vectors, flags=flags,
    )

    return (
        layer_out.reshape(1, 2, rows, span, width),
        grad_hidden.reshape(1, 2, rows, span, width),
        grad_qkv[None],
        grad_self_out[None],
        grad_in[None],
        grad_bias[None],
        grad_out.T[None],
        grad_gains[None],
        grad_shifts[None],
        grad_cross_qkv,
        grad_cross_out,
        grad_cross_gain[0],
        grad_cross_shift[0],
    )


def solution(mesh):
    return jax.shard_map(
        on_device,
        mesh=mesh,
        in_specs=(
            P("section", None, None, "seq", None),
            P(),
            P("section", None, None, "tp"),
            P("section", "tp", None),
            P("section", None, "tp"),
            P("section", "tp", None),
            P("section", "tp", None),
            P("section", None, None),
            P("section", None, None),
            P(None, None, "tp"),
            P("tp", None),
            P(),
            P(),
            P(None, None, "seq", None),
        ),
        out_specs=(
            P("section", None, None, "seq", None),
            P("section", None, None, "seq", None),
            P("section", None, "seq", "tp"),
            P("section", "tp", "seq"),
            P("section", "seq", "tp"),
            P("section", "tp", "seq"),
            P("section", "tp", "seq"),
            P("section", None, "seq"),
            P("section", None, "seq"),
            P(None, ("section", "seq"), "tp"),
            P("tp", ("section", "seq")),
            P(("section", "seq")),
            P(("section", "seq")),
        ),
        check_vma=False,
    )
```

```python
import math

import jax
import jax.numpy as jnp
import numpy as np
from jax import lax
from jax.experimental import pallas as pl
from jax.experimental.pallas import tpu as pltpu
from jax.sharding import PartitionSpec as P

HEAD_DIM = 64
EPSILON = 1e-05
MASKED_OUT = -1e30
SCALE = 1.0 / math.sqrt(HEAD_DIM)
F32 = jnp.float32
BF16 = jnp.bfloat16
MIB = 1 << 20

GAIN_ATT, GAIN_END, SHIFT_ATT, SHIFT_END, BIAS_OUT, BIAS_IN = range(6)


def shape(dims, kind):
    return jax.ShapeDtypeStruct(dims, kind)


def dot(left, right, left_dim=1, right_dim=0):
    return lax.dot_general(
        left, right, (((left_dim,), (right_dim,)), ((), ())), preferred_element_type=F32
    )


class Flags:
    FIRST, LOW, SETTLED, TP, SEQ = range(5)


def call(name, body, outs, *args, flags=None, after=(), flops=0, vmem=16 * MIB):
    scalars = [] if flags is None else [flags]
    after = list(after)
    count = len(scalars) + len(args)

    def kernel(*refs):
        body(refs[:count], refs[count + len(after) :])

    moved = sum(math.prod(a.shape) * a.dtype.itemsize for a in (*args, *outs))
    in_specs = [pl.BlockSpec(memory_space=pltpu.SMEM)] * len(scalars)
    in_specs += [pl.BlockSpec(memory_space=pltpu.VMEM)] * len(args)
    in_specs += [pl.BlockSpec(memory_space=pl.ANY)] * len(after)
    return pl.pallas_call(
        kernel,
        out_shape=outs,
        in_specs=in_specs,
        out_specs=[pl.BlockSpec(memory_space=pltpu.VMEM)] * len(outs),
        compiler_params=pltpu.CompilerParams(vmem_limit_bytes=vmem),
        cost_estimate=pl.CostEstimate(flops=flops, bytes_accessed=moved, transcendentals=0),
        name=name,
    )(*scalars, *args, *after)


def swap_cores(block):
    return lax.ppermute(block, "section", [(0, 1), (1, 0)])


def xor_perm(block, axis, bits):
    return lax.ppermute(block, axis, [(i, i ^ bits) for i in range(lax.axis_size(axis))])


def scatter_tp(pieces):
    order = sorted(range(1, len(pieces) + 1), key=lambda i: -bin(i).count("1"))
    got = {i: xor_perm(pieces[i - 1], "tp", i) for i in order}
    return [got[i] for i in range(1, len(pieces) + 1)]


def gather_tp(block):
    return [block] + scatter_tp([block] * (lax.axis_size("tp") - 1))


def normalized(values):
    centred = values - jnp.mean(values, axis=-1, keepdims=True)
    spread = jnp.mean(centred * centred, axis=-1, keepdims=True)
    inverse = lax.rsqrt(spread + EPSILON)
    return centred * inverse, inverse


def norm_back(values, gain, upstream):
    unit, inverse = normalized(values)
    scaled = gain * upstream
    grad = (
        scaled
        - jnp.mean(scaled, axis=-1, keepdims=True)
        - unit * jnp.mean(scaled * unit, axis=-1, keepdims=True)
    ) * inverse
    gain_grad = jnp.sum(upstream * unit, axis=0, keepdims=True)
    shift_grad = jnp.sum(upstream, axis=0, keepdims=True)
    return grad, gain_grad, shift_grad


def put_rows(ref, rows):
    width = ref.shape[1]
    ref[...] = jnp.concatenate(rows + [jnp.zeros((8 - len(rows), width), F32)], axis=0)


VECTOR_ROWS = 16


def put_vectors(ref, at, rows):
    half = VECTOR_ROWS // 2
    whole = jnp.concatenate(rows + [jnp.zeros((half - len(rows), ref.shape[1]), F32)], axis=0)
    top = whole.astype(BF16)
    left = (whole - top.astype(F32)).astype(BF16)
    ref[at : at + VECTOR_ROWS] = jnp.concatenate([top, left], axis=0)


def vector_sums(refs, at, count):
    half = VECTOR_ROWS // 2
    total = 0.0
    for ref in refs:
        rows = ref[at : at + VECTOR_ROWS].astype(F32)
        total = total + (rows[:half] + rows[half:])
    return total[:count]


def summed(own, received, part=slice(None)):
    total = own
    for ref in received:
        total = total + ref[part].astype(F32)
    return total


def joined(refs, part=slice(None)):
    return jnp.concatenate([ref[part] for ref in refs], axis=0)


def store_pieces(refs, value):
    rows = refs[0].shape[0]
    for i, ref in enumerate(refs):
        ref[...] = value[i * rows : (i + 1) * rows].astype(ref.dtype)


def piece_kinds(tokens, width, count, extra=0):
    rows = tokens // count
    return [shape((rows, width), F32)] + [shape((rows + extra, width), BF16)] * (count - 1)


class Layer:
    def __init__(self, mine, own, other):
        self.mine, self.pair = mine, (own, other)
        self.shape = own.shape

    def read(self, flags, refs, part=Ellipsis):
        return jnp.where(flags[Flags.FIRST] == self.mine, refs[0][part], refs[1][part])


def settle_inputs(name, near, core, far_enc, far_dec, flags, weight_enc, weight_dec, after=()):
    tokens, width = near.shape
    features = weight_enc.shape[1]
    n_tp = lax.axis_size("tp")
    sub = tokens // n_tp

    def body(ins, outs):
        flag, near_ref, core_ref = ins[:3]
        tp = flag[Flags.TP]
        for layer, weight in enumerate((weight_enc, weight_dec)):
            far_ref, weights = ins[3 + layer], ins[5 + 2 * layer : 7 + 2 * layer]
            is_own = flag[Flags.FIRST] == 1 - layer
            pieces = []
            for i in range(n_tp):
                at = pl.ds(pl.multiple_of((tp ^ i) * sub, sub), sub)
                settled = jnp.where(is_own, near_ref[at, :], core_ref[at, :])
                pieces.append(jnp.where(flag[Flags.SETTLED] == 1, settled, far_ref[at, :]))
            values = jnp.concatenate(pieces, axis=0)
            outs[layer][...] = values
            for i in range(3):
                found = dot(values, weight.read(flag, weights, i), 1, 1).astype(BF16)
                if i == 0:
                    outs[2 + layer][...] = found
                else:
                    first = (i - 1) * features
                    outs[4 + layer][:, first : first + features] = found

    kinds = [shape((tokens, width), BF16)] * 2 + [shape((tokens, features), BF16)] * 2
    kinds += [shape((tokens, 2 * features), BF16)] * 2
    return call(
        name, body, kinds, near, core, far_enc, far_dec, *weight_enc.pair, *weight_dec.pair,
        flags=flags, after=after,
    )


HALF_ROOT = 0.5**0.5
DENSITY = 1.0 / math.sqrt(2.0 * math.pi)


def feed_forward(name, pieces, weight_in, vectors, weight_out, flags, rider=None, after=()):
    count = len(pieces)
    tokens = sum(p.shape[0] for p in pieces)
    units, width = weight_out.shape
    step = 256
    riders = [] if rider is None else list(rider[1:])

    def body(ins, outs):
        flag, ins = ins[0], ins[1:]
        values = joined(ins[:count])
        win, vec, wout = ins[count : count + 2], ins[count + 2 : count + 4], ins[count + 4 : count + 6]
        bias = vectors.read(flag, vec)[BIAS_IN : BIAS_IN + 1]
        total = 0.0
        for at in range(0, units, step):
            part = slice(at, at + step)
            before = dot(values, weight_in.read(flag, win, (slice(None), part))) + bias[:, part]
            outs[0][:, part] = before
            active = (0.5 * before * (1.0 + lax.erf(before * HALF_ROOT))).astype(BF16)
            outs[1][:, part] = active
            total = total + dot(active, weight_out.read(flag, wout, part))
        rows = tokens // count
        outs[2][...] = total[:rows]
        for i in range(1, count):
            outs[2 + i][:rows] = total[i * rows : (i + 1) * rows].astype(BF16)
            if riders:
                outs[2 + i][rows:] = ins[count + 5 + i][...]

    kinds = [shape((tokens, units), F32), shape((tokens, units), BF16)]
    extra = riders[0].shape[0] if riders else 0
    kinds += piece_kinds(tokens, width, count, extra)
    flops = 4 * tokens * units * width
    out = call(
        name, body, kinds, *pieces, *weight_in.pair, *vectors.pair, *weight_out.pair, *riders,
        flags=flags, after=after, flops=flops,
    )
    return out[0], out[1], out[2:]


def feed_backward(name, pieces, part_rows, before, weight_in, weight_out, flags, after=()):
    count = len(pieces)
    tokens, units = before.shape
    width = weight_out.shape[1]
    step = 256

    def body(ins, outs):
        flag, ins = ins[0], ins[1:]
        values = joined(ins[:count], part_rows)
        before_ref, win, wout = ins[count], ins[count + 1 : count + 3], ins[count + 3 : count + 5]
        total = 0.0
        sums = []
        for at in range(0, units, step):
            part = slice(at, at + step)
            grad_active = dot(values, weight_out.read(flag, wout, part), 1, 1)
            u = before_ref[:, part]
            slope = 0.5 * (1.0 + lax.erf(u * HALF_ROOT)) + u * (DENSITY * jnp.exp(-0.5 * u * u))
            grad = (slope * grad_active).astype(BF16)
            outs[0][:, part] = grad
            sums.append(jnp.sum(grad.astype(F32), axis=0, keepdims=True))
            total = total + dot(grad, weight_in.read(flag, win, (slice(None), part)), 1, 1)
        put_rows(outs[1], [jnp.concatenate(sums, axis=1)])
        store_pieces(outs[2:], total)

    kinds = [shape((tokens, units), BF16), shape((8, units), F32)]
    kinds += piece_kinds(tokens, width, count)
    flops = 4 * tokens * units * width
    out = call(
        name, body, kinds, *pieces, before, *weight_in.pair, *weight_out.pair,
        flags=flags, after=after, flops=flops,
    )
    return out[0], out[1], out[2:]


KEY_ENC, KEY_DEC, PLACE = range(3)


class Marks:
    def __init__(self, marks, query_row, key_row, causal):
        self.marks, self.query_row, self.key_row, self.causal = marks, query_row, key_row, causal

    def allowed(self, ref, columns, piece, tokens, group, span):
        at = piece * tokens + group * span
        own = slice(group * span, (group + 1) * span)
        allowed = (
            columns[at : at + span, self.key_row : self.key_row + 1]
            == ref[self.query_row : self.query_row + 1, own]
        )
        if self.causal:
            places = columns[at : at + span, PLACE : PLACE + 1]
            allowed = allowed & (places <= ref[PLACE : PLACE + 1, own])
        return allowed


def head_block(flipped, head, heads):
    tokens = flipped.shape[1]
    parts = []
    if head:
        parts.append(jnp.zeros((HEAD_DIM * head, tokens), flipped.dtype))
    parts.append(flipped[HEAD_DIM * head : HEAD_DIM * (head + 1)])
    if head < heads - 1:
        parts.append(jnp.zeros((HEAD_DIM * (heads - 1 - head), tokens), flipped.dtype))
    return jnp.concatenate(parts, axis=0) if len(parts) > 1 else parts[0]


def attend(name, queries, pieces, marks, weight_out, flags, rows, tp, after=(), first=0):
    tokens, width = queries.shape
    span = tokens // rows
    heads = width // HEAD_DIM
    count = len(pieces)
    weights = list(weight_out.pair) if isinstance(weight_out, Layer) else [weight_out]

    def body(ins, outs):
        flag, query_ref, mark = ins[:3]
        wout = ins[3 : 3 + len(weights)]
        kv = ins[3 + len(weights) :]
        columns = mark[...].T
        mixed = []
        for group in range(rows):
            part = slice(group * span, (group + 1) * span)
            flipped = (query_ref[part, :] * BF16(SCALE)).T
            value_rows = [ref[part, first + width : first + 2 * width].T for ref in kv]
            masks = [marks.allowed(mark, columns, p, tokens, group, span) for p in range(count)]
            mixtures, logs = [], []
            for head in range(heads):
                block = head_block(flipped, head, heads)
                scores = [
                    jnp.where(
                        masks[p], dot(kv[p][part, first : first + width], block), MASKED_OUT
                    )
                    for p in range(count)
                ]
                largest = scores[0]
                for s in scores[1:]:
                    largest = jnp.maximum(largest, s)
                largest = jnp.max(largest, axis=0, keepdims=True)
                total, mixture = 0.0, 0.0
                for p in range(count):
                    e = jnp.exp(scores[p] - largest)
                    total = total + jnp.sum(e, axis=0, keepdims=True)
                    own = value_rows[p][HEAD_DIM * head : HEAD_DIM * (head + 1)]
                    mixture = mixture + dot(own, e.astype(BF16))
                mixtures.append(mixture * (1.0 / total))
                logs.append(largest + jnp.log(total))
            logs.append(jnp.zeros((8 - heads, span), F32))
            outs[1][group] = jnp.concatenate(logs, axis=0)
            mixed.append(jnp.concatenate(mixtures, axis=0).T.astype(BF16))
        result = jnp.concatenate(mixed, axis=0) if rows > 1 else mixed[0]
        outs[0][...] = result
        if len(weights) > 1:
            store_pieces(outs[2:], dot(result, weight_out.read(flag, wout)))
        else:
            store_pieces(outs[2:], dot(result, wout[0][...]))

    kinds = [shape((tokens, width), BF16), shape((rows, 8, span), F32)]
    kinds += piece_kinds(tokens, weight_out.shape[1], tp)
    flops = 4 * tokens * span * count * heads * 256
    out = call(
        name, body, kinds, queries, marks.marks, *weights, *pieces,
        flags=flags, after=after, flops=flops,
    )
    return out[0], out[1], out[2:]


def attend_back(
    name, upstream, part_rows, weight_out, queries, pieces, marks, logs, flags, rows, near, after=(),
    first_column=0,
):
    tokens, width = queries.shape
    span = tokens // rows
    heads = width // HEAD_DIM
    count = len(pieces)
    first = len(upstream)
    weights = list(weight_out.pair) if isinstance(weight_out, Layer) else [weight_out]

    def body(ins, outs):
        flag, ins = ins[0], ins[1:]
        all_grad = joined(ins[:first], part_rows)
        query_ref, log_ref, mark = ins[first : first + 3]
        wout = ins[first + 3 : first + 3 + len(weights)]
        wout = weight_out.read(flag, wout) if len(weights) > 1 else wout[0][...]
        kv = ins[first + 3 + len(weights) :]
        columns = mark[...].T
        grad_rows = dot(all_grad, wout, 1, 1).astype(BF16)
        for group in range(rows):
            part = slice(group * span, (group + 1) * span)
            grad = grad_rows[part]
            grad_flipped = dot(wout, all_grad[part], 1, 1).astype(BF16)
            scaled = query_ref[part, :] * BF16(SCALE)
            flipped = scaled.T
            keys_at = slice(first_column, first_column + width)
            values_at = slice(first_column + width, first_column + 2 * width)
            key_rows = [ref[part, keys_at].T for ref in kv]
            masks = [marks.allowed(mark, columns, p, tokens, group, span) for p in range(count)]
            lane = lax.broadcasted_iota(jnp.int32, (span, width), 1)
            key_grads, value_grads, query_grads = [0.0] * count, [0.0] * count, []
            for head in range(heads):
                mine = (lane >= HEAD_DIM * head) & (lane < HEAD_DIM * (head + 1))
                block = head_block(flipped, head, heads)
                grad_block = head_block(grad_flipped, head, heads)
                query_part = jnp.where(mine, scaled, BF16(0.0))
                grad_part = jnp.where(mine, grad, BF16(0.0))
                log_row = log_ref[group, head : head + 1, :]
                shares, share_grads, inner = [], [], 0.0
                for p in range(count):
                    s = jnp.where(masks[p], dot(kv[p][part, keys_at], block), MASKED_OUT)
                    w = jnp.exp(s - log_row)
                    g = dot(kv[p][part, values_at], grad_block)
                    inner = inner + jnp.sum(w * g, axis=0, keepdims=True)
                    value_grads[p] = value_grads[p] + dot(w.astype(BF16), grad_part)
                    shares.append(w)
                    share_grads.append(g)
                query_grad = 0.0
                for p in range(count):
                    score_grad = (shares[p] * (share_grads[p] - inner)).astype(BF16)
                    key_grads[p] = key_grads[p] + dot(score_grad, query_part)
                    own = key_rows[p][HEAD_DIM * head : HEAD_DIM * (head + 1)]
                    query_grad = query_grad + dot(own, score_grad)
                query_grads.append(query_grad)
            outs[0][part, :] = (jnp.concatenate(query_grads, axis=0) * SCALE).T.astype(BF16)
            for p in range(count):
                out, at = (outs[1], p) if p < near else (outs[2], p - near)
                at = slice(at * tokens + group * span, at * tokens + (group + 1) * span)
                out[at, :width] = key_grads[p].astype(out.dtype)
                out[at, width:] = value_grads[p].astype(out.dtype)

    kinds = [
        shape((tokens, width), BF16),
        shape((near * tokens, 2 * width), F32),
        shape(((count - near) * tokens, 2 * width), BF16),
    ]
    flops = 10 * tokens * span * count * heads * 256
    args = (*upstream, queries, logs, marks.marks, *weights, *pieces)
    return call(name, body, kinds, *args, flags=flags, after=after, flops=flops)


def settle_cores(name, mine, theirs, near, after=()):
    tokens = mine.shape[0] // near

    def body(ins, outs):
        total = ins[0][...] + ins[1][...].astype(F32)
        for i, out in enumerate(outs):
            out[...] = total[i * tokens : (i + 1) * tokens].astype(out.dtype)

    dims = (tokens, mine.shape[1])
    return call(
        name, body, [shape(dims, F32)] + [shape(dims, BF16)] * (near - 1), mine, theirs, after=after
    )


def project_back(
    name, flags, weight, pieces, queries=None, own_kv=None, received=(), rider=None, after=()
):
    features, width = weight.shape[1:]
    tokens = (queries if own_kv is None else own_kv).shape[0]
    weights = list(weight.pair) if isinstance(weight, Layer) else [weight]
    args = ([] if queries is None else [queries]) + ([] if own_kv is None else [own_kv, *received])
    riders = [] if rider is None else list(rider[1:])

    def body(ins, outs):
        flag, ins = ins[0], list(ins[1:])

        def chosen(i):
            if len(weights) > 1:
                return weight.read(flag, ins[len(args) : len(args) + 2], i)
            return ins[len(args)][i]

        outs = list(outs)
        total = 0.0
        at = 0
        if queries is not None:
            total = dot(ins[0][...], chosen(0))
            at = 1
        if own_kv is not None:
            kv = summed(ins[at][...], ins[at + 1 : at + 1 + len(received)]).astype(BF16)
            outs.pop(0)[...] = kv
            total = total + dot(kv[:, :features], chosen(1)) + dot(kv[:, features:], chosen(2))
        rows = tokens // pieces
        outs[0][...] = total[:rows]
        for i in range(1, pieces):
            outs[i][:rows] = total[i * rows : (i + 1) * rows].astype(BF16)
            if riders:
                outs[i][rows:] = ins[len(args) + len(weights) + i - 1][...]

    extra = riders[0].shape[0] if riders else 0
    kinds = [] if own_kv is None else [shape(own_kv.shape, BF16)]
    kinds += piece_kinds(tokens, width, pieces, extra)
    out = call(name, body, kinds, *args, *weights, *riders, flags=flags, after=after)
    return out if own_kv is None else (out[0], out[1:])


def turned_products(name, flags, halves, order, per, place, after=(), beside=None):
    columns = sum(r[2] for _, r in halves[0])
    count = len(order)
    arrays, index = [], {}
    for half in halves:
        for (lefts, _), (right, _, _) in half:
            for a in (*lefts, right):
                if id(a) not in index:
                    index[id(a)] = len(arrays)
                    arrays.append(a)
    if beside is not None:
        arrays.append(beside)
    tokens = halves[0][0][1][0].shape[0]
    width = arrays[index[id(halves[0][0][0][0][0])]].shape[1]
    align = 16 if per % 16 == 0 else 8
    kept = BF16 if align == 16 else F32
    n_pairs = len(halves[0])

    def kernel(*refs):
        flag = refs[0]
        ins = refs[1 : 1 + len(arrays)]
        outs = refs[1 + len(arrays) + len(after) :][:2]
        scratch = refs[1 + len(arrays) + len(after) + 2 :]
        first = flag[Flags.FIRST] == 1

        def left_value(half, i):
            lefts, rows = halves[half][i][0]
            return joined([ins[index[id(a)]] for a in lefts], rows)

        def right_value(half, i):
            right, at, size = halves[half][i][1]
            return ins[index[id(right)]][:, at : at + size]

        def same(i):
            a, b = halves[0][i][0], halves[1][i][0]
            return [id(x) for x in a[0]] == [id(x) for x in b[0]] and a[1] == b[1]

        for out_at, out in enumerate(outs):
            at = 0
            for i in range(n_pairs):
                turned = scratch[out_at * n_pairs + i]
                one, two = (0, 1) if out_at == 0 else (1, 0)
                if same(i):
                    left = left_value(0, i)
                else:
                    left = jnp.where(first, left_value(one, i), left_value(two, i))
                right = jnp.where(first, right_value(one, i), right_value(two, i))
                turned[...] = left.astype(kept).T
                size = right.shape[1]
                for k in range(count):
                    start = pl.multiple_of(place(flag, order[k]) * per, align)
                    got = dot(turned[pl.ds(start, per), :].astype(BF16), right)
                    out[k * per : (k + 1) * per, at : at + size] = got.astype(BF16)
                at += size
            for k in range(count if beside is not None else 0):
                start = pl.multiple_of(place(flag, order[k]) * per, align)
                chosen = ins[-1][pl.ds(start, per), :]
                out[k * per : (k + 1) * per, columns:] = chosen

    kind = shape((count * per, columns + (0 if beside is None else beside.shape[1])), BF16)
    moved = sum(math.prod(a.shape) * 2 for a in arrays) + 4 * count * per * columns
    return pl.pallas_call(
        kernel,
        out_shape=[kind, kind],
        in_specs=[pl.BlockSpec(memory_space=pltpu.SMEM)]
        + [pl.BlockSpec(memory_space=pltpu.VMEM)] * len(arrays)
        + [pl.BlockSpec(memory_space=pl.ANY)] * len(after),
        out_specs=[pl.BlockSpec(memory_space=pltpu.VMEM)] * 2,
        scratch_shapes=[pltpu.VMEM((width, tokens), kept)] * (2 * n_pairs),
        compiler_params=pltpu.CompilerParams(vmem_limit_bytes=20 * MIB),
        cost_estimate=pl.CostEstimate(
            flops=4 * tokens * count * per * columns, bytes_accessed=moved, transcendentals=0
        ),
        name=name,
    )(flags, *arrays, *after)


def halved(name, kept, received, last=False, after=(), cuts=None):
    rows, columns = kept.shape
    received = list(received) if isinstance(received, (list, tuple)) else [received]
    cuts = cuts or [columns]
    firsts = [sum(cuts[:i]) for i in range(len(cuts))]

    def body(ins, outs):
        there = [ref[...].astype(F32) for ref in ins[1:]]
        there = jnp.concatenate(there, axis=1) if len(there) > 1 else there[0]
        total = ins[0][...].astype(F32) + there
        if last:
            outs[0][...] = total
        else:
            outs[0][...] = total[: rows // 2].astype(BF16)
            for out, at, size in zip(outs[1:], firsts, cuts):
                out[...] = total[rows // 2 :, at : at + size].astype(BF16)

    if last:
        kinds = [shape((rows, columns), F32)]
    else:
        kinds = [shape((rows // 2, size), BF16) for size in [columns, *cuts]]
    return call(name, body, kinds, kept, *received, after=after)


def one_sided(name, flags, pairs, order, per, place, after=(), sides=1, beside=None):
    arrays, index = [], {}
    for (lefts, _), (right, _, _) in pairs:
        for a in (*lefts, right):
            if id(a) not in index:
                index[id(a)] = len(arrays)
                arrays.append(a)
    if beside is not None:
        arrays.append(beside)
    tokens = pairs[0][1][0].shape[0]
    width = pairs[0][0][0][0].shape[1]
    columns = sum(r[2] for _, r in pairs)
    count = len(order)
    align = 16 if per % 16 == 0 else 8
    kept = BF16 if align == 16 else F32

    def kernel(*refs):
        flag = refs[0]
        ins = refs[1 : 1 + len(arrays)]
        outs = refs[1 + len(arrays) + len(after) :][:sides]
        scratch = refs[1 + len(arrays) + len(after) + sides :]
        at = 0
        for i, ((lefts, rows), (right, first, size)) in enumerate(pairs):
            turned = scratch[i]
            turned[...] = joined([ins[index[id(a)]] for a in lefts], rows).astype(kept).T
            value = ins[index[id(right)]][:, first : first + size]
            for side, out in enumerate(outs):
                for k in range(count):
                    where = place(flag, order[k]) if sides == 1 else place(flag, order[k], side)
                    start = pl.multiple_of(where * per, align)
                    got = dot(turned[pl.ds(start, per), :].astype(BF16), value)
                    out[k * per : (k + 1) * per, at : at + size] = got.astype(BF16)
            at += size
        for k in range(count if beside is not None else 0):
            start = pl.multiple_of(place(flag, order[k]) * per, align)
            outs[0][k * per : (k + 1) * per, columns:] = ins[-1][pl.ds(start, per), :]

    kind = shape((count * per, columns + (0 if beside is None else beside.shape[1])), BF16)
    moved = sum(math.prod(a.shape) * 2 for a in arrays) + 2 * sides * count * per * columns
    return pl.pallas_call(
        kernel,
        out_shape=[kind] * sides,
        in_specs=[pl.BlockSpec(memory_space=pltpu.SMEM)]
        + [pl.BlockSpec(memory_space=pltpu.VMEM)] * len(arrays)
        + [pl.BlockSpec(memory_space=pl.ANY)] * len(after),
        out_specs=[pl.BlockSpec(memory_space=pltpu.VMEM)] * sides,
        scratch_shapes=[pltpu.VMEM((width, tokens), kept)] * len(pairs),
        compiler_params=pltpu.CompilerParams(vmem_limit_bytes=16 * MIB),
        cost_estimate=pl.CostEstimate(
            flops=2 * sides * tokens * count * per * columns, bytes_accessed=moved, transcendentals=0
        ),
        name=name,
    )(flags, *arrays, *after)


def on_device(
    hidden,
    segments,
    self_qkv,
    self_out,
    ffn_in,
    ffn_in_bias,
    ffn_out,
    norm_gains,
    norm_shifts,
    cross_qkv,
    cross_out,
    cross_gain,
    cross_shift,
    cotangent,
):
    section, seq, tp = (lax.axis_index(a) for a in ("section", "seq", "tp"))
    n_seq, n_tp = lax.axis_size("seq"), lax.axis_size("tp")
    half = n_seq // 2
    low_half = seq < half
    on_first = section == 0
    settled = on_first == low_half
    rows, span, width = hidden.shape[2:]
    tokens = rows * span
    sub = tokens // n_tp
    units = ffn_in.shape[2]
    features = cross_out.shape[0]
    flags = jnp.stack([on_first, low_half, settled, tp, seq]).astype(jnp.int32)

    both = ("section", "seq")
    low = range(half)
    to_encoder = [(z, z + half) for z in low] + [(z + half, n_seq + z) for z in low]
    to_decoder = [(n_seq + z, z + half) for z in low] + [(n_seq + z + half, n_seq + z) for z in low]
    across = [(z + half, n_seq + z + half) for z in low] + [(n_seq + z, z) for z in low]

    both_micro = hidden[0].reshape(2, tokens, width)
    far = jnp.where(low_half, both_micro[1], both_micro[0])
    near = jnp.where(low_half, both_micro[0], both_micro[1])
    far_enc = lax.ppermute(far, both, to_encoder)
    core = lax.ppermute(near, both, across)

    def layers(own):
        other = swap_cores(own)
        return Layer(1, own, other), Layer(0, own, other)

    qkv_enc, qkv_dec = layers(jnp.swapaxes(self_qkv[0], 1, 2))
    cross_turned = jnp.swapaxes(cross_qkv, 1, 2)

    def pack(ins, outs):
        zeros = jnp.zeros((2, width), F32)
        outs[0][...] = jnp.concatenate([ins[0][...], ins[1][...], ins[2][...], zeros], axis=0)
        put_rows(outs[1], [ins[3][...], ins[4][...]])

    vectors, vec_cross = call(
        "pack", pack, [shape((8, width), F32)] * 2,
        norm_gains[0], norm_shifts[0], ffn_in_bias[0], cross_gain[None], cross_shift[None],
    )
    vec_enc, vec_dec = layers(vectors)
    out_enc, out_dec = layers(self_out[0])

    small, sums_kind = shape((sub, width), BF16), shape((8, width), F32)

    def cut(ins, outs):
        flag, cot = ins
        at = pl.ds(pl.multiple_of(flag[Flags.TP] * sub, sub), sub)
        low_here = flag[Flags.LOW] == 1
        outs[0][...] = jnp.where(low_here, cot[0, at, :], cot[1, at, :])
        outs[1][...] = jnp.where(low_here, cot[1, at, :], cot[0, at, :])

    cot_near, cot_far = call(
        "cut", cut, [small] * 2, cotangent.reshape(2, tokens, width), flags=flags
    )
    cot_moved = lax.ppermute(
        cot_far, both, [(z, z + half) for z in low] + [(n_seq + z + half, n_seq + z) for z in low]
    )

    n_chunks = 2 * half
    n_keys = n_chunks * tokens
    place = np.broadcast_to(np.arange(n_chunks * span, dtype=np.int32), (1, rows, n_chunks * span))
    base = jnp.concatenate([segments.reshape(4, rows, n_chunks * span), jnp.asarray(place)])
    base = base.reshape(5, rows, n_chunks, span).transpose(0, 2, 1, 3).reshape(5, n_keys)
    z_bits, tp_bits = half.bit_length() - 1, n_tp.bit_length() - 1

    def turn_marks(ins, outs):
        flag, ref = ins
        low_here = flag[Flags.LOW] == 1
        found = jnp.concatenate(
            [
                jnp.where(low_here, ref[0:1, :], ref[1:2, :]),
                jnp.where(low_here, ref[2:3, :], ref[3:4, :]),
                ref[4:5, :],
                jnp.zeros((5, n_keys), jnp.int32),
            ],
            axis=0,
        )
        lane = lax.broadcasted_iota(jnp.int32, found.shape, 1)
        turns = [(1 - flag[Flags.FIRST], half * tokens)]
        turns += [((flag[Flags.SEQ] >> b) & 1, tokens << b) for b in range(z_bits)]
        turns += [((flag[Flags.TP] >> b) & 1, sub << b) for b in range(tp_bits)]
        for turn, step in turns:
            up, down = pltpu.roll(found, step, 1), pltpu.roll(found, n_keys - step, 1)
            other = jnp.where((lane & step) != 0, up, down)
            found = jnp.where(turn == 1, other, found)
        outs[0][...] = found

    (marks,) = call("marks", turn_marks, [shape((8, n_keys), jnp.int32)], base, flags=flags)
    marks_enc = Marks(marks, KEY_ENC, KEY_ENC, False)
    marks_dec = Marks(marks, KEY_DEC, KEY_DEC, True)
    marks_cross = Marks(marks, KEY_DEC, KEY_ENC, False)

    def share(own):
        mine = [own] + [xor_perm(own, "seq", dz) for dz in range(1, half)]
        return mine + [swap_cores(block) for block in mine]

    def settle(name, near_kv, far_kv, after=()):
        own, *sent = settle_cores(name, near_kv, swap_cores(far_kv), half, after)
        return own, [xor_perm(block, "seq", dz + 1) for dz, block in enumerate(sent)]

    top, bottom = slice(0, sub), slice(sub, 2 * sub)

    far_dec = lax.ppermute(far, both, to_decoder)
    input_enc, input_dec, q_enc, q_dec, kv_enc, kv_dec = settle_inputs(
        "qkv_both", near, core, far_enc, far_dec, flags, qkv_enc, qkv_dec,
        after=[marks, cot_moved, *out_enc.pair],
    )
    late_in, late_out, kv_dec = lax.optimization_barrier((ffn_in[0], ffn_out[0], kv_dec))
    all_enc, all_dec = share(kv_enc), share(kv_dec)
    win_enc, win_dec = layers(late_in)
    wout_enc, wout_dec = layers(late_out)
    a_enc, log_enc, part = attend(
        "attend_enc", q_enc, all_enc, marks_enc, out_enc, flags, rows, n_tp
    )
    got = scatter_tp(part[1:])
    a_dec, log_dec, part_dec = attend(
        "attend_dec", q_dec, all_dec, marks_dec, out_dec, flags, rows, n_tp, after=[a_enc],
    )

    def norm_first(ins, outs):
        flag, ins = ins[0], ins[1:]
        total = summed(ins[0][...], ins[1:n_tp]) + ins[n_tp][:sub].astype(F32)
        vec = vec_enc.read(flag, ins[n_tp + 1 : n_tp + 3])
        unit, _ = normalized(total)
        result = unit * vec[GAIN_ATT : GAIN_ATT + 1] + vec[SHIFT_ATT : SHIFT_ATT + 1]
        outs[0][...] = total
        outs[1][...] = result.astype(BF16)

    full = shape((sub, width), F32)
    small_sums = shape((sub + VECTOR_ROWS, width), BF16)
    double_sums = shape((2 * sub + VECTOR_ROWS, width), BF16)
    z1_enc, h1b_enc = call(
        "norm_att_enc", norm_first, [full, small], part[0], *got, input_enc, *vec_enc.pair,
        flags=flags,
    )
    h1_pieces_enc = gather_tp(h1b_enc)

    u_enc, g_enc, part = feed_forward(
        "ffn_enc", h1_pieces_enc, win_enc, vec_enc, wout_enc, flags, rider=part_dec
    )
    got = scatter_tp(part[1:])

    def norm_second(ins, outs):
        flag, ins = ins[0], ins[1:]
        own_enc, own_dec, z1, inputs = ins[:4]
        received = ins[4 : 3 + n_tp]
        vec = vec_enc.read(flag, ins[3 + n_tp : 5 + n_tp])
        unit, _ = normalized(z1[...])
        h1 = unit * vec[GAIN_ATT : GAIN_ATT + 1] + vec[SHIFT_ATT : SHIFT_ATT + 1]
        total = summed(own_enc[...], received, top) + h1 + vec[BIAS_OUT : BIAS_OUT + 1]
        unit, _ = normalized(total)
        memory = unit * vec[GAIN_END : GAIN_END + 1] + vec[SHIFT_END : SHIFT_END + 1]
        outs[0][...] = total
        outs[1][...] = memory.astype(BF16)
        outs[3][:sub] = memory.astype(BF16)
        vec = vec_dec.read(flag, ins[3 + n_tp : 5 + n_tp])
        total = summed(own_dec[...], received, bottom) + inputs[:sub].astype(F32)
        unit, _ = normalized(total)
        result = unit * vec[GAIN_ATT : GAIN_ATT + 1] + vec[SHIFT_ATT : SHIFT_ATT + 1]
        outs[2][...] = total
        outs[3][sub:] = result.astype(BF16)

    double = shape((2 * sub, width), BF16)
    z2_enc, memory, z1_dec, message = call(
        "norm_end_enc", norm_second, [full, small, full, double],
        part[0], part_dec[0], z1_enc, input_dec, *got, *vec_enc.pair, flags=flags,
    )
    mid_pieces = gather_tp(message)

    def cross_projections(ins, outs):
        refs, weight = ins[:n_tp], ins[n_tp]
        values = joined(refs, top)
        for i in (1, 2):
            outs[0][:, (i - 1) * features : i * features] = dot(values, weight[i], 1, 1).astype(BF16)
        outs[1][...] = dot(joined(refs, bottom), weight[0], 1, 1).astype(BF16)

    kv_cross, q_cross = call(
        "qkv_cross", cross_projections,
        [shape((tokens, 2 * features), BF16), shape((tokens, features), BF16)],
        *mid_pieces, cross_turned,
    )
    all_cross = share(kv_cross)
    a_cross, log_cross, part = attend(
        "attend_cross", q_cross, all_cross, marks_cross, cross_out, flags, rows, n_tp
    )
    got = scatter_tp(part[1:])

    def norm_crossed(ins, outs):
        flag, ins = ins[0], ins[1:]
        vec = vec_dec.read(flag, ins[n_tp + 2 : n_tp + 4])
        unit, _ = normalized(ins[n_tp][...])
        h1 = unit * vec[GAIN_ATT : GAIN_ATT + 1] + vec[SHIFT_ATT : SHIFT_ATT + 1]
        total = summed(ins[0][...], ins[1:n_tp]) + h1
        vec = ins[n_tp + 1]
        unit, _ = normalized(total)
        outs[0][...] = total
        outs[1][...] = (unit * vec[0:1] + vec[1:2]).astype(BF16)

    z_cross, h2b = call(
        "norm_cross", norm_crossed, [full, small], part[0], *got, z1_dec, vec_cross,
        *vec_dec.pair, flags=flags,
    )
    h2_pieces = gather_tp(h2b)
    u_dec, g_dec, part = feed_forward("ffn_dec", h2_pieces, win_dec, vec_dec, wout_dec, flags)
    got = scatter_tp(part[1:])

    def norm_turn(ins, outs):
        flag, ins = ins[0], ins[1:]
        crossed, cot_here, cot_there, cross_vec = ins[n_tp : n_tp + 4]
        vec = vec_dec.read(flag, ins[n_tp + 4 : n_tp + 6])
        unit, _ = normalized(crossed[...])
        h2 = unit * cross_vec[0:1] + cross_vec[1:2]
        total = summed(ins[0][...], ins[1:n_tp]) + h2 + vec[BIAS_OUT : BIAS_OUT + 1]
        unit, _ = normalized(total)
        gain = vec[GAIN_END : GAIN_END + 1]
        decoded = (unit * gain + vec[SHIFT_END : SHIFT_END + 1]).astype(BF16)
        upstream = jnp.where(flag[Flags.SETTLED] == 1, cot_here[...], cot_there[...]).astype(F32)
        grad, gain_grad, shift_grad = norm_back(total, gain, upstream)
        outs[0][...] = grad
        outs[1][:sub] = grad.astype(BF16)
        put_vectors(outs[1], sub, [gain_grad, shift_grad, jnp.sum(grad, axis=0, keepdims=True)])
        outs[2][...] = decoded

    dz2_dec, dz2b_dec, decoded = call(
        "norm_end_dec", norm_turn, [full, small_sums, small],
        part[0], *got, z_cross, cot_near, cot_moved, vec_cross, *vec_dec.pair, flags=flags,
    )

    bits = n_seq.bit_length() - 1
    order = sorted(range(n_seq), key=lambda r: int(format(r, f"0{bits}b")[::-1], 2))

    def seq_place(flag, r):
        return flag[Flags.SEQ] ^ r

    def grads_start(name, halves, the_order, per, place, after=(), beside=None):
        mine, theirs = turned_products(name, flags, halves, the_order, per, place, after, beside)
        return mine, swap_cores(theirs)

    def grads_step(name, state, step, after=(), cuts=None):
        kept, received = state
        if step == bits:
            (total,) = halved(f"{name}_sum", kept, received, last=True, after=after)
            return total
        kept, *sent = halved(f"{name}_add{step}", kept, received, after=after, cuts=cuts)
        return kept, [xor_perm(block, "seq", 1 << step) for block in sent]

    def grads_finish(name, state, step=0, after=()):
        while isinstance(state, tuple):
            state = grads_step(name, state, step, after)
            step += 1
        return state

    def self_grads(name, member, pairs, after=(), beside=None):
        (block,) = one_sided(name, flags, pairs, order, per, seq_place, after, beside=beside)
        keeper = 1 - member
        return block, lax.ppermute(block, "section", [(1 - keeper, keeper)])

    def self_step(name, member, state, step, after=()):
        kept, received = state
        if step == bits:
            (total,) = halved(f"{name}_sum", kept, received, last=True, after=after)
            return total
        kept, sent = halved(f"{name}_add{step}", kept, received, after=after)
        at = (1 - member) * n_seq
        route = [(at + z, at + (z ^ (1 << step))) for z in range(n_seq)]
        return kept, lax.ppermute(sent, both, route)

    def self_finish(name, member, state, step, after=()):
        while isinstance(state, tuple):
            state = self_step(name, member, state, step, after)
            step += 1
        return state

    per = width // n_seq
    anything = slice(None)

    r_pieces_dec = gather_tp(dz2b_dec)
    du_dec, sums_in_dec, part = feed_backward(
        "ffn_back_dec", r_pieces_dec, top, u_dec, win_dec, wout_dec, flags
    )
    ffn_dec_state = grads_start(
        "grad_ffn_dec",
        [
            [((h2_pieces, anything), (du_dec, 0, units))],
            [((r_pieces_dec, top), (g_dec, 0, units))],
        ],
        order, per, seq_place,
    )

    got = scatter_tp(part[1:])

    ffn_dec_state = grads_step("grad_ffn_dec", ffn_dec_state, 0)

    def norm_cross_back(ins, outs):
        upstream = summed(ins[0][...], ins[1:n_tp]) + ins[n_tp][...]
        grad, gain_grad, shift_grad = norm_back(ins[n_tp + 1][...], ins[n_tp + 2][0:1], upstream)
        outs[0][...] = grad
        outs[1][:sub] = grad.astype(BF16)
        put_vectors(outs[1], sub, [gain_grad, shift_grad])

    dzc, dzcb = call(
        "norm_back_cross", norm_cross_back, [full, small_sums],
        part[0], *got, dz2_dec, z_cross, vec_cross, after=[ffn_dec_state[0]],
    )
    dzc_pieces = gather_tp(dzcb)

    dq_cross, near_kv, far_kv = attend_back(
        "attend_back_cross", dzc_pieces, top, cross_out, q_cross, all_cross, marks_cross,
        log_cross, flags, rows, half,
    )
    ffn_dec_state = grads_step("grad_ffn_dec", ffn_dec_state, 1, after=[dq_cross])
    own_kv, received_kv = settle("settle_cross", near_kv, far_kv, after=[ffn_dec_state[0]])
    part_query = project_back("query_back", flags, cross_turned, n_tp, queries=dq_cross)
    dkv_cross, part = project_back(
        "memory_back", flags, cross_turned, n_tp, own_kv=own_kv, received=received_kv,
        rider=part_query,
    )
    got = scatter_tp(part[1:])
    per_cross = width // (2 * n_seq)

    def cross_place(flag, r, side):
        return ((1 - flag[Flags.FIRST]) ^ side) * n_seq + (flag[Flags.SEQ] ^ r)

    cross_pairs = [
        ((mid_pieces, bottom), (dq_cross, 0, features)),
        ((mid_pieces, top), (dkv_cross, 0, 2 * features)),
        ((dzc_pieces, top), (a_cross, 0, features)),
    ]
    mine, theirs = one_sided("grad_cross", flags, cross_pairs, order, per_cross, cross_place, sides=2)
    cross_state = mine, swap_cores(theirs)
    cross_state = grads_step("grad_cross", cross_state, 0, after=[dkv_cross])

    def norm_middle_back(ins, outs):
        flag, ins = ins[0], ins[1:]
        own_memory, own_query, residual, z2, z1 = ins[:5]
        received = ins[5 : 4 + n_tp]
        vec = vec_enc.read(flag, ins[4 + n_tp : 6 + n_tp])
        upstream = summed(own_memory[...], received, top).astype(BF16).astype(F32)
        grad, gain_grad, shift_grad = norm_back(z2[...], vec[GAIN_END : GAIN_END + 1], upstream)
        sums = [gain_grad, shift_grad, jnp.sum(grad, axis=0, keepdims=True)]
        outs[0][...] = grad
        outs[2][:sub] = grad.astype(BF16)
        vec = vec_dec.read(flag, ins[4 + n_tp : 6 + n_tp])
        upstream = summed(own_query[...], received, bottom) + residual[...]
        grad, gain_grad, shift_grad = norm_back(z1[...], vec[GAIN_ATT : GAIN_ATT + 1], upstream)
        outs[1][...] = grad
        outs[2][sub : 2 * sub] = grad.astype(BF16)
        put_vectors(outs[2], 2 * sub, sums + [gain_grad, shift_grad])

    dz2_enc, dz1_dec, message = call(
        "norm_back_end_enc", norm_middle_back, [full, full, double_sums],
        part[0], part_query[0], dzc, z2_enc, z1_dec, *got, *vec_enc.pair, flags=flags,
        after=[cross_state[0]],
    )
    back_pieces = gather_tp(message)

    cross_state = grads_step("grad_cross", cross_state, 1, after=[dz2_enc])
    ffn_dec = grads_finish("grad_ffn_dec", ffn_dec_state, 2, after=[dz2_enc])
    du_enc, sums_in_enc, part = feed_backward(
        "ffn_back_enc", back_pieces, top, u_enc, win_enc, wout_enc, flags,
        after=[cross_state[0], ffn_dec],
    )
    got = scatter_tp(part[1:])
    dq_dec, near_kv, far_kv = attend_back(
        "attend_back_dec", back_pieces, bottom, out_dec, q_dec, all_dec, marks_dec,
        log_dec, flags, rows, half, after=[du_enc],
    )

    n_vec, n_columns = 14, 128

    def vector_columns(ins, outs):
        end_dec, cross, mid = (ins[i * n_tp : (i + 1) * n_tp] for i in range(3))
        in_enc, in_dec = ins[3 * n_tp : 3 * n_tp + 2]
        mid_rows = vector_sums(mid, 2 * sub, 5)
        zero = jnp.zeros((1, width), F32)
        dec_rows = vector_sums(end_dec, sub, 3)
        cross_rows = vector_sums(cross, sub, 2)
        found = [
            zero, mid_rows[0:1], zero, mid_rows[1:3], in_enc[0:1],
            mid_rows[3:4], dec_rows[0:1], mid_rows[4:5], dec_rows[1:3], in_dec[0:1],
            cross_rows, jnp.zeros((n_columns - n_vec, width), F32),
        ]
        columns = jnp.concatenate(found, axis=0).T
        moved = jnp.concatenate(
            [
                columns[(core * n_seq + z) * per_cross : (core * n_seq + z + 1) * per_cross]
                for z in range(n_seq)
                for core in range(2)
            ],
            axis=0,
        )
        lane = lax.broadcasted_iota(jnp.int32, columns.shape, 1)
        outs[0][...] = jnp.where(lane >= n_vec - 2, moved, columns).astype(BF16)

    (vectors_here,) = call(
        "vector_columns", vector_columns, [shape((width, n_columns), BF16)],
        *r_pieces_dec, *dzc_pieces, *back_pieces, sums_in_enc, sums_in_dec,
    )
    ffn_enc_state = grads_start(
        "grad_ffn_enc",
        [
            [((h1_pieces_enc, anything), (du_enc, 0, units))],
            [((back_pieces, top), (g_enc, 0, units))],
        ],
        order, per, seq_place, after=[dq_dec], beside=vectors_here,
    )

    dec_kv, dec_received = settle("settle_dec", near_kv, far_kv)
    ffn_enc_state = grads_step("grad_ffn_enc", ffn_enc_state, 0)

    def norm_first_back(ins, outs):
        flag, ins = ins[0], ins[1:]
        upstream = summed(ins[0][...], ins[1:n_tp]) + ins[n_tp][...]
        vec = vec_enc.read(flag, ins[n_tp + 2 : n_tp + 4])
        grad, gain_grad, shift_grad = norm_back(
            ins[n_tp + 1][...], vec[GAIN_ATT : GAIN_ATT + 1], upstream
        )
        outs[0][...] = grad
        outs[1][:sub] = grad.astype(BF16)
        put_vectors(outs[1], sub, [gain_grad, shift_grad])

    dz1_enc, dz1b_enc = call(
        "norm_back_att_enc", norm_first_back, [full, small_sums],
        part[0], *got, dz2_enc, z1_enc, *vec_enc.pair, flags=flags,
        after=[dec_kv, ffn_enc_state[0]],
    )
    dz1_pieces_enc = gather_tp(dz1b_enc)


    dkv_dec, part_dec = project_back(
        "input_back_dec", flags, qkv_dec, n_tp, queries=dq_dec, own_kv=dec_kv,
        received=dec_received, after=[dz1_enc],
    )
    cross_sum = grads_finish("grad_cross", cross_state, 2, after=[dkv_dec])
    dq_enc, near_kv, far_kv = attend_back(
        "attend_back_enc", dz1_pieces_enc, top, out_enc, q_enc, all_enc, marks_enc,
        log_enc, flags, rows, half, after=[cross_sum],
    )
    own_kv, received_kv = settle("settle_enc", near_kv, far_kv)
    self_dec_state = self_grads(
        "grad_self_dec", 0,
        [
            (([input_dec], anything), (dq_dec, 0, features)),
            (([input_dec], anything), (dkv_dec, 0, 2 * features)),
            ((back_pieces, bottom), (a_dec, 0, features)),
        ],
        after=[own_kv],
    )
    ffn_enc_state = grads_step(
        "grad_ffn_enc", ffn_enc_state, 1, after=[self_dec_state[0]], cuts=[units // 2, units // 2 + n_columns]
    )
    dkv_enc, part = project_back(
        "input_back_enc", flags, qkv_enc, n_tp, queries=dq_enc, own_kv=own_kv,
        received=received_kv, rider=part_dec, after=[ffn_enc_state[0]],
    )
    got = scatter_tp(part[1:])
    def att_columns(ins, outs):
        found = [vector_sums(ins, sub, 2), jnp.zeros((n_columns - 2, width), F32)]
        outs[0][...] = jnp.concatenate(found, axis=0).T.astype(BF16)

    (vectors_att,) = call(
        "vector_columns_att", att_columns, [shape((width, n_columns), BF16)], *dz1_pieces_enc,
        after=[part[0]],
    )
    self_enc_state = self_grads(
        "grad_self_enc", 1,
        [
            (([input_enc], anything), (dq_enc, 0, features)),
            (([input_enc], anything), (dkv_enc, 0, 2 * features)),
            ((dz1_pieces_enc, top), (a_enc, 0, features)),
        ],
        after=[part[0]], beside=vectors_att,
    )
    self_dec_state = self_step("grad_self_dec", 0, self_dec_state, 0, after=[part[0]])


    def finish_cross(ins, outs):
        whole = ins[0][...]
        for i in range(3):
            outs[0][i] = whole[:, i * features : (i + 1) * features]
        outs[1][...] = whole[:, 3 * features :].T

    grad_cross_qkv, grad_cross_out = call(
        "finish_cross", finish_cross,
        [shape((3, per_cross, features), F32), shape((features, per_cross), F32)], cross_sum,
        after=[part[0]],
    )

    def input_sums(ins, outs):
        flag, ins = ins[0], ins[1:]
        received = ins[4 : 3 + n_tp]
        enc = (summed(ins[0][...], received, top) + ins[2][...]).astype(BF16)
        dec = (summed(ins[1][...], received, bottom) + ins[3][...]).astype(BF16)
        enc = jnp.concatenate([ins[3 + n_tp][...], enc], axis=0)
        dec = jnp.concatenate([ins[4 + n_tp][...], dec], axis=0)
        outs[0][...] = enc
        outs[1][...] = dec
        outs[2][...] = jnp.where(flag[Flags.FIRST] == 1, dec, enc)

    done_enc, done_dec, done_across = call(
        "input_sums", input_sums, [double, double, double],
        part[0], part_dec[0], dz1_enc, dz1_dec, *got, memory, decoded, flags=flags,
        after=[self_enc_state[0], ffn_enc_state[1][0], grad_cross_out],
    )
    self_enc_state = self_step("grad_self_enc", 1, self_enc_state, 0, after=[done_enc])
    self_dec_state = self_step("grad_self_dec", 0, self_dec_state, 1, after=[self_enc_state[0]])

    ffn_enc = grads_finish("grad_ffn_enc", ffn_enc_state, 2, after=[self_enc_state[0]])
    def to_other(ins, outs):
        outs[0][...] = jnp.where(ins[0][Flags.FIRST] == 1, ins[1][...], ins[2][:, :units])

    (sent,) = call(
        "grad_swap", to_other, [shape((per, units), F32)], ffn_dec, ffn_enc, flags=flags
    )

    far_enc = lax.ppermute(done_enc, both, [(b, a) for a, b in to_encoder])
    far_dec = lax.ppermute(done_dec, both, [(b, a) for a, b in to_decoder])
    from_core = lax.ppermute(done_across, both, [(b, a) for a, b in across])

    def order_body(ins, outs):
        flag = ins[0]
        first = flag[Flags.FIRST] == 1
        stays = jnp.where(first, ins[1][...], ins[2][...])
        near = jnp.where(flag[Flags.SETTLED] == 1, stays, ins[3][...])
        far = jnp.where(first, ins[4][...], ins[5][...])
        low_here = flag[Flags.LOW] == 1
        outs[0][: 2 * sub] = jnp.where(low_here, near, far)
        outs[0][2 * sub :] = jnp.where(low_here, far, near)

    (found,) = call(
        "outputs_order", order_body, [shape((4 * sub, width), BF16)],
        done_enc, done_dec, from_core, far_enc, far_dec, flags=flags,
        after=[self_dec_state[0]],
    )
    self_enc_state = self_step("grad_self_enc", 1, self_enc_state, 1, after=[found])
    self_dec = self_finish("grad_self_dec", 0, self_dec_state, 2, after=[self_enc_state[0]])
    self_enc = self_finish("grad_self_enc", 1, self_enc_state, 2, after=[self_dec])
    pieces = gather_tp(found)
    swapped = swap_cores(sent)

    def finish(ins, outs):
        flag, dec_ffn, enc_ffn, other = ins
        first = flag[Flags.FIRST] == 1
        mine = jnp.where(first, enc_ffn[:, :units], dec_ffn[...])
        theirs = other[...]
        outs[0][...] = jnp.where(first, mine, theirs)
        outs[1][...] = jnp.where(first, theirs, mine)
        table = enc_ffn[:, units:].T
        vectors_here = jnp.where(first, table[0:6], table[6:12])
        outs[2][...] = jnp.concatenate([vectors_here, jnp.zeros((2, per), F32)], axis=0)
        outs[3][...] = vectors_here[5:6]
        crossed = table[n_vec - 2 : n_vec]
        crossed = jnp.where(first, crossed[:, :per_cross], crossed[:, per_cross:])
        outs[4][...] = crossed[0:1]
        outs[5][...] = crossed[1:2]

    grad_in, grad_out, layer_vectors, grad_bias, grad_cross_gain, grad_cross_shift = call(
        "finish_ffn", finish,
        [shape((per, units), F32)] * 2
        + [shape((8, per), F32), shape((1, per), F32)]
        + [shape((1, per_cross), F32)] * 2,
        ffn_dec, ffn_enc, swapped, flags=flags,
    )


    def place_body(ins, outs):
        here = ins[0][Flags.TP]
        for i, ref in enumerate(ins[1:]):
            at = pl.ds(pl.multiple_of((here ^ i) * sub, sub), sub)
            for micro in range(2):
                first_row = 2 * micro * sub
                outs[0][micro, at, :] = ref[first_row : first_row + sub]
                outs[1][micro, at, :] = ref[first_row + sub : first_row + 2 * sub]

    layer_out, grad_hidden = call(
        "outputs_place", place_body, [shape((2, tokens, width), BF16)] * 2, *pieces, flags=flags,
        after=[self_enc, grad_in],
    )

    def finish_self(ins, outs):
        first = ins[0][Flags.FIRST] == 1
        whole = jnp.where(first, ins[1][:, : 4 * features], ins[2][...])
        own = ins[3][...]
        att = ins[1][:, 4 * features :].T
        outs[2][0:1] = own[0:1] + jnp.where(first, att[0:1], 0.0)
        outs[2][1:2] = own[1:2]
        outs[3][0:1] = own[2:3] + jnp.where(first, att[1:2], 0.0)
        outs[3][1:3] = own[3:5]
        for i in range(3):
            outs[0][i] = whole[:, i * features : (i + 1) * features]
        outs[1][...] = whole[:, 3 * features :].T

    grad_qkv, grad_self_out, grad_gains, grad_shifts = call(
        "finish_self", finish_self,
        [
            shape((3, per, features), F32), shape((features, per), F32),
            shape((2, per), F32), shape((3, per), F32),
        ],
        self_enc, self_dec, layer_vectors, flags=flags,
    )

    return (
        layer_out.reshape(1, 2, rows, span, width),
        grad_hidden.reshape(1, 2, rows, span, width),
        grad_qkv[None],
        grad_self_out[None],
        grad_in[None],
        grad_bias[None],
        grad_out.T[None],
        grad_gains[None],
        grad_shifts[None],
        grad_cross_qkv,
        grad_cross_out,
        grad_cross_gain[0],
        grad_cross_shift[0],
    )


def solution(mesh):
    return jax.shard_map(
        on_device,
        mesh=mesh,
        in_specs=(
            P("section", None, None, "seq", None),
            P(),
            P("section", None, None, "tp"),
            P("section", "tp", None),
            P("section", None, "tp"),
            P("section", "tp", None),
            P("section", "tp", None),
            P("section", None, None),
            P("section", None, None),
            P(None, None, "tp"),
            P("tp", None),
            P(),
            P(),
            P(None, None, "seq", None),
        ),
        out_specs=(
            P("section", None, None, "seq", None),
            P("section", None, None, "seq", None),
            P("section", None, "seq", "tp"),
            P("section", "tp", "seq"),
            P("section", "seq", "tp"),
            P("section", "tp", "seq"),
            P("section", "tp", "seq"),
            P("section", None, "seq"),
            P("section", None, "seq"),
            P(None, ("section", "seq"), "tp"),
            P("tp", ("section", "seq")),
            P(("section", "seq")),
            P(("section", "seq")),
        ),
        check_vma=False,
    )
```

```python
import math

import jax
import jax.numpy as jnp
import numpy as np
from jax import lax
from jax.experimental import pallas as pl
from jax.experimental.pallas import tpu as pltpu
from jax.sharding import PartitionSpec as P

HEAD_DIM = 64
EPSILON = 1e-05
MASKED_OUT = -1e30
SCALE = 1.0 / math.sqrt(HEAD_DIM)
F32 = jnp.float32
BF16 = jnp.bfloat16
MIB = 1 << 20

GAIN_ATT, GAIN_END, SHIFT_ATT, SHIFT_END, BIAS_OUT, BIAS_IN = range(6)


def shape(dims, kind):
    return jax.ShapeDtypeStruct(dims, kind)


def dot(left, right, left_dim=1, right_dim=0):
    return lax.dot_general(
        left, right, (((left_dim,), (right_dim,)), ((), ())), preferred_element_type=F32
    )


class Flags:
    FIRST, LOW, SETTLED, TP, SEQ = range(5)


def call(name, body, outs, *args, flags=None, after=(), flops=0, vmem=16 * MIB):
    scalars = [] if flags is None else [flags]
    after = list(after)
    count = len(scalars) + len(args)

    def kernel(*refs):
        body(refs[:count], refs[count + len(after) :])

    moved = sum(math.prod(a.shape) * a.dtype.itemsize for a in (*args, *outs))
    in_specs = [pl.BlockSpec(memory_space=pltpu.SMEM)] * len(scalars)
    in_specs += [pl.BlockSpec(memory_space=pltpu.VMEM)] * len(args)
    in_specs += [pl.BlockSpec(memory_space=pl.ANY)] * len(after)
    return pl.pallas_call(
        kernel,
        out_shape=outs,
        in_specs=in_specs,
        out_specs=[pl.BlockSpec(memory_space=pltpu.VMEM)] * len(outs),
        compiler_params=pltpu.CompilerParams(vmem_limit_bytes=vmem),
        cost_estimate=pl.CostEstimate(flops=flops, bytes_accessed=moved, transcendentals=0),
        name=name,
    )(*scalars, *args, *after)


def swap_cores(block):
    return lax.ppermute(block, "section", [(0, 1), (1, 0)])


def xor_perm(block, axis, bits):
    return lax.ppermute(block, axis, [(i, i ^ bits) for i in range(lax.axis_size(axis))])


def scatter_tp(pieces):
    order = sorted(range(1, len(pieces) + 1), key=lambda i: -bin(i).count("1"))
    got = {i: xor_perm(pieces[i - 1], "tp", i) for i in order}
    return [got[i] for i in range(1, len(pieces) + 1)]


def gather_tp(block):
    return [block] + scatter_tp([block] * (lax.axis_size("tp") - 1))


def normalized(values):
    centred = values - jnp.mean(values, axis=-1, keepdims=True)
    spread = jnp.mean(centred * centred, axis=-1, keepdims=True)
    inverse = lax.rsqrt(spread + EPSILON)
    return centred * inverse, inverse


def norm_back(values, gain, upstream):
    unit, inverse = normalized(values)
    scaled = gain * upstream
    grad = (
        scaled
        - jnp.mean(scaled, axis=-1, keepdims=True)
        - unit * jnp.mean(scaled * unit, axis=-1, keepdims=True)
    ) * inverse
    gain_grad = jnp.sum(upstream * unit, axis=0, keepdims=True)
    shift_grad = jnp.sum(upstream, axis=0, keepdims=True)
    return grad, gain_grad, shift_grad


def put_rows(ref, rows):
    width = ref.shape[1]
    ref[...] = jnp.concatenate(rows + [jnp.zeros((8 - len(rows), width), F32)], axis=0)


VECTOR_ROWS = 16


def put_vectors(ref, at, rows):
    half = VECTOR_ROWS // 2
    whole = jnp.concatenate(rows + [jnp.zeros((half - len(rows), ref.shape[1]), F32)], axis=0)
    top = whole.astype(BF16)
    left = (whole - top.astype(F32)).astype(BF16)
    ref[at : at + VECTOR_ROWS] = jnp.concatenate([top, left], axis=0)


def vector_sums(refs, at, count):
    half = VECTOR_ROWS // 2
    total = 0.0
    for ref in refs:
        rows = ref[at : at + VECTOR_ROWS].astype(F32)
        total = total + (rows[:half] + rows[half:])
    return total[:count]


def summed(own, received, part=slice(None)):
    total = own
    for ref in received:
        total = total + ref[part].astype(F32)
    return total


def joined(refs, part=slice(None)):
    return jnp.concatenate([ref[part] for ref in refs], axis=0)


def store_pieces(refs, value):
    rows = refs[0].shape[0]
    for i, ref in enumerate(refs):
        ref[...] = value[i * rows : (i + 1) * rows].astype(ref.dtype)


def piece_kinds(tokens, width, count, extra=0):
    rows = tokens // count
    return [shape((rows, width), F32)] + [shape((rows + extra, width), BF16)] * (count - 1)


class Layer:
    def __init__(self, mine, own, other):
        self.mine, self.pair = mine, (own, other)
        self.shape = own.shape

    def read(self, flags, refs, part=Ellipsis):
        return jnp.where(flags[Flags.FIRST] == self.mine, refs[0][part], refs[1][part])


def settle_inputs(name, near, core, far_enc, far_dec, flags, weight_enc, weight_dec, after=()):
    tokens, width = near.shape
    features = weight_enc.shape[1]
    n_tp = lax.axis_size("tp")
    sub = tokens // n_tp

    def body(ins, outs):
        flag, near_ref, core_ref = ins[:3]
        tp = flag[Flags.TP]
        for layer, weight in enumerate((weight_enc, weight_dec)):
            far_ref, weights = ins[3 + layer], ins[5 + 2 * layer : 7 + 2 * layer]
            is_own = flag[Flags.FIRST] == 1 - layer
            pieces = []
            for i in range(n_tp):
                at = pl.ds(pl.multiple_of((tp ^ i) * sub, sub), sub)
                settled = jnp.where(is_own, near_ref[at, :], core_ref[at, :])
                pieces.append(jnp.where(flag[Flags.SETTLED] == 1, settled, far_ref[at, :]))
            values = jnp.concatenate(pieces, axis=0)
            outs[layer][...] = values
            for i in range(3):
                found = dot(values, weight.read(flag, weights, i), 1, 1).astype(BF16)
                if i == 0:
                    outs[2 + layer][...] = found
                else:
                    first = (i - 1) * features
                    outs[4 + layer][:, first : first + features] = found

    kinds = [shape((tokens, width), BF16)] * 2 + [shape((tokens, features), BF16)] * 2
    kinds += [shape((tokens, 2 * features), BF16)] * 2
    return call(
        name, body, kinds, near, core, far_enc, far_dec, *weight_enc.pair, *weight_dec.pair,
        flags=flags, after=after,
    )


HALF_ROOT = 0.5**0.5
DENSITY = 1.0 / math.sqrt(2.0 * math.pi)


def feed_forward(name, pieces, weight_in, vectors, weight_out, flags, rider=None, after=()):
    count = len(pieces)
    tokens = sum(p.shape[0] for p in pieces)
    units, width = weight_out.shape
    step = 256
    riders = [] if rider is None else list(rider[1:])

    def body(ins, outs):
        flag, ins = ins[0], ins[1:]
        values = joined(ins[:count])
        win, vec, wout = ins[count : count + 2], ins[count + 2 : count + 4], ins[count + 4 : count + 6]
        bias = vectors.read(flag, vec)[BIAS_IN : BIAS_IN + 1]
        total = 0.0
        for at in range(0, units, step):
            part = slice(at, at + step)
            before = dot(values, weight_in.read(flag, win, (slice(None), part))) + bias[:, part]
            outs[0][:, part] = before
            active = (0.5 * before * (1.0 + lax.erf(before * HALF_ROOT))).astype(BF16)
            outs[1][:, part] = active
            total = total + dot(active, weight_out.read(flag, wout, part))
        rows = tokens // count
        outs[2][...] = total[:rows]
        for i in range(1, count):
            outs[2 + i][:rows] = total[i * rows : (i + 1) * rows].astype(BF16)
            if riders:
                outs[2 + i][rows:] = ins[count + 5 + i][...]

    kinds = [shape((tokens, units), F32), shape((tokens, units), BF16)]
    extra = riders[0].shape[0] if riders else 0
    kinds += piece_kinds(tokens, width, count, extra)
    flops = 4 * tokens * units * width
    out = call(
        name, body, kinds, *pieces, *weight_in.pair, *vectors.pair, *weight_out.pair, *riders,
        flags=flags, after=after, flops=flops,
    )
    return out[0], out[1], out[2:]


def feed_backward(name, pieces, part_rows, before, weight_in, weight_out, flags, after=()):
    count = len(pieces)
    tokens, units = before.shape
    width = weight_out.shape[1]
    step = 256

    def body(ins, outs):
        flag, ins = ins[0], ins[1:]
        values = joined(ins[:count], part_rows)
        before_ref, win, wout = ins[count], ins[count + 1 : count + 3], ins[count + 3 : count + 5]
        total = 0.0
        sums = []
        for at in range(0, units, step):
            part = slice(at, at + step)
            grad_active = dot(values, weight_out.read(flag, wout, part), 1, 1)
            u = before_ref[:, part]
            slope = 0.5 * (1.0 + lax.erf(u * HALF_ROOT)) + u * (DENSITY * jnp.exp(-0.5 * u * u))
            grad = (slope * grad_active).astype(BF16)
            outs[0][:, part] = grad
            sums.append(jnp.sum(grad.astype(F32), axis=0, keepdims=True))
            total = total + dot(grad, weight_in.read(flag, win, (slice(None), part)), 1, 1)
        put_rows(outs[1], [jnp.concatenate(sums, axis=1)])
        store_pieces(outs[2:], total)

    kinds = [shape((tokens, units), BF16), shape((8, units), F32)]
    kinds += piece_kinds(tokens, width, count)
    flops = 4 * tokens * units * width
    out = call(
        name, body, kinds, *pieces, before, *weight_in.pair, *weight_out.pair,
        flags=flags, after=after, flops=flops,
    )
    return out[0], out[1], out[2:]


KEY_ENC, KEY_DEC, PLACE = range(3)


class Marks:
    def __init__(self, marks, query_row, key_row, causal):
        self.marks, self.query_row, self.key_row, self.causal = marks, query_row, key_row, causal

    def allowed(self, ref, columns, piece, tokens, group, span):
        at = piece * tokens + group * span
        own = slice(group * span, (group + 1) * span)
        allowed = (
            columns[at : at + span, self.key_row : self.key_row + 1]
            == ref[self.query_row : self.query_row + 1, own]
        )
        if self.causal:
            places = columns[at : at + span, PLACE : PLACE + 1]
            allowed = allowed & (places <= ref[PLACE : PLACE + 1, own])
        return allowed


def head_block(flipped, head, heads):
    tokens = flipped.shape[1]
    parts = []
    if head:
        parts.append(jnp.zeros((HEAD_DIM * head, tokens), flipped.dtype))
    parts.append(flipped[HEAD_DIM * head : HEAD_DIM * (head + 1)])
    if head < heads - 1:
        parts.append(jnp.zeros((HEAD_DIM * (heads - 1 - head), tokens), flipped.dtype))
    return jnp.concatenate(parts, axis=0) if len(parts) > 1 else parts[0]


def attend(name, queries, pieces, marks, weight_out, flags, rows, tp, after=(), first=0):
    tokens, width = queries.shape
    span = tokens // rows
    heads = width // HEAD_DIM
    count = len(pieces)
    weights = list(weight_out.pair) if isinstance(weight_out, Layer) else [weight_out]

    def body(ins, outs):
        flag, query_ref, mark = ins[:3]
        wout = ins[3 : 3 + len(weights)]
        kv = ins[3 + len(weights) :]
        columns = mark[...].T
        mixed = []
        for group in range(rows):
            part = slice(group * span, (group + 1) * span)
            flipped = (query_ref[part, :] * BF16(SCALE)).T
            value_rows = [ref[part, first + width : first + 2 * width].T for ref in kv]
            masks = [marks.allowed(mark, columns, p, tokens, group, span) for p in range(count)]
            mixtures, logs = [], []
            for head in range(heads):
                block = head_block(flipped, head, heads)
                scores = [
                    jnp.where(
                        masks[p], dot(kv[p][part, first : first + width], block), MASKED_OUT
                    )
                    for p in range(count)
                ]
                largest = scores[0]
                for s in scores[1:]:
                    largest = jnp.maximum(largest, s)
                largest = jnp.max(largest, axis=0, keepdims=True)
                total, mixture = 0.0, 0.0
                for p in range(count):
                    e = jnp.exp(scores[p] - largest)
                    total = total + jnp.sum(e, axis=0, keepdims=True)
                    own = value_rows[p][HEAD_DIM * head : HEAD_DIM * (head + 1)]
                    mixture = mixture + dot(own, e.astype(BF16))
                mixtures.append(mixture * (1.0 / total))
                logs.append(largest + jnp.log(total))
            logs.append(jnp.zeros((8 - heads, span), F32))
            outs[1][group] = jnp.concatenate(logs, axis=0)
            mixed.append(jnp.concatenate(mixtures, axis=0).T.astype(BF16))
        result = jnp.concatenate(mixed, axis=0) if rows > 1 else mixed[0]
        outs[0][...] = result
        if len(weights) > 1:
            store_pieces(outs[2:], dot(result, weight_out.read(flag, wout)))
        else:
            store_pieces(outs[2:], dot(result, wout[0][...]))

    kinds = [shape((tokens, width), BF16), shape((rows, 8, span), F32)]
    kinds += piece_kinds(tokens, weight_out.shape[1], tp)
    flops = 4 * tokens * span * count * heads * 256
    out = call(
        name, body, kinds, queries, marks.marks, *weights, *pieces,
        flags=flags, after=after, flops=flops,
    )
    return out[0], out[1], out[2:]


def attend_back(
    name, upstream, part_rows, weight_out, queries, pieces, marks, logs, flags, rows, near, after=(),
    first_column=0,
):
    tokens, width = queries.shape
    span = tokens // rows
    heads = width // HEAD_DIM
    count = len(pieces)
    first = len(upstream)
    weights = list(weight_out.pair) if isinstance(weight_out, Layer) else [weight_out]

    def body(ins, outs):
        flag, ins = ins[0], ins[1:]
        all_grad = joined(ins[:first], part_rows)
        query_ref, log_ref, mark = ins[first : first + 3]
        wout = ins[first + 3 : first + 3 + len(weights)]
        wout = weight_out.read(flag, wout) if len(weights) > 1 else wout[0][...]
        kv = ins[first + 3 + len(weights) :]
        columns = mark[...].T
        grad_rows = dot(all_grad, wout, 1, 1).astype(BF16)
        for group in range(rows):
            part = slice(group * span, (group + 1) * span)
            grad = grad_rows[part]
            grad_flipped = dot(wout, all_grad[part], 1, 1).astype(BF16)
            scaled = query_ref[part, :] * BF16(SCALE)
            flipped = scaled.T
            keys_at = slice(first_column, first_column + width)
            values_at = slice(first_column + width, first_column + 2 * width)
            key_rows = [ref[part, keys_at].T for ref in kv]
            masks = [marks.allowed(mark, columns, p, tokens, group, span) for p in range(count)]
            lane = lax.broadcasted_iota(jnp.int32, (span, width), 1)
            key_grads, value_grads, query_grads = [0.0] * count, [0.0] * count, []
            for head in range(heads):
                mine = (lane >= HEAD_DIM * head) & (lane < HEAD_DIM * (head + 1))
                block = head_block(flipped, head, heads)
                grad_block = head_block(grad_flipped, head, heads)
                query_part = jnp.where(mine, scaled, BF16(0.0))
                grad_part = jnp.where(mine, grad, BF16(0.0))
                log_row = log_ref[group, head : head + 1, :]
                shares, share_grads, inner = [], [], 0.0
                for p in range(count):
                    s = jnp.where(masks[p], dot(kv[p][part, keys_at], block), MASKED_OUT)
                    w = jnp.exp(s - log_row)
                    g = dot(kv[p][part, values_at], grad_block)
                    inner = inner + jnp.sum(w * g, axis=0, keepdims=True)
                    value_grads[p] = value_grads[p] + dot(w.astype(BF16), grad_part)
                    shares.append(w)
                    share_grads.append(g)
                query_grad = 0.0
                for p in range(count):
                    score_grad = (shares[p] * (share_grads[p] - inner)).astype(BF16)
                    key_grads[p] = key_grads[p] + dot(score_grad, query_part)
                    own = key_rows[p][HEAD_DIM * head : HEAD_DIM * (head + 1)]
                    query_grad = query_grad + dot(own, score_grad)
                query_grads.append(query_grad)
            outs[0][part, :] = (jnp.concatenate(query_grads, axis=0) * SCALE).T.astype(BF16)
            for p in range(count):
                out, at = (outs[1], p) if p < near else (outs[2], p - near)
                at = slice(at * tokens + group * span, at * tokens + (group + 1) * span)
                out[at, :width] = key_grads[p].astype(out.dtype)
                out[at, width:] = value_grads[p].astype(out.dtype)

    kinds = [
        shape((tokens, width), BF16),
        shape((near * tokens, 2 * width), F32),
        shape(((count - near) * tokens, 2 * width), BF16),
    ]
    flops = 10 * tokens * span * count * heads * 256
    args = (*upstream, queries, logs, marks.marks, *weights, *pieces)
    return call(name, body, kinds, *args, flags=flags, after=after, flops=flops)


def settle_cores(name, mine, theirs, near, after=()):
    tokens = mine.shape[0] // near

    def body(ins, outs):
        total = ins[0][...] + ins[1][...].astype(F32)
        for i, out in enumerate(outs):
            out[...] = total[i * tokens : (i + 1) * tokens].astype(out.dtype)

    dims = (tokens, mine.shape[1])
    return call(
        name, body, [shape(dims, F32)] + [shape(dims, BF16)] * (near - 1), mine, theirs, after=after
    )


def project_back(
    name, flags, weight, pieces, queries=None, own_kv=None, received=(), rider=None, after=()
):
    features, width = weight.shape[1:]
    tokens = (queries if own_kv is None else own_kv).shape[0]
    weights = list(weight.pair) if isinstance(weight, Layer) else [weight]
    args = ([] if queries is None else [queries]) + ([] if own_kv is None else [own_kv, *received])
    riders = [] if rider is None else list(rider[1:])

    def body(ins, outs):
        flag, ins = ins[0], list(ins[1:])

        def chosen(i):
            if len(weights) > 1:
                return weight.read(flag, ins[len(args) : len(args) + 2], i)
            return ins[len(args)][i]

        outs = list(outs)
        total = 0.0
        at = 0
        if queries is not None:
            total = dot(ins[0][...], chosen(0))
            at = 1
        if own_kv is not None:
            kv = summed(ins[at][...], ins[at + 1 : at + 1 + len(received)]).astype(BF16)
            outs.pop(0)[...] = kv
            total = total + dot(kv[:, :features], chosen(1)) + dot(kv[:, features:], chosen(2))
        rows = tokens // pieces
        outs[0][...] = total[:rows]
        for i in range(1, pieces):
            outs[i][:rows] = total[i * rows : (i + 1) * rows].astype(BF16)
            if riders:
                outs[i][rows:] = ins[len(args) + len(weights) + i - 1][...]

    extra = riders[0].shape[0] if riders else 0
    kinds = [] if own_kv is None else [shape(own_kv.shape, BF16)]
    kinds += piece_kinds(tokens, width, pieces, extra)
    out = call(name, body, kinds, *args, *weights, *riders, flags=flags, after=after)
    return out if own_kv is None else (out[0], out[1:])


def turned_products(name, flags, halves, order, per, place, after=(), beside=None):
    columns = sum(r[2] for _, r in halves[0])
    count = len(order)
    arrays, index = [], {}
    for half in halves:
        for (lefts, _), (right, _, _) in half:
            for a in (*lefts, right):
                if id(a) not in index:
                    index[id(a)] = len(arrays)
                    arrays.append(a)
    if beside is not None:
        arrays.append(beside)
    tokens = halves[0][0][1][0].shape[0]
    width = arrays[index[id(halves[0][0][0][0][0])]].shape[1]
    align = 16 if per % 16 == 0 else 8
    kept = BF16 if align == 16 else F32
    n_pairs = len(halves[0])

    def kernel(*refs):
        flag = refs[0]
        ins = refs[1 : 1 + len(arrays)]
        outs = refs[1 + len(arrays) + len(after) :][:2]
        scratch = refs[1 + len(arrays) + len(after) + 2 :]
        first = flag[Flags.FIRST] == 1

        def left_value(half, i):
            lefts, rows = halves[half][i][0]
            return joined([ins[index[id(a)]] for a in lefts], rows)

        def right_value(half, i):
            right, at, size = halves[half][i][1]
            return ins[index[id(right)]][:, at : at + size]

        def same(i):
            a, b = halves[0][i][0], halves[1][i][0]
            return [id(x) for x in a[0]] == [id(x) for x in b[0]] and a[1] == b[1]

        for out_at, out in enumerate(outs):
            at = 0
            for i in range(n_pairs):
                turned = scratch[out_at * n_pairs + i]
                one, two = (0, 1) if out_at == 0 else (1, 0)
                if same(i):
                    left = left_value(0, i)
                else:
                    left = jnp.where(first, left_value(one, i), left_value(two, i))
                right = jnp.where(first, right_value(one, i), right_value(two, i))
                turned[...] = left.astype(kept).T
                size = right.shape[1]
                for k in range(count):
                    start = pl.multiple_of(place(flag, order[k]) * per, align)
                    got = dot(turned[pl.ds(start, per), :].astype(BF16), right)
                    out[k * per : (k + 1) * per, at : at + size] = got.astype(BF16)
                at += size
            for k in range(count if beside is not None else 0):
                start = pl.multiple_of(place(flag, order[k]) * per, align)
                chosen = ins[-1][pl.ds(start, per), :]
                out[k * per : (k + 1) * per, columns:] = chosen

    kind = shape((count * per, columns + (0 if beside is None else beside.shape[1])), BF16)
    moved = sum(math.prod(a.shape) * 2 for a in arrays) + 4 * count * per * columns
    return pl.pallas_call(
        kernel,
        out_shape=[kind, kind],
        in_specs=[pl.BlockSpec(memory_space=pltpu.SMEM)]
        + [pl.BlockSpec(memory_space=pltpu.VMEM)] * len(arrays)
        + [pl.BlockSpec(memory_space=pl.ANY)] * len(after),
        out_specs=[pl.BlockSpec(memory_space=pltpu.VMEM)] * 2,
        scratch_shapes=[pltpu.VMEM((width, tokens), kept)] * (2 * n_pairs),
        compiler_params=pltpu.CompilerParams(vmem_limit_bytes=20 * MIB),
        cost_estimate=pl.CostEstimate(
            flops=4 * tokens * count * per * columns, bytes_accessed=moved, transcendentals=0
        ),
        name=name,
    )(flags, *arrays, *after)


def halved(name, kept, received, last=False, after=(), cuts=None):
    rows, columns = kept.shape
    received = list(received) if isinstance(received, (list, tuple)) else [received]
    cuts = cuts or [columns]
    firsts = [sum(cuts[:i]) for i in range(len(cuts))]

    def body(ins, outs):
        there = [ref[...].astype(F32) for ref in ins[1:]]
        there = jnp.concatenate(there, axis=1) if len(there) > 1 else there[0]
        total = ins[0][...].astype(F32) + there
        if last:
            outs[0][...] = total
        else:
            outs[0][...] = total[: rows // 2].astype(BF16)
            for out, at, size in zip(outs[1:], firsts, cuts):
                out[...] = total[rows // 2 :, at : at + size].astype(BF16)

    if last:
        kinds = [shape((rows, columns), F32)]
    else:
        kinds = [shape((rows // 2, size), BF16) for size in [columns, *cuts]]
    return call(name, body, kinds, kept, *received, after=after)


def one_sided(name, flags, pairs, order, per, place, after=(), sides=1, beside=None):
    arrays, index = [], {}
    for (lefts, _), (right, _, _) in pairs:
        for a in (*lefts, right):
            if id(a) not in index:
                index[id(a)] = len(arrays)
                arrays.append(a)
    if beside is not None:
        arrays.append(beside)
    tokens = pairs[0][1][0].shape[0]
    width = pairs[0][0][0][0].shape[1]
    columns = sum(r[2] for _, r in pairs)
    count = len(order)
    align = 16 if per % 16 == 0 else 8
    kept = BF16 if align == 16 else F32

    def kernel(*refs):
        flag = refs[0]
        ins = refs[1 : 1 + len(arrays)]
        outs = refs[1 + len(arrays) + len(after) :][:sides]
        scratch = refs[1 + len(arrays) + len(after) + sides :]
        at = 0
        for i, ((lefts, rows), (right, first, size)) in enumerate(pairs):
            turned = scratch[i]
            turned[...] = joined([ins[index[id(a)]] for a in lefts], rows).astype(kept).T
            value = ins[index[id(right)]][:, first : first + size]
            for side, out in enumerate(outs):
                for k in range(count):
                    where = place(flag, order[k]) if sides == 1 else place(flag, order[k], side)
                    start = pl.multiple_of(where * per, align)
                    got = dot(turned[pl.ds(start, per), :].astype(BF16), value)
                    out[k * per : (k + 1) * per, at : at + size] = got.astype(BF16)
            at += size
        for k in range(count if beside is not None else 0):
            start = pl.multiple_of(place(flag, order[k]) * per, align)
            outs[0][k * per : (k + 1) * per, columns:] = ins[-1][pl.ds(start, per), :]

    kind = shape((count * per, columns + (0 if beside is None else beside.shape[1])), BF16)
    moved = sum(math.prod(a.shape) * 2 for a in arrays) + 2 * sides * count * per * columns
    return pl.pallas_call(
        kernel,
        out_shape=[kind] * sides,
        in_specs=[pl.BlockSpec(memory_space=pltpu.SMEM)]
        + [pl.BlockSpec(memory_space=pltpu.VMEM)] * len(arrays)
        + [pl.BlockSpec(memory_space=pl.ANY)] * len(after),
        out_specs=[pl.BlockSpec(memory_space=pltpu.VMEM)] * sides,
        scratch_shapes=[pltpu.VMEM((width, tokens), kept)] * len(pairs),
        compiler_params=pltpu.CompilerParams(vmem_limit_bytes=16 * MIB),
        cost_estimate=pl.CostEstimate(
            flops=2 * sides * tokens * count * per * columns, bytes_accessed=moved, transcendentals=0
        ),
        name=name,
    )(flags, *arrays, *after)


def on_device(
    hidden,
    segments,
    self_qkv,
    self_out,
    ffn_in,
    ffn_in_bias,
    ffn_out,
    norm_gains,
    norm_shifts,
    cross_qkv,
    cross_out,
    cross_gain,
    cross_shift,
    cotangent,
):
    section, seq, tp = (lax.axis_index(a) for a in ("section", "seq", "tp"))
    n_seq, n_tp = lax.axis_size("seq"), lax.axis_size("tp")
    half = n_seq // 2
    low_half = seq < half
    on_first = section == 0
    settled = on_first == low_half
    rows, span, width = hidden.shape[2:]
    tokens = rows * span
    sub = tokens // n_tp
    units = ffn_in.shape[2]
    features = cross_out.shape[0]
    flags = jnp.stack([on_first, low_half, settled, tp, seq]).astype(jnp.int32)

    both = ("section", "seq")
    low = range(half)
    to_encoder = [(z, z + half) for z in low] + [(z + half, n_seq + z) for z in low]
    to_decoder = [(n_seq + z, z + half) for z in low] + [(n_seq + z + half, n_seq + z) for z in low]
    across = [(z + half, n_seq + z + half) for z in low] + [(n_seq + z, z) for z in low]

    both_micro = hidden[0].reshape(2, tokens, width)
    far = jnp.where(low_half, both_micro[1], both_micro[0])
    near = jnp.where(low_half, both_micro[0], both_micro[1])
    far_enc = lax.ppermute(far, both, to_encoder)
    core = lax.ppermute(near, both, across)

    def layers(own):
        other = swap_cores(own)
        return Layer(1, own, other), Layer(0, own, other)

    qkv_enc, qkv_dec = layers(jnp.swapaxes(self_qkv[0], 1, 2))
    cross_turned = jnp.swapaxes(cross_qkv, 1, 2)

    def pack(ins, outs):
        zeros = jnp.zeros((2, width), F32)
        outs[0][...] = jnp.concatenate([ins[0][...], ins[1][...], ins[2][...], zeros], axis=0)
        put_rows(outs[1], [ins[3][...], ins[4][...]])

    vectors, vec_cross = call(
        "pack", pack, [shape((8, width), F32)] * 2,
        norm_gains[0], norm_shifts[0], ffn_in_bias[0], cross_gain[None], cross_shift[None],
    )
    vec_enc, vec_dec = layers(vectors)
    out_enc, out_dec = layers(self_out[0])

    small, sums_kind = shape((sub, width), BF16), shape((8, width), F32)

    def cut(ins, outs):
        flag, cot = ins
        at = pl.ds(pl.multiple_of(flag[Flags.TP] * sub, sub), sub)
        low_here = flag[Flags.LOW] == 1
        outs[0][...] = jnp.where(low_here, cot[0, at, :], cot[1, at, :])
        outs[1][...] = jnp.where(low_here, cot[1, at, :], cot[0, at, :])

    cot_near, cot_far = call(
        "cut", cut, [small] * 2, cotangent.reshape(2, tokens, width), flags=flags
    )
    cot_moved = lax.ppermute(
        cot_far, both, [(z, z + half) for z in low] + [(n_seq + z + half, n_seq + z) for z in low]
    )

    n_chunks = 2 * half
    n_keys = n_chunks * tokens
    place = np.broadcast_to(np.arange(n_chunks * span, dtype=np.int32), (1, rows, n_chunks * span))
    base = jnp.concatenate([segments.reshape(4, rows, n_chunks * span), jnp.asarray(place)])
    base = base.reshape(5, rows, n_chunks, span).transpose(0, 2, 1, 3).reshape(5, n_keys)
    z_bits, tp_bits = half.bit_length() - 1, n_tp.bit_length() - 1

    def turn_marks(ins, outs):
        flag, ref = ins
        low_here = flag[Flags.LOW] == 1
        found = jnp.concatenate(
            [
                jnp.where(low_here, ref[0:1, :], ref[1:2, :]),
                jnp.where(low_here, ref[2:3, :], ref[3:4, :]),
                ref[4:5, :],
                jnp.zeros((5, n_keys), jnp.int32),
            ],
            axis=0,
        )
        lane = lax.broadcasted_iota(jnp.int32, found.shape, 1)
        turns = [(1 - flag[Flags.FIRST], half * tokens)]
        turns += [((flag[Flags.SEQ] >> b) & 1, tokens << b) for b in range(z_bits)]
        turns += [((flag[Flags.TP] >> b) & 1, sub << b) for b in range(tp_bits)]
        for turn, step in turns:
            up, down = pltpu.roll(found, step, 1), pltpu.roll(found, n_keys - step, 1)
            other = jnp.where((lane & step) != 0, up, down)
            found = jnp.where(turn == 1, other, found)
        outs[0][...] = found

    (marks,) = call("marks", turn_marks, [shape((8, n_keys), jnp.int32)], base, flags=flags)
    marks_enc = Marks(marks, KEY_ENC, KEY_ENC, False)
    marks_dec = Marks(marks, KEY_DEC, KEY_DEC, True)
    marks_cross = Marks(marks, KEY_DEC, KEY_ENC, False)

    def share(own):
        mine = [own] + [xor_perm(own, "seq", dz) for dz in range(1, half)]
        return mine + [swap_cores(block) for block in mine]

    def settle(name, near_kv, far_kv, after=()):
        own, *sent = settle_cores(name, near_kv, swap_cores(far_kv), half, after)
        return own, [xor_perm(block, "seq", dz + 1) for dz, block in enumerate(sent)]

    top, bottom = slice(0, sub), slice(sub, 2 * sub)

    far_dec = lax.ppermute(far, both, to_decoder)
    input_enc, input_dec, q_enc, q_dec, kv_enc, kv_dec = settle_inputs(
        "qkv_both", near, core, far_enc, far_dec, flags, qkv_enc, qkv_dec,
        after=[marks, cot_moved, *out_enc.pair],
    )
    late_in, late_out, kv_dec = lax.optimization_barrier((ffn_in[0], ffn_out[0], kv_dec))
    all_enc, all_dec = share(kv_enc), share(kv_dec)
    win_enc, win_dec = layers(late_in)
    wout_enc, wout_dec = layers(late_out)
    a_enc, log_enc, part = attend(
        "attend_enc", q_enc, all_enc, marks_enc, out_enc, flags, rows, n_tp
    )
    got = scatter_tp(part[1:])
    a_dec, log_dec, part_dec = attend(
        "attend_dec", q_dec, all_dec, marks_dec, out_dec, flags, rows, n_tp, after=[a_enc],
    )

    def norm_first(ins, outs):
        flag, ins = ins[0], ins[1:]
        total = summed(ins[0][...], ins[1:n_tp]) + ins[n_tp][:sub].astype(F32)
        vec = vec_enc.read(flag, ins[n_tp + 1 : n_tp + 3])
        unit, _ = normalized(total)
        result = unit * vec[GAIN_ATT : GAIN_ATT + 1] + vec[SHIFT_ATT : SHIFT_ATT + 1]
        outs[0][...] = total
        outs[1][...] = result.astype(BF16)

    full = shape((sub, width), F32)
    small_sums = shape((sub + VECTOR_ROWS, width), BF16)
    double_sums = shape((2 * sub + VECTOR_ROWS, width), BF16)
    z1_enc, h1b_enc = call(
        "norm_att_enc", norm_first, [full, small], part[0], *got, input_enc, *vec_enc.pair,
        flags=flags,
    )
    h1_pieces_enc = gather_tp(h1b_enc)

    u_enc, g_enc, part = feed_forward(
        "ffn_enc", h1_pieces_enc, win_enc, vec_enc, wout_enc, flags, rider=part_dec
    )
    got = scatter_tp(part[1:])

    def norm_second(ins, outs):
        flag, ins = ins[0], ins[1:]
        own_enc, own_dec, z1, inputs = ins[:4]
        received = ins[4 : 3 + n_tp]
        vec = vec_enc.read(flag, ins[3 + n_tp : 5 + n_tp])
        unit, _ = normalized(z1[...])
        h1 = unit * vec[GAIN_ATT : GAIN_ATT + 1] + vec[SHIFT_ATT : SHIFT_ATT + 1]
        total = summed(own_enc[...], received, top) + h1 + vec[BIAS_OUT : BIAS_OUT + 1]
        unit, _ = normalized(total)
        memory = unit * vec[GAIN_END : GAIN_END + 1] + vec[SHIFT_END : SHIFT_END + 1]
        outs[0][...] = total
        outs[1][...] = memory.astype(BF16)
        outs[3][:sub] = memory.astype(BF16)
        vec = vec_dec.read(flag, ins[3 + n_tp : 5 + n_tp])
        total = summed(own_dec[...], received, bottom) + inputs[:sub].astype(F32)
        unit, _ = normalized(total)
        result = unit * vec[GAIN_ATT : GAIN_ATT + 1] + vec[SHIFT_ATT : SHIFT_ATT + 1]
        outs[2][...] = total
        outs[3][sub:] = result.astype(BF16)

    double = shape((2 * sub, width), BF16)
    z2_enc, memory, z1_dec, message = call(
        "norm_end_enc", norm_second, [full, small, full, double],
        part[0], part_dec[0], z1_enc, input_dec, *got, *vec_enc.pair, flags=flags,
    )
    mid_pieces = gather_tp(message)

    def cross_projections(ins, outs):
        refs, weight = ins[:n_tp], ins[n_tp]
        values = joined(refs, top)
        for i in (1, 2):
            outs[0][:, (i - 1) * features : i * features] = dot(values, weight[i], 1, 1).astype(BF16)
        outs[1][...] = dot(joined(refs, bottom), weight[0], 1, 1).astype(BF16)

    kv_cross, q_cross = call(
        "qkv_cross", cross_projections,
        [shape((tokens, 2 * features), BF16), shape((tokens, features), BF16)],
        *mid_pieces, cross_turned,
    )
    all_cross = share(kv_cross)
    a_cross, log_cross, part = attend(
        "attend_cross", q_cross, all_cross, marks_cross, cross_out, flags, rows, n_tp
    )
    got = scatter_tp(part[1:])

    def norm_crossed(ins, outs):
        flag, ins = ins[0], ins[1:]
        vec = vec_dec.read(flag, ins[n_tp + 2 : n_tp + 4])
        unit, _ = normalized(ins[n_tp][...])
        h1 = unit * vec[GAIN_ATT : GAIN_ATT + 1] + vec[SHIFT_ATT : SHIFT_ATT + 1]
        total = summed(ins[0][...], ins[1:n_tp]) + h1
        vec = ins[n_tp + 1]
        unit, _ = normalized(total)
        outs[0][...] = total
        outs[1][...] = (unit * vec[0:1] + vec[1:2]).astype(BF16)

    z_cross, h2b = call(
        "norm_cross", norm_crossed, [full, small], part[0], *got, z1_dec, vec_cross,
        *vec_dec.pair, flags=flags,
    )
    h2_pieces = gather_tp(h2b)
    u_dec, g_dec, part = feed_forward("ffn_dec", h2_pieces, win_dec, vec_dec, wout_dec, flags)
    got = scatter_tp(part[1:])

    def norm_turn(ins, outs):
        flag, ins = ins[0], ins[1:]
        crossed, cot_here, cot_there, cross_vec = ins[n_tp : n_tp + 4]
        vec = vec_dec.read(flag, ins[n_tp + 4 : n_tp + 6])
        unit, _ = normalized(crossed[...])
        h2 = unit * cross_vec[0:1] + cross_vec[1:2]
        total = summed(ins[0][...], ins[1:n_tp]) + h2 + vec[BIAS_OUT : BIAS_OUT + 1]
        unit, _ = normalized(total)
        gain = vec[GAIN_END : GAIN_END + 1]
        decoded = (unit * gain + vec[SHIFT_END : SHIFT_END + 1]).astype(BF16)
        upstream = jnp.where(flag[Flags.SETTLED] == 1, cot_here[...], cot_there[...]).astype(F32)
        grad, gain_grad, shift_grad = norm_back(total, gain, upstream)
        outs[0][...] = grad
        outs[1][:sub] = grad.astype(BF16)
        put_vectors(outs[1], sub, [gain_grad, shift_grad, jnp.sum(grad, axis=0, keepdims=True)])
        outs[2][...] = decoded

    dz2_dec, dz2b_dec, decoded = call(
        "norm_end_dec", norm_turn, [full, small_sums, small],
        part[0], *got, z_cross, cot_near, cot_moved, vec_cross, *vec_dec.pair, flags=flags,
    )

    bits = n_seq.bit_length() - 1
    order = sorted(range(n_seq), key=lambda r: int(format(r, f"0{bits}b")[::-1], 2))

    def seq_place(flag, r):
        return flag[Flags.SEQ] ^ r

    def grads_start(name, halves, the_order, per, place, after=(), beside=None):
        mine, theirs = turned_products(name, flags, halves, the_order, per, place, after, beside)
        return mine, swap_cores(theirs)

    def grads_step(name, state, step, after=(), cuts=None):
        kept, received = state
        if step == bits:
            (total,) = halved(f"{name}_sum", kept, received, last=True, after=after)
            return total
        kept, *sent = halved(f"{name}_add{step}", kept, received, after=after, cuts=cuts)
        return kept, [xor_perm(block, "seq", 1 << step) for block in sent]

    def grads_finish(name, state, step=0, after=()):
        while isinstance(state, tuple):
            state = grads_step(name, state, step, after)
            step += 1
        return state

    def self_grads(name, member, pairs, after=(), beside=None):
        (block,) = one_sided(name, flags, pairs, order, per, seq_place, after, beside=beside)
        keeper = 1 - member
        return block, lax.ppermute(block, "section", [(1 - keeper, keeper)])

    def self_step(name, member, state, step, after=()):
        kept, received = state
        if step == bits:
            (total,) = halved(f"{name}_sum", kept, received, last=True, after=after)
            return total
        kept, sent = halved(f"{name}_add{step}", kept, received, after=after)
        at = (1 - member) * n_seq
        route = [(at + z, at + (z ^ (1 << step))) for z in range(n_seq)]
        return kept, lax.ppermute(sent, both, route)

    def self_finish(name, member, state, step, after=()):
        while isinstance(state, tuple):
            state = self_step(name, member, state, step, after)
            step += 1
        return state

    per = width // n_seq
    anything = slice(None)

    r_pieces_dec = gather_tp(dz2b_dec)
    du_dec, sums_in_dec, part = feed_backward(
        "ffn_back_dec", r_pieces_dec, top, u_dec, win_dec, wout_dec, flags
    )
    ffn_dec_state = grads_start(
        "grad_ffn_dec",
        [
            [((h2_pieces, anything), (du_dec, 0, units))],
            [((r_pieces_dec, top), (g_dec, 0, units))],
        ],
        order, per, seq_place,
    )

    got = scatter_tp(part[1:])

    ffn_dec_state = grads_step("grad_ffn_dec", ffn_dec_state, 0)

    def norm_cross_back(ins, outs):
        upstream = summed(ins[0][...], ins[1:n_tp]) + ins[n_tp][...]
        grad, gain_grad, shift_grad = norm_back(ins[n_tp + 1][...], ins[n_tp + 2][0:1], upstream)
        outs[0][...] = grad
        outs[1][:sub] = grad.astype(BF16)
        put_vectors(outs[1], sub, [gain_grad, shift_grad])

    dzc, dzcb = call(
        "norm_back_cross", norm_cross_back, [full, small_sums],
        part[0], *got, dz2_dec, z_cross, vec_cross, after=[ffn_dec_state[0]],
    )
    dzc_pieces = gather_tp(dzcb)

    dq_cross, near_kv, far_kv = attend_back(
        "attend_back_cross", dzc_pieces, top, cross_out, q_cross, all_cross, marks_cross,
        log_cross, flags, rows, half,
    )
    ffn_dec_state = grads_step("grad_ffn_dec", ffn_dec_state, 1, after=[dq_cross])
    own_kv, received_kv = settle("settle_cross", near_kv, far_kv, after=[ffn_dec_state[0]])
    part_query = project_back("query_back", flags, cross_turned, n_tp, queries=dq_cross)
    dkv_cross, part = project_back(
        "memory_back", flags, cross_turned, n_tp, own_kv=own_kv, received=received_kv,
        rider=part_query,
    )
    got = scatter_tp(part[1:])
    per_cross = width // (2 * n_seq)

    def cross_place(flag, r, side):
        return ((1 - flag[Flags.FIRST]) ^ side) * n_seq + (flag[Flags.SEQ] ^ r)

    cross_pairs = [
        ((mid_pieces, bottom), (dq_cross, 0, features)),
        ((mid_pieces, top), (dkv_cross, 0, 2 * features)),
        ((dzc_pieces, top), (a_cross, 0, features)),
    ]
    mine, theirs = one_sided("grad_cross", flags, cross_pairs, order, per_cross, cross_place, sides=2)
    cross_state = mine, swap_cores(theirs)
    cross_state = grads_step("grad_cross", cross_state, 0, after=[dkv_cross])

    def norm_middle_back(ins, outs):
        flag, ins = ins[0], ins[1:]
        own_memory, own_query, residual, z2, z1 = ins[:5]
        received = ins[5 : 4 + n_tp]
        vec = vec_enc.read(flag, ins[4 + n_tp : 6 + n_tp])
        upstream = summed(own_memory[...], received, top).astype(BF16).astype(F32)
        grad, gain_grad, shift_grad = norm_back(z2[...], vec[GAIN_END : GAIN_END + 1], upstream)
        sums = [gain_grad, shift_grad, jnp.sum(grad, axis=0, keepdims=True)]
        outs[0][...] = grad
        outs[2][:sub] = grad.astype(BF16)
        vec = vec_dec.read(flag, ins[4 + n_tp : 6 + n_tp])
        upstream = summed(own_query[...], received, bottom) + residual[...]
        grad, gain_grad, shift_grad = norm_back(z1[...], vec[GAIN_ATT : GAIN_ATT + 1], upstream)
        outs[1][...] = grad
        outs[2][sub : 2 * sub] = grad.astype(BF16)
        put_vectors(outs[2], 2 * sub, sums + [gain_grad, shift_grad])

    dz2_enc, dz1_dec, message = call(
        "norm_back_end_enc", norm_middle_back, [full, full, double_sums],
        part[0], part_query[0], dzc, z2_enc, z1_dec, *got, *vec_enc.pair, flags=flags,
        after=[cross_state[0]],
    )
    back_pieces = gather_tp(message)

    cross_state = grads_step("grad_cross", cross_state, 1, after=[dz2_enc])
    ffn_dec = grads_finish("grad_ffn_dec", ffn_dec_state, 2, after=[dz2_enc])
    du_enc, sums_in_enc, part = feed_backward(
        "ffn_back_enc", back_pieces, top, u_enc, win_enc, wout_enc, flags,
        after=[cross_state[0], ffn_dec],
    )
    got = scatter_tp(part[1:])
    dq_dec, near_kv, far_kv = attend_back(
        "attend_back_dec", back_pieces, bottom, out_dec, q_dec, all_dec, marks_dec,
        log_dec, flags, rows, half, after=[du_enc],
    )

    n_vec, n_columns = 14, 128

    def vector_columns(ins, outs):
        end_dec, cross, mid = (ins[i * n_tp : (i + 1) * n_tp] for i in range(3))
        in_enc, in_dec = ins[3 * n_tp : 3 * n_tp + 2]
        mid_rows = vector_sums(mid, 2 * sub, 5)
        zero = jnp.zeros((1, width), F32)
        dec_rows = vector_sums(end_dec, sub, 3)
        cross_rows = vector_sums(cross, sub, 2)
        found = [
            zero, mid_rows[0:1], zero, mid_rows[1:3], in_enc[0:1],
            mid_rows[3:4], dec_rows[0:1], mid_rows[4:5], dec_rows[1:3], in_dec[0:1],
            cross_rows, jnp.zeros((n_columns - n_vec, width), F32),
        ]
        columns = jnp.concatenate(found, axis=0).T
        moved = jnp.concatenate(
            [
                columns[(core * n_seq + z) * per_cross : (core * n_seq + z + 1) * per_cross]
                for z in range(n_seq)
                for core in range(2)
            ],
            axis=0,
        )
        lane = lax.broadcasted_iota(jnp.int32, columns.shape, 1)
        outs[0][...] = jnp.where(lane >= n_vec - 2, moved, columns).astype(BF16)

    (vectors_here,) = call(
        "vector_columns", vector_columns, [shape((width, n_columns), BF16)],
        *r_pieces_dec, *dzc_pieces, *back_pieces, sums_in_enc, sums_in_dec,
    )
    ffn_enc_state = grads_start(
        "grad_ffn_enc",
        [
            [((h1_pieces_enc, anything), (du_enc, 0, units))],
            [((back_pieces, top), (g_enc, 0, units))],
        ],
        order, per, seq_place, after=[dq_dec], beside=vectors_here,
    )

    dec_kv, dec_received = settle("settle_dec", near_kv, far_kv)
    ffn_enc_state = grads_step("grad_ffn_enc", ffn_enc_state, 0)

    def norm_first_back(ins, outs):
        flag, ins = ins[0], ins[1:]
        upstream = summed(ins[0][...], ins[1:n_tp]) + ins[n_tp][...]
        vec = vec_enc.read(flag, ins[n_tp + 2 : n_tp + 4])
        grad, gain_grad, shift_grad = norm_back(
            ins[n_tp + 1][...], vec[GAIN_ATT : GAIN_ATT + 1], upstream
        )
        outs[0][...] = grad
        outs[1][:sub] = grad.astype(BF16)
        put_vectors(outs[1], sub, [gain_grad, shift_grad])

    dz1_enc, dz1b_enc = call(
        "norm_back_att_enc", norm_first_back, [full, small_sums],
        part[0], *got, dz2_enc, z1_enc, *vec_enc.pair, flags=flags,
        after=[dec_kv, ffn_enc_state[0]],
    )
    dz1_pieces_enc = gather_tp(dz1b_enc)


    dkv_dec, part_dec = project_back(
        "input_back_dec", flags, qkv_dec, n_tp, queries=dq_dec, own_kv=dec_kv,
        received=dec_received, after=[dz1_enc],
    )
    cross_sum = grads_finish("grad_cross", cross_state, 2, after=[dkv_dec])
    dq_enc, near_kv, far_kv = attend_back(
        "attend_back_enc", dz1_pieces_enc, top, out_enc, q_enc, all_enc, marks_enc,
        log_enc, flags, rows, half, after=[cross_sum],
    )
    own_kv, received_kv = settle("settle_enc", near_kv, far_kv)
    self_dec_state = self_grads(
        "grad_self_dec", 0,
        [
            (([input_dec], anything), (dq_dec, 0, features)),
            (([input_dec], anything), (dkv_dec, 0, 2 * features)),
            ((back_pieces, bottom), (a_dec, 0, features)),
        ],
        after=[own_kv],
    )
    ffn_enc_state = grads_step(
        "grad_ffn_enc", ffn_enc_state, 1, after=[self_dec_state[0]], cuts=[units // 2, units // 2 + n_columns]
    )
    dkv_enc, part = project_back(
        "input_back_enc", flags, qkv_enc, n_tp, queries=dq_enc, own_kv=own_kv,
        received=received_kv, rider=part_dec, after=[ffn_enc_state[0]],
    )
    got = scatter_tp(part[1:])
    def att_columns(ins, outs):
        found = [vector_sums(ins, sub, 2), jnp.zeros((n_columns - 2, width), F32)]
        outs[0][...] = jnp.concatenate(found, axis=0).T.astype(BF16)

    (vectors_att,) = call(
        "vector_columns_att", att_columns, [shape((width, n_columns), BF16)], *dz1_pieces_enc,
        after=[part[0]],
    )
    self_enc_state = self_grads(
        "grad_self_enc", 1,
        [
            (([input_enc], anything), (dq_enc, 0, features)),
            (([input_enc], anything), (dkv_enc, 0, 2 * features)),
            ((dz1_pieces_enc, top), (a_enc, 0, features)),
        ],
        after=[part[0]], beside=vectors_att,
    )
    self_dec_state = self_step("grad_self_dec", 0, self_dec_state, 0, after=[part[0]])
    self_enc_state = self_step("grad_self_enc", 1, self_enc_state, 0, after=[self_dec_state[0]])


    def finish_cross(ins, outs):
        whole = ins[0][...]
        for i in range(3):
            outs[0][i] = whole[:, i * features : (i + 1) * features]
        outs[1][...] = whole[:, 3 * features :].T

    grad_cross_qkv, grad_cross_out = call(
        "finish_cross", finish_cross,
        [shape((3, per_cross, features), F32), shape((features, per_cross), F32)], cross_sum,
        after=[part[0]],
    )

    def input_sums(ins, outs):
        flag, ins = ins[0], ins[1:]
        received = ins[4 : 3 + n_tp]
        enc = (summed(ins[0][...], received, top) + ins[2][...]).astype(BF16)
        dec = (summed(ins[1][...], received, bottom) + ins[3][...]).astype(BF16)
        enc = jnp.concatenate([ins[3 + n_tp][...], enc], axis=0)
        dec = jnp.concatenate([ins[4 + n_tp][...], dec], axis=0)
        outs[0][...] = enc
        outs[1][...] = dec
        outs[2][...] = jnp.where(flag[Flags.FIRST] == 1, dec, enc)

    done_enc, done_dec, done_across = call(
        "input_sums", input_sums, [double, double, double],
        part[0], part_dec[0], dz1_enc, dz1_dec, *got, memory, decoded, flags=flags,
        after=[self_enc_state[0], ffn_enc_state[1][0], grad_cross_out],
    )
    self_dec_state = self_step("grad_self_dec", 0, self_dec_state, 1, after=[done_enc])

    self_enc_state = self_step("grad_self_enc", 1, self_enc_state, 1, after=[self_dec_state[0]])
    ffn_enc = grads_finish("grad_ffn_enc", ffn_enc_state, 2, after=[done_enc])
    def to_other(ins, outs):
        outs[0][...] = jnp.where(ins[0][Flags.FIRST] == 1, ins[1][...], ins[2][:, :units])

    (sent,) = call(
        "grad_swap", to_other, [shape((per, units), F32)], ffn_dec, ffn_enc, flags=flags
    )

    far_enc = lax.ppermute(done_enc, both, [(b, a) for a, b in to_encoder])
    far_dec = lax.ppermute(done_dec, both, [(b, a) for a, b in to_decoder])
    from_core = lax.ppermute(done_across, both, [(b, a) for a, b in across])

    def order_body(ins, outs):
        flag = ins[0]
        first = flag[Flags.FIRST] == 1
        stays = jnp.where(first, ins[1][...], ins[2][...])
        near = jnp.where(flag[Flags.SETTLED] == 1, stays, ins[3][...])
        far = jnp.where(first, ins[4][...], ins[5][...])
        low_here = flag[Flags.LOW] == 1
        outs[0][: 2 * sub] = jnp.where(low_here, near, far)
        outs[0][2 * sub :] = jnp.where(low_here, far, near)

    (found,) = call(
        "outputs_order", order_body, [shape((4 * sub, width), BF16)],
        done_enc, done_dec, from_core, far_enc, far_dec, flags=flags,
        after=[self_enc_state[0]],
    )
    self_dec = self_finish("grad_self_dec", 0, self_dec_state, 2, after=[found])
    self_enc = self_finish("grad_self_enc", 1, self_enc_state, 2, after=[self_dec])
    pieces = gather_tp(found)
    swapped = swap_cores(sent)

    def finish(ins, outs):
        flag, dec_ffn, enc_ffn, other = ins
        first = flag[Flags.FIRST] == 1
        mine = jnp.where(first, enc_ffn[:, :units], dec_ffn[...])
        theirs = other[...]
        outs[0][...] = jnp.where(first, mine, theirs)
        outs[1][...] = jnp.where(first, theirs, mine)
        table = enc_ffn[:, units:].T
        vectors_here = jnp.where(first, table[0:6], table[6:12])
        outs[2][...] = jnp.concatenate([vectors_here, jnp.zeros((2, per), F32)], axis=0)
        outs[3][...] = vectors_here[5:6]
        crossed = table[n_vec - 2 : n_vec]
        crossed = jnp.where(first, crossed[:, :per_cross], crossed[:, per_cross:])
        outs[4][...] = crossed[0:1]
        outs[5][...] = crossed[1:2]

    grad_in, grad_out, layer_vectors, grad_bias, grad_cross_gain, grad_cross_shift = call(
        "finish_ffn", finish,
        [shape((per, units), F32)] * 2
        + [shape((8, per), F32), shape((1, per), F32)]
        + [shape((1, per_cross), F32)] * 2,
        ffn_dec, ffn_enc, swapped, flags=flags,
    )


    def place_body(ins, outs):
        here = ins[0][Flags.TP]
        for i, ref in enumerate(ins[1:]):
            at = pl.ds(pl.multiple_of((here ^ i) * sub, sub), sub)
            for micro in range(2):
                first_row = 2 * micro * sub
                outs[0][micro, at, :] = ref[first_row : first_row + sub]
                outs[1][micro, at, :] = ref[first_row + sub : first_row + 2 * sub]

    layer_out, grad_hidden = call(
        "outputs_place", place_body, [shape((2, tokens, width), BF16)] * 2, *pieces, flags=flags,
        after=[self_enc, grad_in],
    )

    def finish_self(ins, outs):
        first = ins[0][Flags.FIRST] == 1
        whole = jnp.where(first, ins[1][:, : 4 * features], ins[2][...])
        own = ins[3][...]
        att = ins[1][:, 4 * features :].T
        outs[2][0:1] = own[0:1] + jnp.where(first, att[0:1], 0.0)
        outs[2][1:2] = own[1:2]
        outs[3][0:1] = own[2:3] + jnp.where(first, att[1:2], 0.0)
        outs[3][1:3] = own[3:5]
        for i in range(3):
            outs[0][i] = whole[:, i * features : (i + 1) * features]
        outs[1][...] = whole[:, 3 * features :].T

    grad_qkv, grad_self_out, grad_gains, grad_shifts = call(
        "finish_self", finish_self,
        [
            shape((3, per, features), F32), shape((features, per), F32),
            shape((2, per), F32), shape((3, per), F32),
        ],
        self_enc, self_dec, layer_vectors, flags=flags,
    )

    return (
        layer_out.reshape(1, 2, rows, span, width),
        grad_hidden.reshape(1, 2, rows, span, width),
        grad_qkv[None],
        grad_self_out[None],
        grad_in[None],
        grad_bias[None],
        grad_out.T[None],
        grad_gains[None],
        grad_shifts[None],
        grad_cross_qkv,
        grad_cross_out,
        grad_cross_gain[0],
        grad_cross_shift[0],
    )


def solution(mesh):
    return jax.shard_map(
        on_device,
        mesh=mesh,
        in_specs=(
            P("section", None, None, "seq", None),
            P(),
            P("section", None, None, "tp"),
            P("section", "tp", None),
            P("section", None, "tp"),
            P("section", "tp", None),
            P("section", "tp", None),
            P("section", None, None),
            P("section", None, None),
            P(None, None, "tp"),
            P("tp", None),
            P(),
            P(),
            P(None, None, "seq", None),
        ),
        out_specs=(
            P("section", None, None, "seq", None),
            P("section", None, None, "seq", None),
            P("section", None, "seq", "tp"),
            P("section", "tp", "seq"),
            P("section", "seq", "tp"),
            P("section", "tp", "seq"),
            P("section", "tp", "seq"),
            P("section", None, "seq"),
            P("section", None, "seq"),
            P(None, ("section", "seq"), "tp"),
            P("tp", ("section", "seq")),
            P(("section", "seq")),
            P(("section", "seq")),
        ),
        check_vma=False,
    )
```
